32 devices in a mesh: row: 8 (over z, core), col: 4 (over y, x).
Axes of the slice: x: 2, y: 2, z: 4, core: 2. Of those that a mesh axis runs over, the one named last changes fastest.
Arguments:
- query: bfloat16 [192, 1024, 128], P('row', 'col'), may hold values from -12 to 12
- key: bfloat16 [192, 1024, 128], P('row', 'col'), may hold values from -6 to 6
- value: bfloat16 [192, 1024, 128], P('row', 'col'), may hold values from -6 to 6
- gate: bfloat16 [192, 1024, 128], P('row', 'col'), may hold values from -6 to 6
- d_out: bfloat16 [192, 1024, 128], P('row', 'col'), may hold values from -6 to 6
- bias: bfloat16 [4, 1024, 1024], P(None, 'col'), may hold values from -6 to 6
- length: int32 [1], replicated, may hold values from 513 to 1024
Outputs:
- d_query: bfloat16 [192, 1024, 128], P('row', 'col')
- d_key: bfloat16 [192, 1024, 128], P('row', 'col')
- d_value: bfloat16 [192, 1024, 128], P('row', 'col')
- d_gate: bfloat16 [192, 1024, 128], P('row', 'col')
- d_bias: float32 [4, 1024, 1024], P(None, 'row', 'col')
The draws below stay inside these ranges and needn't reach their ends.
All inputs are finite; a program needn't handle non-finite values.
Results may differ from the reference program's by a relative error of at most 0.014.
Values may be sent and summed in bfloat16 or wider, within the bound.
No kernel may reach another device: no remote copies, remote signals or barrier semaphores. Data moves between devices by JAX's collectives and lax.ppermute only.
A program may use at most 128 MiB of HBM per device.

```python
import jax
import jax.numpy as jnp
from jax import lax

N = 1024
HEADS = 4
HEAD_DIM = 32
GROUP = 4
HH = 128
NI = 192
BLK = 256
N_COL = 4


def draw_key(key, part):
    base = jax.random.normal(jax.random.fold_in(key, 11), (NI, N, HEADS * HEAD_DIM), jnp.float32)
    base = jnp.clip(base, -6.0, 6.0)
    return base.astype(jnp.bfloat16)


def draw_query(key, part):
    base = jax.random.normal(jax.random.fold_in(key, 13), (NI, N, HEADS * HEAD_DIM), jnp.float32)
    base = jnp.clip(base, -6.0, 6.0)
    return base.astype(jnp.bfloat16)


def shard_levels(key, extent, shards, least, top_value):
    loudness = 1.0
    for position, shards_of in shards:
        draws = jax.random.uniform(jax.random.fold_in(jax.random.fold_in(key, 6), position), (shards_of,), jnp.float32, least / len(shards), top_value / len(shards))
        loudness = loudness * jnp.repeat(jnp.exp(draws), extent[position] // shards_of).reshape((-1,) + (1,) * (len(extent) - 1 - position))
    return loudness


def bell_draw(stream_key, dims, width, bound, cuts=(), held_as=jnp.bfloat16):
    drawn = jax.random.normal(stream_key, dims, jnp.float32) * width
    if len(cuts) > 0:
        drawn = shard_levels(stream_key, dims, cuts, -0.22, 0.18) * drawn
    return jnp.clip(drawn, min=-bound, max=bound).astype(held_as)


def setup_inputs(seed: int = 0) -> dict:
    seeds = jax.random.split(jax.random.key(seed), 8)
    return {
        "query": draw_query(jax.random.fold_in(seeds[7], 71), 0),
        "key": draw_key(jax.random.fold_in(seeds[7], 71), 0),
        "value": bell_draw(seeds[2], (NI, N, HH), 1.0, 6.0, ((0, 8), (1, 4))),
        "gate": bell_draw(seeds[3], (NI, N, HH), 1.0, 6.0, ((0, 8), (1, 4))),
        "d_out": bell_draw(seeds[4], (NI, N, HH), 1.0, 6.0, ((0, 8), (1, 4))),
        "bias": bell_draw(seeds[5], (HEADS, N, N), 1.0, 6.0, ((1, 4),)),
        "length": jax.random.randint(seeds[6], (1,), N // 2 + 1, N + 1).astype(jnp.int32),
    }


def reference(query, key, value, gate, d_out, bias, length):
    scaling = HEAD_DIM ** -0.5
    key_valid = jnp.arange(N) < length[0]
    bias_f = bias.astype(jnp.float32)
    blocks = NI // GROUP

    def split(array):
        return array.reshape(blocks, GROUP, N, HEADS * HEAD_DIM)

    def one_block(bias_sum, pieces):
        query_block, key_block, value_block, gate_block, dout_block = pieces
        q_heads = query_block.astype(jnp.float32).reshape(GROUP, N, HEADS, HEAD_DIM)
        k_heads = key_block.astype(jnp.float32).reshape(GROUP, N, HEADS, HEAD_DIM)
        v_heads = value_block.astype(jnp.float32).reshape(GROUP, N, HEADS, HEAD_DIM)
        logits = jnp.einsum("ijhc,ikhc->ihjk", q_heads, k_heads) * scaling + bias_f[None]
        logits = jnp.where(key_valid, logits, -1e30)
        row_max = jnp.max(logits, axis=-1, keepdims=True)
        exponent = jnp.where(key_valid, jnp.exp(logits - row_max), 0.0)
        weights = exponent / jnp.sum(exponent, axis=-1, keepdims=True)
        weights_bf = weights.astype(jnp.bfloat16).astype(jnp.float32)
        attended = jnp.einsum("ihjk,ikhc->ijhc", weights_bf, v_heads)
        gate_sig = jax.nn.sigmoid(gate_block.astype(jnp.float32).reshape(GROUP, N, HEADS, HEAD_DIM))
        upstream = dout_block.astype(jnp.float32).reshape(GROUP, N, HEADS, HEAD_DIM)
        gate_grad = (upstream * attended * gate_sig * (1.0 - gate_sig)).astype(jnp.bfloat16)
        grad_att = upstream * gate_sig
        row_dot = jnp.sum(grad_att * attended, axis=-1)
        grad_att_bf = grad_att.astype(jnp.bfloat16).astype(jnp.float32)
        grad_weight = jnp.einsum("ijhc,ikhc->ihjk", grad_att_bf, v_heads)
        grad_logits = weights * (grad_weight - jnp.transpose(row_dot, (0, 2, 1))[..., None])
        grad_logits_bf = grad_logits.astype(jnp.bfloat16).astype(jnp.float32)
        query_grad = (jnp.einsum("ihjk,ikhc->ijhc", grad_logits_bf, k_heads) * scaling).astype(jnp.bfloat16)
        grad_split = grad_logits_bf.reshape(GROUP, HEADS, N_COL, BLK, N)
        weight_split = weights_bf.reshape(GROUP, HEADS, N_COL, BLK, N)
        query_split = q_heads.reshape(GROUP, N_COL, BLK, HEADS, HEAD_DIM)
        att_split = grad_att_bf.reshape(GROUP, N_COL, BLK, HEADS, HEAD_DIM)
        key_parts = (jnp.einsum("ihnjk,injhc->nikhc", grad_split, query_split) * scaling).astype(jnp.bfloat16)
        key_parts = lax.optimization_barrier(key_parts)
        key_grad = jnp.sum(key_parts.astype(jnp.float32), axis=0).astype(jnp.bfloat16)
        value_parts = jnp.einsum("ihnjk,injhc->nikhc", weight_split, att_split).astype(jnp.bfloat16)
        value_parts = lax.optimization_barrier(value_parts)
        value_grad = jnp.sum(value_parts.astype(jnp.float32), axis=0).astype(jnp.bfloat16)
        shaped = (GROUP, N, HEADS * HEAD_DIM)
        outputs = (query_grad.reshape(shaped), key_grad.reshape(shaped), value_grad.reshape(shaped), gate_grad.reshape(shaped))
        return bias_sum + jnp.sum(grad_logits, axis=0), outputs

    start = jnp.zeros((HEADS, N, N), jnp.float32)
    bias_grad, stacked = lax.scan(one_block, start, (split(query), split(key), split(value), split(gate), split(d_out)))
    whole = (NI, N, HEADS * HEAD_DIM)
    return (stacked[0].reshape(whole), stacked[1].reshape(whole), stacked[2].reshape(whole), stacked[3].reshape(whole), bias_grad)
```

```python
import functools

import jax
import jax.numpy as jnp
from jax import lax
from jax.experimental import pallas as pl
from jax.experimental.pallas import tpu as pltpu
from jax.sharding import PartitionSpec as P

LOG2E = 1.4426950408889634
MASKED = -1e30
CHUNKS = 4
PIECES = 4


def dot(a, b, dims):
    return lax.dot_general(a, b, (dims, ((), ())), preferred_element_type=jnp.float32)


def peer_of(me, step):
    return jnp.bitwise_xor(me, step)


def pack_kernel(heads, groups, info, q_ref, k_ref, v_ref, g_ref, o_ref, *refs):
    outs, turned = refs[:-1], refs[-1]
    me = info[0]
    c = q_ref.shape[3] // heads

    @pl.loop(0, q_ref.shape[1])
    def _(i):
        for g in range(groups):
            gated = o_ref[g, i].astype(jnp.float32) * jax.nn.sigmoid(g_ref[g, i].astype(jnp.float32))
            pieces = (q_ref[g, i], k_ref[g, i], v_ref[g, i], gated.astype(jnp.bfloat16))
            for piece, x in enumerate(pieces):
                turned[g, piece] = x.T
        for step in range(heads * groups):
            peer = peer_of(me, step)
            at = pl.multiple_of(peer // groups * c, c)
            for piece in range(PIECES):
                outs[step][piece, i] = turned[peer % groups, piece, pl.ds(at, c), :]


def unpack_kernel(heads, groups, info, g_ref, o_ref, *refs):
    ins, (dq, dk, dv, dg), whole = refs[: heads * groups], refs[-5:-1], refs[-1]
    me = info[0]
    c = ins[0].shape[2]

    @pl.loop(0, g_ref.shape[1])
    def _(i):
        for step in range(heads * groups):
            peer = peer_of(me, step)
            at = pl.multiple_of(peer // groups * c, c)
            for piece in range(PIECES):
                whole[peer % groups, piece, pl.ds(at, c), :] = ins[step][piece, i]
        for g in range(groups):
            dq[g, i] = whole[g, 0].T
            dk[g, i] = whole[g, 1].T
            dv[g, i] = whole[g, 2].T
            attended = whole[g, 3].T.astype(jnp.float32)
            s = jax.nn.sigmoid(g_ref[g, i].astype(jnp.float32))
            dg[g, i] = (o_ref[g, i].astype(jnp.float32) * attended * s * (1.0 - s)).astype(jnp.bfloat16)


def attention_kernel(n_col, scaling, first, info, bias_ref, *refs):
    if not first:
        total_in, refs = refs[0], refs[1:]
    ins, outs, total = refs[:n_col], refs[n_col : 2 * n_col], refs[2 * n_col]
    bias, q_s, g_s, k_s, v_s, dq_s, at_s, dkv, dkv_t = refs[2 * n_col + 1 :]
    me, length = info[0], info[1]
    c, blk = ins[0].shape[2], ins[0].shape[3]
    n = n_col * blk
    extra = k_s.shape[0] - 2 * c
    step_i = pl.program_id(0)

    @pl.when(step_i == 0)
    def _():
        for jb in range(n_col):
            bias[jb] = bias_ref[:, jb].reshape(n, blk).astype(jnp.float32) * LOG2E
        if first:
            total[...] = jnp.zeros_like(total)
        else:
            total[...] = total_in[...]
        rows = lax.broadcasted_iota(jnp.int32, (extra, n), 0)
        keys = lax.broadcasted_iota(jnp.int32, (extra, n), 1)
        k_s[2 * c :, :] = jnp.where(
            jnp.logical_and(rows == 0, keys >= length), MASKED, 0.0
        ).astype(jnp.bfloat16)
        v_s[c:, :] = jnp.ones((v_s.shape[0] - c, n), jnp.bfloat16)
        q_s[:, 2 * c :, :] = jnp.ones((n_col, extra, blk), jnp.bfloat16)

    for step in range(n_col):
        peer = peer_of(me, step)
        at = pl.multiple_of(peer * blk, blk)
        q = ins[step][0, 0].astype(jnp.float32) * (scaling * LOG2E)
        high = q.astype(jnp.bfloat16)
        q_s[peer, :c, :] = high
        q_s[peer, c : 2 * c, :] = (q - high.astype(jnp.float32)).astype(jnp.bfloat16)
        k = ins[step][1, 0]
        k_s[:c, pl.ds(at, blk)] = k
        k_s[c : 2 * c, pl.ds(at, blk)] = k
        v_s[:c, pl.ds(at, blk)] = ins[step][2, 0]
        g_s[peer] = ins[step][3, 0]

    dkv[...] = jnp.zeros_like(dkv)

    @pl.loop(0, n_col)
    def _(jb):
        logits = dot(k_s[...], q_s[jb], ((0,), (0,))) + bias[jb]
        weights = jnp.exp2(logits - jnp.max(logits, axis=0, keepdims=True)).astype(jnp.bfloat16)
        summed = dot(v_s[...], weights, ((1,), (0,)))
        inverse = 1.0 / summed[c : c + 1, :]
        attended = summed[:c, :] * inverse
        at_s[jb] = attended.astype(jnp.bfloat16)
        g = g_s[jb].astype(jnp.float32)
        row_dot = jnp.sum(g * attended, axis=0, keepdims=True) * (-inverse)
        high = row_dot.astype(jnp.bfloat16).astype(jnp.float32)
        low = row_dot - high
        rows = lax.broadcasted_iota(jnp.int32, (v_s.shape[0] - c, blk), 0)
        tail = jnp.where(rows == 0, high, jnp.where(rows == 1, low, 0.0)).astype(jnp.bfloat16)
        g_scaled = (g * inverse).astype(jnp.bfloat16)
        grad_weight = dot(v_s[...], jnp.concatenate([g_scaled, tail], axis=0), ((0,), (0,)))
        grad = weights.astype(jnp.float32) * grad_weight
        total[jb] += grad
        grad = grad.astype(jnp.bfloat16)
        dq_s[jb] = (dot(k_s[:c, :], grad, ((1,), (0,))) * scaling).astype(jnp.bfloat16)
        q_back = q_s[jb, :c, :]
        dkv[:, :c] += dot(grad, q_back, ((1,), (1,)))
        dkv[:, c : 2 * c] += dot(weights, g_scaled, ((1,), (1,)))

    dkv_t[...] = dkv[...].T
    for step in range(n_col):
        peer = peer_of(me, step)
        at = pl.multiple_of(peer * blk, blk)
        outs[step][0, 0] = dq_s[peer]
        outs[step][1, 0] = (dkv_t[:c, pl.ds(at, blk)] * (1.0 / LOG2E)).astype(jnp.bfloat16)
        outs[step][2, 0] = dkv_t[c : 2 * c, pl.ds(at, blk)].astype(jnp.bfloat16)
        outs[step][3, 0] = at_s[peer]


def params(mib):
    return pltpu.CompilerParams(
        dimension_semantics=("arbitrary",), vmem_limit_bytes=mib * 1024 * 1024
    )


def on_device(n_row, n_col, query, key, value, gate, d_out, bias, length):
    rows, blk, channels = query.shape
    heads, _, n = bias.shape
    c = channels // heads
    groups = n_col // heads
    assert groups * heads == n_col and n == n_col * blk and rows % (CHUNKS * groups) == 0
    scaling = c ** (-0.5)
    chunk = rows // (CHUNKS * groups)
    per = 3 if chunk % 3 == 0 else 1
    split_rows = (CHUNKS * groups, chunk, blk, channels)
    query, key, value, gate, d_out = (x.reshape(split_rows) for x in (query, key, value, gate, d_out))
    row, me = lax.axis_index("row"), lax.axis_index("col")
    info = jnp.stack([me.astype(jnp.int32), length[0].astype(jnp.int32)])
    width = n // n_row

    part = lax.dynamic_slice_in_dim(bias, row * width, width, axis=2)
    part = jnp.repeat(jnp.transpose(part, (0, 2, 1)), groups, axis=0)
    part = lax.all_to_all(part, "col", split_axis=0, concat_axis=0, tiled=True)
    part = jnp.transpose(part, (1, 0, 2))
    bias_head = lax.all_gather(part, "row", axis=0, tiled=True)

    def exchange(pieces):
        moved = [pieces[0]]
        for step in range(1, n_col):
            pairs = [(a, a ^ step) for a in range(n_col)]
            moved.append(lax.ppermute(pieces[step], "col", pairs))
        return moved

    piece_shape = jax.ShapeDtypeStruct((PIECES, chunk, c, blk), jnp.bfloat16)

    def pack(m):
        whole = pl.BlockSpec((groups, per, blk, channels), lambda i, info: (m, i, 0, 0))
        return pl.pallas_call(
            functools.partial(pack_kernel, heads, groups),
            grid_spec=pltpu.PrefetchScalarGridSpec(
                num_scalar_prefetch=1,
                grid=(chunk // per,),
                in_specs=[whole] * 5,
                out_specs=[pl.BlockSpec((PIECES, per, c, blk), lambda i, info: (0, i, 0, 0))] * n_col,
                scratch_shapes=[pltpu.VMEM((groups, PIECES, channels, blk), jnp.bfloat16)],
            ),
            out_shape=[piece_shape] * n_col,
            compiler_params=params(32),
            cost_estimate=pl.CostEstimate(
                flops=chunk * 10**6, bytes_accessed=chunk * blk * channels * 18, transcendentals=0
            ),
            name="pack",
        )(info, query, key, value, gate, d_out)

    def attend(total, pieces):
        first = total is None
        one = pl.BlockSpec((PIECES, 1, c, blk), lambda i, info: (0, i, 0, 0))
        still = pl.BlockSpec((n_col, n, blk), lambda i, info: (0, 0, 0), pipeline_mode=pl.Buffered(1))
        kept = [] if first else [total]
        depth = 2 * c + 16
        result = pl.pallas_call(
            functools.partial(attention_kernel, n_col, scaling, first),
            grid_spec=pltpu.PrefetchScalarGridSpec(
                num_scalar_prefetch=1,
                grid=(chunk,),
                in_specs=[
                    pl.BlockSpec(
                        (n, n_col, blk), lambda i, info: (0, 0, 0), pipeline_mode=pl.Buffered(1)
                    )
                ]
                + [still] * len(kept)
                + [one] * n_col,
                out_specs=[one] * n_col + [still],
                scratch_shapes=[
                    pltpu.VMEM((n_col, n, blk), jnp.float32),
                    pltpu.VMEM((n_col, depth, blk), jnp.bfloat16),
                    pltpu.VMEM((n_col, c, blk), jnp.bfloat16),
                    pltpu.VMEM((depth, n), jnp.bfloat16),
                    pltpu.VMEM((c + 16, n), jnp.bfloat16),
                    pltpu.VMEM((n_col, c, blk), jnp.bfloat16),
                    pltpu.VMEM((n_col, c, blk), jnp.bfloat16),
                    pltpu.VMEM((n, 2 * c), jnp.float32),
                    pltpu.VMEM((2 * c, n), jnp.float32),
                ],
            ),
            out_shape=[piece_shape] * n_col + [jax.ShapeDtypeStruct((n_col, n, blk), jnp.float32)],
            compiler_params=params(56),
            cost_estimate=pl.CostEstimate(
                flops=chunk * 4 * 10**9, bytes_accessed=10**7, transcendentals=chunk * n * n
            ),
            name="attend",
        )(info, bias_head, *kept, *pieces)
        return result[:n_col], result[n_col]

    def unpack(m, pieces, grads):
        whole = pl.BlockSpec((groups, per, blk, channels), lambda i, info: (m, i, 0, 0))
        kept = [] if grads is None else list(grads)
        return pl.pallas_call(
            functools.partial(unpack_kernel, heads, groups),
            grid_spec=pltpu.PrefetchScalarGridSpec(
                num_scalar_prefetch=1,
                grid=(chunk // per,),
                in_specs=[whole] * 2
                + [pl.BlockSpec((PIECES, per, c, blk), lambda i, info: (0, i, 0, 0))] * n_col
                + [pl.BlockSpec(memory_space=pl.ANY)] * len(kept),
                out_specs=[whole] * 4,
                scratch_shapes=[pltpu.VMEM((groups, PIECES, channels, blk), jnp.bfloat16)],
            ),
            out_shape=[jax.ShapeDtypeStruct(query.shape, jnp.bfloat16)] * 4,
            input_output_aliases={3 + n_col + a: a for a in range(len(kept))},
            compiler_params=params(32),
            cost_estimate=pl.CostEstimate(
                flops=chunk * 10**6, bytes_accessed=chunk * blk * channels * 18, transcendentals=0
            ),
            name="unpack",
        )(info, gate, d_out, *pieces, *kept)

    arrived = [exchange(pack(m)) for m in range(CHUNKS)]
    total, sent = None, []
    for m in range(CHUNKS):
        results, total = attend(total, arrived[m])
        sent.append(exchange(results))
    grads = None
    for m in range(CHUNKS):
        grads = unpack(m, sent[m], grads)

    split = n_row // n_col
    total = total.astype(jnp.bfloat16).reshape(n_col, n, split, width)
    total = jnp.transpose(total, (0, 2, 1, 3)).reshape(n_row, n, width)
    total = lax.psum_scatter(total, "row", scatter_dimension=0, tiled=False)
    total = total.reshape(n_col, blk, width)
    total = lax.all_to_all(total, "col", split_axis=0, concat_axis=0, tiled=True)
    total = jnp.sum(total.reshape(heads, groups, blk, width).astype(jnp.float32), axis=1)
    bias_grad = jnp.transpose(total, (0, 2, 1))
    d_query, d_key, d_value, d_gate = (x.reshape(rows, blk, channels) for x in grads)
    return d_query, d_key, d_value, d_gate, bias_grad


def solution(mesh):
    pair = P("row", "col", None)
    return jax.shard_map(
        functools.partial(on_device, mesh.shape["row"], mesh.shape["col"]),
        mesh=mesh,
        in_specs=(pair, pair, pair, pair, pair, P(None, "col", None), P()),
        out_specs=(pair, pair, pair, pair, P(None, "row", "col")),
        check_vma=False,
    )
```

```python
import functools

import jax
import jax.numpy as jnp
from jax import lax
from jax.experimental import pallas as pl
from jax.experimental.pallas import tpu as pltpu
from jax.sharding import PartitionSpec as P

LOG2E = 1.4426950408889634
MASKED = -1e30
CHUNKS = 4
PIECES = 4


def dot(a, b, dims):
    return lax.dot_general(a, b, (dims, ((), ())), preferred_element_type=jnp.float32)


def peer_of(me, step):
    return jnp.bitwise_xor(me, step)


def pack_kernel(heads, groups, info, q_ref, k_ref, v_ref, g_ref, o_ref, *refs):
    outs, turned = refs[:-1], refs[-1]
    me = info[0]
    c = q_ref.shape[3] // heads

    @pl.loop(0, q_ref.shape[1])
    def _(i):
        for g in range(groups):
            gated = o_ref[g, i].astype(jnp.float32) * jax.nn.sigmoid(g_ref[g, i].astype(jnp.float32))
            pieces = (q_ref[g, i], k_ref[g, i], v_ref[g, i], gated.astype(jnp.bfloat16))
            for piece, x in enumerate(pieces):
                turned[g, piece] = x.T
        for step in range(heads * groups):
            peer = peer_of(me, step)
            at = pl.multiple_of(peer // groups * c, c)
            for piece in range(PIECES):
                outs[step][piece, i] = turned[peer % groups, piece, pl.ds(at, c), :]


def unpack_kernel(heads, groups, info, g_ref, o_ref, *refs):
    ins, (dq, dk, dv, dg), whole = refs[: heads * groups], refs[-6:-2], refs[-1]
    refs[-2][...] = jnp.zeros_like(refs[-2])
    me = info[0]
    c = ins[0].shape[2]

    @pl.loop(0, g_ref.shape[1])
    def _(i):
        for step in range(heads * groups):
            peer = peer_of(me, step)
            at = pl.multiple_of(peer // groups * c, c)
            for piece in range(PIECES):
                whole[peer % groups, piece, pl.ds(at, c), :] = ins[step][piece, i]
        for g in range(groups):
            dq[g, i] = whole[g, 0].T
            dk[g, i] = whole[g, 1].T
            dv[g, i] = whole[g, 2].T
            attended = whole[g, 3].T.astype(jnp.float32)
            s = jax.nn.sigmoid(g_ref[g, i].astype(jnp.float32))
            dg[g, i] = (o_ref[g, i].astype(jnp.float32) * attended * s * (1.0 - s)).astype(jnp.bfloat16)


def bias_kernel(n_col, info, *refs):
    ins, out = refs[:n_col], refs[n_col]
    for step in range(n_col):
        out[peer_of(info[0], step)] = ins[step][...].astype(jnp.float32).T * LOG2E


def attention_kernel(n_col, scaling, first, info, bias, *refs):
    if not first:
        total_in, refs = refs[0], refs[1:]
    ins, refs = refs[:n_col], refs[n_col:]
    outs, total = refs[-n_col - 13 : -13], refs[-13]
    q_s, g_s, k_s, v_s, k_turned, v_turned, dq_s, at_s, dkv, logits, weights, grads = refs[-12:]
    me, length = info[0], info[1]
    together, c, blk = ins[0].shape[1:]
    n = n_col * blk
    tile = min(256, n)
    deep = k_s.shape[1]
    some = range(together)

    @pl.when(pl.program_id(0) == 0)
    def _():
        if first:
            total[...] = jnp.zeros_like(total)
        else:
            total[...] = total_in[...]
        rows = lax.broadcasted_iota(jnp.int32, (deep - 2 * c, n), 0)
        keys = lax.broadcasted_iota(jnp.int32, (deep - 2 * c, n), 1)
        mask = jnp.logical_and(rows == 0, keys >= length)
        for r in some:
            k_s[r, 2 * c :, :] = jnp.where(mask, MASKED, 0.0).astype(jnp.bfloat16)
            v_s[r, c:, :] = jnp.ones((deep - c, n), jnp.bfloat16)
            q_s[r, :, 2 * c :, :] = jnp.ones((n_col, deep - 2 * c, blk), jnp.bfloat16)

    for r in some:
        for step in range(n_col):
            peer = peer_of(me, step)
            at = pl.multiple_of(peer * blk, blk)
            q = ins[step][0, r].astype(jnp.float32) * (scaling * LOG2E)
            high = q.astype(jnp.bfloat16)
            q_s[r, peer, :c, :] = high
            q_s[r, peer, c : 2 * c, :] = (q - high.astype(jnp.float32)).astype(jnp.bfloat16)
            k = ins[step][1, r]
            k_s[r, :c, pl.ds(at, blk)] = k
            k_s[r, c : 2 * c, pl.ds(at, blk)] = k
            v_s[r, :c, pl.ds(at, blk)] = ins[step][2, r]
            g_s[r, peer] = ins[step][3, r]
    for r in some:
        k_turned[r] = k_s[r].T
        v_turned[r] = v_s[r].T
    dkv[...] = jnp.zeros_like(dkv)

    @pl.loop(0, n_col)
    def _(jb):
        scaled, scales = [], []
        for r in some:
            top = jnp.full((8, blk), -jnp.inf, jnp.float32)
            for t in range(0, n, tile):
                part = dot(k_turned[r, t : t + tile, :], q_s[r, jb], ((1,), (0,)))
                part = part + bias[jb, t : t + tile, :]
                logits[r, t : t + tile, :] = part
                top = jnp.maximum(top, jnp.max(part.reshape(tile // 8, 8, blk), axis=0))
            top = jnp.max(top, axis=0, keepdims=True)
            for t in range(0, n, tile):
                part = jnp.exp2(logits[r, t : t + tile, :] - top)
                weights[r, t : t + tile, :] = part.astype(jnp.bfloat16)
            summed = dot(v_s[r, : c + 16, :], weights[r], ((1,), (0,)))
            inverse = 1.0 / summed[c : c + 1, :]
            attended = summed[:c, :] * inverse
            at_s[r, jb] = attended.astype(jnp.bfloat16)
            g = g_s[r, jb].astype(jnp.float32)
            row_dot = jnp.sum(g * attended, axis=0, keepdims=True) * (-inverse)
            high = row_dot.astype(jnp.bfloat16).astype(jnp.float32)
            rows = lax.broadcasted_iota(jnp.int32, (deep - c, blk), 0)
            tail = jnp.where(rows == 0, high, jnp.where(rows == 1, row_dot - high, 0.0))
            g_scaled = (g * inverse).astype(jnp.bfloat16)
            scaled.append(g_scaled)
            scales.append(jnp.concatenate([g_scaled, tail.astype(jnp.bfloat16)], axis=0))
        for t in range(0, n, tile):
            added = total[jb, t : t + tile, :]
            for r in some:
                grad = dot(v_turned[r, t : t + tile, :], scales[r], ((1,), (0,)))
                grad = grad * weights[r, t : t + tile, :].astype(jnp.float32)
                added = added + grad
                grads[r, t : t + tile, :] = grad.astype(jnp.bfloat16)
            total[jb, t : t + tile, :] = added
        for r in some:
            dq_s[r, jb] = (dot(k_s[r, :c, :], grads[r], ((1,), (0,))) * scaling).astype(jnp.bfloat16)
            dkv[r, :c, :] += dot(q_s[r, jb, :c, :], grads[r], ((1,), (1,)))
            dkv[r, c:, :] += dot(scaled[r], weights[r], ((1,), (1,)))

    for r in some:
        for step in range(n_col):
            peer = peer_of(me, step)
            at = pl.multiple_of(peer * blk, blk)
            outs[step][0, r] = dq_s[r, peer]
            outs[step][1, r] = (dkv[r, :c, pl.ds(at, blk)] * (1.0 / LOG2E)).astype(jnp.bfloat16)
            outs[step][2, r] = dkv[r, c:, pl.ds(at, blk)].astype(jnp.bfloat16)
            outs[step][3, r] = at_s[r, peer]


def params(mib):
    return pltpu.CompilerParams(
        dimension_semantics=("arbitrary",), vmem_limit_bytes=mib * 1024 * 1024
    )


def on_device(n_row, n_col, query, key, value, gate, d_out, bias, length):
    rows, blk, channels = query.shape
    heads, _, n = bias.shape
    c = channels // heads
    groups = n_col // heads
    assert groups * heads == n_col and n == n_col * blk and rows % (CHUNKS * groups) == 0
    scaling = c ** (-0.5)
    chunk = rows // (CHUNKS * groups)
    per = 3 if chunk % 3 == 0 else 1
    split_rows = (CHUNKS * groups, chunk, blk, channels)
    query, key, value, gate, d_out = (x.reshape(split_rows) for x in (query, key, value, gate, d_out))
    row, me = lax.axis_index("row"), lax.axis_index("col")
    info = jnp.stack([me.astype(jnp.int32), length[0].astype(jnp.int32)])
    width = n // n_row

    def exchange(pieces):
        moved = [pieces[0]]
        for step in range(1, n_col):
            pairs = [(a, a ^ step) for a in range(n_col)]
            moved.append(lax.ppermute(pieces[step], "col", pairs))
        return moved

    tables = [lax.dynamic_index_in_dim(bias, peer_of(me, step) // groups, 0, False) for step in range(n_col)]
    bias_head = pl.pallas_call(
        functools.partial(bias_kernel, n_col),
        grid_spec=pltpu.PrefetchScalarGridSpec(
            num_scalar_prefetch=1,
            grid=(n // blk,),
            in_specs=[pl.BlockSpec((blk, blk), lambda i, info: (0, i))] * n_col,
            out_specs=pl.BlockSpec((n_col, blk, blk), lambda i, info: (0, i, 0)),
        ),
        out_shape=jax.ShapeDtypeStruct((n_col, n, blk), jnp.float32),
        compiler_params=params(60),
        cost_estimate=pl.CostEstimate(flops=10**7, bytes_accessed=n * n * 6, transcendentals=0),
        name="turn_bias",
    )(info, *exchange(tables))

    piece_shape = jax.ShapeDtypeStruct((PIECES, chunk, c, blk), jnp.bfloat16)

    def pack(m):
        whole = pl.BlockSpec((groups, per, blk, channels), lambda i, info: (m, i, 0, 0))
        return pl.pallas_call(
            functools.partial(pack_kernel, heads, groups),
            grid_spec=pltpu.PrefetchScalarGridSpec(
                num_scalar_prefetch=1,
                grid=(chunk // per,),
                in_specs=[whole] * 5,
                out_specs=[pl.BlockSpec((PIECES, per, c, blk), lambda i, info: (0, i, 0, 0))] * n_col,
                scratch_shapes=[pltpu.VMEM((groups, PIECES, channels, blk), jnp.bfloat16)],
            ),
            out_shape=[piece_shape] * n_col,
            compiler_params=params(60),
            cost_estimate=pl.CostEstimate(
                flops=chunk * 10**6, bytes_accessed=chunk * blk * channels * 18, transcendentals=0
            ),
            name="pack",
        )(info, query, key, value, gate, d_out)

    def attend(total, pieces, after):
        first = total is None
        together = 2 if chunk % 2 == 0 else 1
        some = pl.BlockSpec((PIECES, together, c, blk), lambda i, info: (0, i, 0, 0))
        still = pl.BlockSpec((n_col, n, blk), lambda i, info: (0, 0, 0), pipeline_mode=pl.Buffered(1))
        kept = [] if first else [total]
        deep = 4 * c

        def scratch(*shape, dtype=jnp.bfloat16):
            return pltpu.VMEM((together, *shape), dtype)

        result = pl.pallas_call(
            functools.partial(attention_kernel, n_col, scaling, first),
            grid_spec=pltpu.PrefetchScalarGridSpec(
                num_scalar_prefetch=1,
                grid=(chunk // together,),
                in_specs=[still] * (1 + len(kept))
                + [some] * n_col
                + [pl.BlockSpec(memory_space=pl.ANY)] * len(after),
                out_specs=[some] * n_col + [still],
                scratch_shapes=[
                    scratch(n_col, deep, blk),
                    scratch(n_col, c, blk),
                    scratch(deep, n),
                    scratch(deep, n),
                    scratch(n, deep),
                    scratch(n, deep),
                    scratch(n_col, c, blk),
                    scratch(n_col, c, blk),
                    scratch(2 * c, n, dtype=jnp.float32),
                    scratch(n, blk, dtype=jnp.float32),
                    scratch(n, blk),
                    scratch(n, blk),
                ],
            ),
            out_shape=[piece_shape] * n_col + [jax.ShapeDtypeStruct((n_col, n, blk), jnp.float32)],
            compiler_params=params(60),
            cost_estimate=pl.CostEstimate(
                flops=chunk * 4 * 10**9, bytes_accessed=10**7, transcendentals=chunk * n * n
            ),
            name="attend",
        )(info, bias_head, *kept, *pieces, *after)
        return result[:n_col], result[n_col]

    def unpack(m, pieces, grads):
        whole = pl.BlockSpec((groups, per, blk, channels), lambda i, info: (m, i, 0, 0))
        kept = [] if grads is None else list(grads)
        return pl.pallas_call(
            functools.partial(unpack_kernel, heads, groups),
            grid_spec=pltpu.PrefetchScalarGridSpec(
                num_scalar_prefetch=1,
                grid=(chunk // per,),
                in_specs=[whole] * 2
                + [pl.BlockSpec((PIECES, per, c, blk), lambda i, info: (0, i, 0, 0))] * n_col
                + [pl.BlockSpec(memory_space=pl.ANY)] * len(kept),
                out_specs=[whole] * 4 + [pl.BlockSpec((8, 128), lambda i, info: (0, 0))],
                scratch_shapes=[pltpu.VMEM((groups, PIECES, channels, blk), jnp.bfloat16)],
            ),
            out_shape=[jax.ShapeDtypeStruct(query.shape, jnp.bfloat16)] * 4
            + [jax.ShapeDtypeStruct((8, 128), jnp.float32)],
            input_output_aliases={3 + n_col + a: a for a in range(len(kept))},
            compiler_params=params(60),
            cost_estimate=pl.CostEstimate(
                flops=chunk * 10**6, bytes_accessed=chunk * blk * channels * 18, transcendentals=0
            ),
            name="unpack",
        )(info, gate, d_out, *pieces, *kept)

    arrived = [exchange(pack(m)) for m in range(CHUNKS)]
    total, sent, grads, home = None, [], None, []
    for m in range(CHUNKS):
        results, total = attend(total, arrived[m], home[m - 2 : m - 1] if m >= 2 else [])
        sent.append(exchange(results))
        if m >= 1:
            *grads, token = unpack(m - 1, sent[m - 1], grads)
            home.append(token)
    *grads, _ = unpack(CHUNKS - 1, sent[-1], grads)

    split = n_row // n_col
    total = total.astype(jnp.bfloat16).reshape(n_col, n, split, width)
    total = jnp.transpose(total, (0, 2, 1, 3)).reshape(n_row, n, width)
    total = lax.psum_scatter(total, "row", scatter_dimension=0, tiled=False)
    total = total.reshape(n_col, blk, width)
    total = lax.all_to_all(total, "col", split_axis=0, concat_axis=0, tiled=True)
    total = jnp.sum(total.reshape(heads, groups, blk, width).astype(jnp.float32), axis=1)
    bias_grad = jnp.transpose(total, (0, 2, 1))
    d_query, d_key, d_value, d_gate = (x.reshape(rows, blk, channels) for x in grads)
    return d_query, d_key, d_value, d_gate, bias_grad


def solution(mesh):
    pair = P("row", "col", None)
    return jax.shard_map(
        functools.partial(on_device, mesh.shape["row"], mesh.shape["col"]),
        mesh=mesh,
        in_specs=(pair, pair, pair, pair, pair, P(None, "col", None), P()),
        out_specs=(pair, pair, pair, pair, P(None, "row", "col")),
        check_vma=False,
    )
```

```python
import functools
import itertools

import jax
import jax.numpy as jnp
from jax import lax
from jax.experimental import pallas as pl
from jax.experimental.pallas import tpu as pltpu
from jax.sharding import PartitionSpec as P

LOG2E = 1.4426950408889634
MASKED = -1e30
SHARES = (1, 2, 2, 1)
PIECES = 4


def dot(a, b, dims):
    return lax.dot_general(a, b, (dims, ((), ())), preferred_element_type=jnp.float32)


def peer_of(me, step):
    return jnp.bitwise_xor(me, step)


def pack_kernel(heads, groups, info, q_ref, k_ref, v_ref, g_ref, o_ref, *refs):
    outs, turned = refs[:-1], refs[-1]
    me = info[0]
    c = q_ref.shape[3] // heads

    @pl.loop(0, q_ref.shape[1])
    def _(i):
        for g in range(groups):
            gated = o_ref[g, i].astype(jnp.float32) * jax.nn.sigmoid(g_ref[g, i].astype(jnp.float32))
            pieces = (q_ref[g, i], k_ref[g, i], v_ref[g, i], gated.astype(jnp.bfloat16))
            for piece, x in enumerate(pieces):
                turned[g, piece] = x.T
        for step in range(heads * groups):
            peer = peer_of(me, step)
            at = pl.multiple_of(peer // groups * c, c)
            for piece in range(PIECES):
                outs[step][piece, i] = turned[peer % groups, piece, pl.ds(at, c), :]


def unpack_kernel(heads, groups, info, g_ref, o_ref, *refs):
    ins, (dq, dk, dv, dg), whole = refs[: heads * groups], refs[-6:-2], refs[-1]
    refs[-2][...] = jnp.zeros_like(refs[-2])
    me = info[0]
    c = ins[0].shape[2]

    @pl.loop(0, g_ref.shape[1])
    def _(i):
        for step in range(heads * groups):
            peer = peer_of(me, step)
            at = pl.multiple_of(peer // groups * c, c)
            for piece in range(PIECES):
                whole[peer % groups, piece, pl.ds(at, c), :] = ins[step][piece, i]
        for g in range(groups):
            dq[g, i] = whole[g, 0].T
            dk[g, i] = whole[g, 1].T
            dv[g, i] = whole[g, 2].T
            attended = whole[g, 3].T.astype(jnp.float32)
            s = jax.nn.sigmoid(g_ref[g, i].astype(jnp.float32))
            dg[g, i] = (o_ref[g, i].astype(jnp.float32) * attended * s * (1.0 - s)).astype(jnp.bfloat16)


def bias_kernel(n_col, info, *refs):
    ins, out = refs[:n_col], refs[n_col]
    for step in range(n_col):
        out[peer_of(info[0], step)] = ins[step][...].T


def woven(*queues):
    order = [(at / len(q), which, at) for which, q in enumerate(queues) for at in range(len(q))]
    for _, which, at in sorted(order):
        queues[which][at]()


def attention_kernel(n_col, scaling, first, last, info, bias_own, bias_other, *refs):
    if not first:
        total_in, refs = refs[0], refs[1:]
    ins, refs = refs[:n_col], refs[n_col:]
    scratch = refs[-14:]
    outs, total_out = refs[-15 - n_col : -15], refs[-15]
    bias, total_s, q_s, g_s, k_s, v_s, k_turned, v_turned, dq_s, at_s, dkv, logits, weights, grads = scratch
    total = total_s if last else total_out
    me, length, side = info[0], info[1], info[2]
    together, c, blk = ins[0].shape[1:]
    n = n_col * blk
    half = n // 2
    tile = min(256, n)
    tiles = range(0, n, tile)
    deep = k_s.shape[1]
    some = range(together)

    @pl.when(pl.program_id(0) == 0)
    def _():
        for part, which in ((bias_own, side), (bias_other, 1 - side)):
            at = pl.multiple_of(which * half, half)
            for jb in range(n_col):
                bias[jb, pl.ds(at, half), :] = part[jb].astype(jnp.float32) * LOG2E
        if first:
            total[...] = jnp.zeros_like(total)
        else:
            total[...] = total_in[...]
        rows = lax.broadcasted_iota(jnp.int32, (deep - 2 * c, n), 0)
        keys = lax.broadcasted_iota(jnp.int32, (deep - 2 * c, n), 1)
        mask = jnp.logical_and(rows == 0, keys >= length)
        for r in some:
            k_s[r, 2 * c :, :] = jnp.where(mask, MASKED, 0.0).astype(jnp.bfloat16)
            v_s[r, c:, :] = jnp.ones((deep - c, n), jnp.bfloat16)
            q_s[r, :, 2 * c :, :] = jnp.ones((n_col, deep - 2 * c, blk), jnp.bfloat16)

    for r in some:
        for step in range(n_col):
            peer = peer_of(me, step)
            at = pl.multiple_of(peer * blk, blk)
            q = ins[step][0, r].astype(jnp.float32) * (scaling * LOG2E)
            high = q.astype(jnp.bfloat16)
            q_s[r, peer, :c, :] = high
            q_s[r, peer, c : 2 * c, :] = (q - high.astype(jnp.float32)).astype(jnp.bfloat16)
            k = ins[step][1, r]
            k_s[r, :c, pl.ds(at, blk)] = k
            k_s[r, c : 2 * c, pl.ds(at, blk)] = k
            v_s[r, :c, pl.ds(at, blk)] = ins[step][2, r]
            g_s[r, peer] = ins[step][3, r]
    for r in some:
        k_turned[r] = k_s[r].T
        v_turned[r] = v_s[r].T
    tops, scaled, scales = {}, {}, {}

    def score(jb, r, t):
        part = dot(k_turned[r, t : t + tile, :], q_s[r, jb], ((1,), (0,))) + bias[jb, t : t + tile, :]
        logits[jb % 2, r, t : t + tile, :] = part
        top = jnp.max(part.reshape(tile // 8, 8, blk), axis=0)
        tops[jb, r] = jnp.maximum(tops[jb, r], top) if t else top

    def expand(jb, r, t):
        if t == 0:
            tops[jb, r] = jnp.max(tops[jb, r], axis=0, keepdims=True)
        part = jnp.exp2(logits[jb % 2, r, t : t + tile, :] - tops[jb, r])
        weights[jb % 2, r, t : t + tile, :] = part.astype(jnp.bfloat16)

    def attend(jb, r):
        summed = dot(v_s[r, : c + 16, :], weights[jb % 2, r], ((1,), (0,)))
        inverse = 1.0 / summed[c : c + 1, :]
        attended = summed[:c, :] * inverse
        at_s[r, jb] = attended.astype(jnp.bfloat16)
        g = g_s[r, jb].astype(jnp.float32)
        row_dot = jnp.sum(g * attended, axis=0, keepdims=True) * (-inverse)
        high = row_dot.astype(jnp.bfloat16).astype(jnp.float32)
        rows = lax.broadcasted_iota(jnp.int32, (deep - c, blk), 0)
        tail = jnp.where(rows == 0, high, jnp.where(rows == 1, row_dot - high, 0.0))
        scaled[jb, r] = (g * inverse).astype(jnp.bfloat16)
        scales[jb, r] = jnp.concatenate([scaled[jb, r], tail.astype(jnp.bfloat16)], axis=0)

    def back(jb, t):
        added = total[jb, t : t + tile, :]
        for r in some:
            grad = dot(v_turned[r, t : t + tile, :], scales[jb, r], ((1,), (0,)))
            grad = grad * weights[jb % 2, r, t : t + tile, :].astype(jnp.float32)
            added = added + grad
            grads[jb % 2, r, t : t + tile, :] = grad.astype(jnp.bfloat16)
        total[jb, t : t + tile, :] = added

    def query_grad(jb, r):
        dq_s[r, jb] = (dot(k_s[r, :c, :], grads[jb % 2, r], ((1,), (0,))) * scaling).astype(jnp.bfloat16)

    def add_to(at, r, jb, part):
        if jb:
            part = part + dkv[r, at : at + c, :]
        dkv[r, at : at + c, :] = part

    def key_grad(jb, r):
        add_to(0, r, jb, dot(q_s[r, jb, :c, :], grads[jb % 2, r], ((1,), (1,))))

    def value_grad(jb, r):
        add_to(c, r, jb, dot(scaled[jb, r], weights[jb % 2, r], ((1,), (1,))))

    def each(step, jb, *ranges):
        if not 0 <= jb < n_col:
            return []
        return [functools.partial(step, jb, *at) for at in itertools.product(*ranges)]

    def finish(jb):
        return each(value_grad, jb, some) + each(query_grad, jb, some) + each(key_grad, jb, some)

    woven(each(score, 0, some, tiles))
    for jb in range(n_col):
        woven(each(expand, jb, some, tiles), finish(jb - 1))
        woven(each(attend, jb, some), each(score, jb + 1, some, tiles[: len(tiles) // 2]))
        woven(each(back, jb, tiles), each(score, jb + 1, some, tiles[len(tiles) // 2 :]))
    woven(finish(n_col - 1))

    for r in some:
        for step in range(n_col):
            peer = peer_of(me, step)
            at = pl.multiple_of(peer * blk, blk)
            outs[step][0, r] = dq_s[r, peer]
            outs[step][1, r] = (dkv[r, :c, pl.ds(at, blk)] * (1.0 / LOG2E)).astype(jnp.bfloat16)
            outs[step][2, r] = dkv[r, c:, pl.ds(at, blk)].astype(jnp.bfloat16)
            outs[step][3, r] = at_s[r, peer]

    if last:

        @pl.when(pl.program_id(0) == pl.num_programs(0) - 1)
        def _():
            width = total_out.shape[2]
            for jb in range(n_col):
                for at in range(0, blk, width):
                    share = total[jb, :, at : at + width].astype(jnp.bfloat16)
                    total_out[(jb * blk + at) // width] = share


def params(mib):
    return pltpu.CompilerParams(
        dimension_semantics=("arbitrary",), vmem_limit_bytes=mib * 1024 * 1024
    )


def on_device(n_row, n_col, query, key, value, gate, d_out, bias, length):
    rows, blk, channels = query.shape
    heads, _, n = bias.shape
    c = channels // heads
    groups = n_col // heads
    share = rows // groups
    sizes = [share * weight // sum(SHARES) for weight in SHARES]
    starts = [sum(sizes[:m]) for m in range(len(sizes))]
    assert groups * heads == n_col and n == n_col * blk and groups * sum(sizes) == rows
    scaling = c ** (-0.5)
    per = 2 if all(size % 2 == 0 for size in sizes) else 1
    split_rows = (groups, share, blk, channels)
    query, key, value, gate, d_out = (x.reshape(split_rows) for x in (query, key, value, gate, d_out))
    row, me = lax.axis_index("row"), lax.axis_index("col")
    side = row % 2
    info = jnp.stack([me, length[0], side]).astype(jnp.int32)
    width, half = n // n_row, n // 2

    def exchange(pieces):
        moved = [pieces[0]]
        for step in range(1, n_col):
            pairs = [(a, a ^ step) for a in range(n_col)]
            moved.append(lax.ppermute(pieces[step], "col", pairs))
        return moved

    tables = [
        lax.dynamic_slice(bias, (peer_of(me, step) // groups, 0, side * half), (1, blk, half))[0]
        for step in range(n_col)
    ]
    bias_own = pl.pallas_call(
        functools.partial(bias_kernel, n_col),
        grid_spec=pltpu.PrefetchScalarGridSpec(
            num_scalar_prefetch=1,
            grid=(half // blk,),
            in_specs=[pl.BlockSpec((blk, blk), lambda i, info: (0, i))] * n_col,
            out_specs=pl.BlockSpec((n_col, blk, blk), lambda i, info: (0, i, 0)),
        ),
        out_shape=jax.ShapeDtypeStruct((n_col, half, blk), jnp.bfloat16),
        compiler_params=params(60),
        cost_estimate=pl.CostEstimate(flops=10**7, bytes_accessed=n * n * 4, transcendentals=0),
        name="turn_bias",
    )(info, *exchange(tables))
    bias_other = lax.ppermute(bias_own, "row", [(r, r ^ 1) for r in range(n_row)])

    def piece_shape(m):
        return jax.ShapeDtypeStruct((PIECES, sizes[m], c, blk), jnp.bfloat16)

    def pack(m):
        base = starts[m] // per
        whole = pl.BlockSpec((groups, per, blk, channels), lambda i, info: (0, base + i, 0, 0))
        return pl.pallas_call(
            functools.partial(pack_kernel, heads, groups),
            grid_spec=pltpu.PrefetchScalarGridSpec(
                num_scalar_prefetch=1,
                grid=(sizes[m] // per,),
                in_specs=[whole] * 5,
                out_specs=[pl.BlockSpec((PIECES, per, c, blk), lambda i, info: (0, i, 0, 0))] * n_col,
                scratch_shapes=[pltpu.VMEM((groups, PIECES, channels, blk), jnp.bfloat16)],
            ),
            out_shape=[piece_shape(m)] * n_col,
            compiler_params=params(60),
            cost_estimate=pl.CostEstimate(
                flops=sizes[m] * 10**6, bytes_accessed=sizes[m] * blk * channels * 18, transcendentals=0
            ),
            name="pack",
        )(info, query, key, value, gate, d_out)

    def attend(m, total, pieces, after):
        first, last = m == 0, m == len(sizes) - 1
        together = per
        some = pl.BlockSpec((PIECES, together, c, blk), lambda i, info: (0, i, 0, 0))

        def still(*shape):
            return pl.BlockSpec(shape, lambda i, info: (0,) * len(shape), pipeline_mode=pl.Buffered(1))

        def scratch(*shape, dtype=jnp.bfloat16):
            return pltpu.VMEM((together, *shape), dtype)

        kept = [] if first else [total]
        deep = 4 * c
        square = (n_col, n, blk)
        if last:
            total_shape = jax.ShapeDtypeStruct((n_row, n, width), jnp.bfloat16)
        else:
            total_shape = jax.ShapeDtypeStruct(square, jnp.float32)
        result = pl.pallas_call(
            functools.partial(attention_kernel, n_col, scaling, first, last),
            grid_spec=pltpu.PrefetchScalarGridSpec(
                num_scalar_prefetch=1,
                grid=(sizes[m] // together,),
                in_specs=[still(n_col, half, blk)] * 2
                + [still(*square)] * len(kept)
                + [some] * n_col
                + [pl.BlockSpec(memory_space=pl.ANY)] * len(after),
                out_specs=[some] * n_col + [still(*total_shape.shape)],
                scratch_shapes=[
                    pltpu.VMEM(square, jnp.float32),
                    pltpu.VMEM(square if last else (8, 128), jnp.float32),
                    scratch(n_col, deep, blk),
                    scratch(n_col, c, blk),
                    scratch(deep, n),
                    scratch(deep, n),
                    scratch(n, deep),
                    scratch(n, deep),
                    scratch(n_col, c, blk),
                    scratch(n_col, c, blk),
                    scratch(2 * c, n, dtype=jnp.float32),
                    pltpu.VMEM((2, together, n, blk), jnp.float32),
                    pltpu.VMEM((2, together, n, blk), jnp.bfloat16),
                    pltpu.VMEM((2, together, n, blk), jnp.bfloat16),
                ],
            ),
            out_shape=[piece_shape(m)] * n_col + [total_shape],
            compiler_params=params(60),
            cost_estimate=pl.CostEstimate(
                flops=sizes[m] * 4 * 10**9, bytes_accessed=10**7, transcendentals=sizes[m] * n * n
            ),
            name="attend",
        )(info, bias_own, bias_other, *kept, *pieces, *after)
        return result[:n_col], result[n_col]

    def unpack(m, pieces, grads):
        base = starts[m] // per
        whole = pl.BlockSpec((groups, per, blk, channels), lambda i, info: (0, base + i, 0, 0))
        kept = [] if grads is None else list(grads)
        return pl.pallas_call(
            functools.partial(unpack_kernel, heads, groups),
            grid_spec=pltpu.PrefetchScalarGridSpec(
                num_scalar_prefetch=1,
                grid=(sizes[m] // per,),
                in_specs=[whole] * 2
                + [pl.BlockSpec((PIECES, per, c, blk), lambda i, info: (0, i, 0, 0))] * n_col
                + [pl.BlockSpec(memory_space=pl.ANY)] * len(kept),
                out_specs=[whole] * 4 + [pl.BlockSpec((8, 128), lambda i, info: (0, 0))],
                scratch_shapes=[pltpu.VMEM((groups, PIECES, channels, blk), jnp.bfloat16)],
            ),
            out_shape=[jax.ShapeDtypeStruct(query.shape, jnp.bfloat16)] * 4
            + [jax.ShapeDtypeStruct((8, 128), jnp.float32)],
            input_output_aliases={3 + n_col + a: a for a in range(len(kept))},
            compiler_params=params(60),
            cost_estimate=pl.CostEstimate(
                flops=sizes[m] * 10**6, bytes_accessed=sizes[m] * blk * channels * 18, transcendentals=0
            ),
            name="unpack",
        )(info, gate, d_out, *pieces, *kept)

    arrived = [exchange(pack(m)) for m in range(len(sizes))]
    total, sent, grads, home = None, [], None, []
    for m in range(len(sizes)):
        results, total = attend(m, total, arrived[m], home[m - 2 : m - 1] if m >= 2 else [])
        sent.append(exchange(results))
        if m >= 1:
            *grads, token = unpack(m - 1, sent[m - 1], grads)
            home.append(token)
    *grads, token = unpack(len(sizes) - 1, sent[-1], grads)

    total = lax.psum_scatter(total, "row", scatter_dimension=0, tiled=False)
    total = total.reshape(n_col, blk, width) + token[0, 0].astype(jnp.bfloat16)
    total = lax.all_to_all(total, "col", split_axis=0, concat_axis=0, tiled=True)
    total = jnp.sum(total.reshape(heads, groups, blk, width).astype(jnp.float32), axis=1)
    bias_grad = jnp.transpose(total, (0, 2, 1))
    d_query, d_key, d_value, d_gate = (x.reshape(rows, blk, channels) for x in grads)
    return d_query, d_key, d_value, d_gate, bias_grad


def solution(mesh):
    pair = P("row", "col", None)
    return jax.shard_map(
        functools.partial(on_device, mesh.shape["row"], mesh.shape["col"]),
        mesh=mesh,
        in_specs=(pair, pair, pair, pair, pair, P(None, "col", None), P()),
        out_specs=(pair, pair, pair, pair, P(None, "row", "col")),
        check_vma=False,
    )
```

```python
import functools
import itertools

import jax
import jax.numpy as jnp
from jax import lax
from jax.experimental import pallas as pl
from jax.experimental.pallas import tpu as pltpu
from jax.sharding import PartitionSpec as P

LOG2E = 1.4426950408889634
MASKED = -1e30
SHARES = (1, 3, 4, 4)
PIECES = 4


def dot(a, b, dims):
    return lax.dot_general(a, b, (dims, ((), ())), preferred_element_type=jnp.float32)


def pack_kernel(heads, groups, with_bias, q_ref, k_ref, v_ref, g_ref, o_ref, *refs):
    out = refs[-1]
    count, _, channels = q_ref.shape[1:]
    c = channels // heads
    base = out.shape[1] - count * PIECES * c
    if with_bias:
        for head in range(heads):
            turned = refs[0][head].T
            for g in range(groups):
                out[head * groups + g, :base, :] = turned
    for i in range(count):
        for g in range(groups):
            gated = o_ref[g, i].astype(jnp.float32) * jax.nn.sigmoid(g_ref[g, i].astype(jnp.float32))
            pieces = (q_ref[g, i], k_ref[g, i], v_ref[g, i], gated.astype(jnp.bfloat16))
            for piece, x in enumerate(pieces):
                turned = x.T
                at = base + (i * PIECES + piece) * c
                for head in range(heads):
                    out[head * groups + g, at : at + c, :] = turned[head * c : (head + 1) * c, :]


def unpack_kernel(heads, groups, g_ref, o_ref, ins, *refs):
    dq, dk, dv, dg, token = refs[-5:]
    token[...] = jnp.zeros_like(token)
    count, _, channels = g_ref.shape[1:]
    c = channels // heads
    for i in range(count):
        for g in range(groups):

            def whole(piece):
                at = (i * PIECES + piece) * c
                parts = [ins[head * groups + g, at : at + c, :] for head in range(heads)]
                return jnp.concatenate(parts, axis=0).T

            dq[g, i] = whole(0)
            dk[g, i] = whole(1)
            dv[g, i] = whole(2)
            attended = whole(3).astype(jnp.float32)
            s = jax.nn.sigmoid(g_ref[g, i].astype(jnp.float32))
            dg[g, i] = (o_ref[g, i].astype(jnp.float32) * attended * s * (1.0 - s)).astype(jnp.bfloat16)


def woven(*queues):
    order = [(at / len(q), which, at) for which, q in enumerate(queues) for at in range(len(q))]
    for _, which, at in sorted(order):
        queues[which][at]()


def attention_kernel(n_col, together, c, scaling, first, last, info, bias_ref, *refs):
    if not first:
        total_in, refs = refs[0], refs[1:]
    ins, out, total_out = refs[0], refs[-16], refs[-15]
    bias, total_s, q_s, g_s, k_s, v_s, k_turned, v_turned, dq_s, at_s, dkv, logits, weights, grads = refs[-14:]
    total = total_s if last else total_out
    length = info[0]
    blk = ins.shape[2]
    n = n_col * blk
    tile = min(256, n)
    tiles = range(0, n, tile)
    deep = k_s.shape[1]
    some = range(together)

    @pl.when(pl.program_id(0) == 0)
    def _():
        for jb in range(n_col):
            bias[jb] = bias_ref[jb].astype(jnp.float32) * LOG2E
        if first:
            total[...] = jnp.zeros_like(total)
        else:
            total[...] = total_in[...]
        rows = lax.broadcasted_iota(jnp.int32, (deep - 2 * c, n), 0)
        keys = lax.broadcasted_iota(jnp.int32, (deep - 2 * c, n), 1)
        mask = jnp.logical_and(rows == 0, keys >= length)
        for r in some:
            k_s[r, 2 * c :, :] = jnp.where(mask, MASKED, 0.0).astype(jnp.bfloat16)
            v_s[r, c:, :] = jnp.ones((deep - c, n), jnp.bfloat16)
            q_s[r, :, 2 * c :, :] = jnp.ones((n_col, deep - 2 * c, blk), jnp.bfloat16)

    def rows_of(r, piece):
        at = (r * PIECES + piece) * c
        return slice(at, at + c)

    for r in some:
        for jb in range(n_col):
            span = slice(jb * blk, (jb + 1) * blk)
            q = ins[jb, rows_of(r, 0), :].astype(jnp.float32) * (scaling * LOG2E)
            high = q.astype(jnp.bfloat16)
            q_s[r, jb, :c, :] = high
            q_s[r, jb, c : 2 * c, :] = (q - high.astype(jnp.float32)).astype(jnp.bfloat16)
            k = ins[jb, rows_of(r, 1), :]
            k_s[r, :c, span] = k
            k_s[r, c : 2 * c, span] = k
            v_s[r, :c, span] = ins[jb, rows_of(r, 2), :]
            g_s[r, jb] = ins[jb, rows_of(r, 3), :]
    for r in some:
        k_turned[r] = k_s[r].T
        v_turned[r] = v_s[r].T
    tops, scaled, scales = {}, {}, {}

    def score(jb, r, t):
        part = dot(k_turned[r, t : t + tile, :], q_s[r, jb], ((1,), (0,))) + bias[jb, t : t + tile, :]
        logits[jb % 2, r, t : t + tile, :] = part
        top = jnp.max(part.reshape(tile // 8, 8, blk), axis=0)
        tops[jb, r] = jnp.maximum(tops[jb, r], top) if t else top

    def expand(jb, r, t):
        if t == 0:
            tops[jb, r] = jnp.max(tops[jb, r], axis=0, keepdims=True)
        part = jnp.exp2(logits[jb % 2, r, t : t + tile, :] - tops[jb, r])
        weights[jb % 2, r, t : t + tile, :] = part.astype(jnp.bfloat16)

    def attend(jb, r):
        summed = dot(v_s[r, : c + 16, :], weights[jb % 2, r], ((1,), (0,)))
        inverse = 1.0 / summed[c : c + 1, :]
        attended = summed[:c, :] * inverse
        at_s[r, jb] = attended.astype(jnp.bfloat16)
        g = g_s[r, jb].astype(jnp.float32)
        row_dot = jnp.sum(g * attended, axis=0, keepdims=True) * (-inverse)
        high = row_dot.astype(jnp.bfloat16).astype(jnp.float32)
        rows = lax.broadcasted_iota(jnp.int32, (deep - c, blk), 0)
        tail = jnp.where(rows == 0, high, jnp.where(rows == 1, row_dot - high, 0.0))
        scaled[jb, r] = (g * inverse).astype(jnp.bfloat16)
        scales[jb, r] = jnp.concatenate([scaled[jb, r], tail.astype(jnp.bfloat16)], axis=0)

    def back(jb, t):
        added = total[jb, t : t + tile, :]
        for r in some:
            grad = dot(v_turned[r, t : t + tile, :], scales[jb, r], ((1,), (0,)))
            grad = grad * weights[jb % 2, r, t : t + tile, :].astype(jnp.float32)
            added = added + grad
            grads[jb % 2, r, t : t + tile, :] = grad.astype(jnp.bfloat16)
        total[jb, t : t + tile, :] = added

    def query_grad(jb, r):
        dq_s[r, jb] = (dot(k_s[r, :c, :], grads[jb % 2, r], ((1,), (0,))) * scaling).astype(jnp.bfloat16)

    def add_to(at, r, jb, part):
        if jb:
            part = part + dkv[r, at : at + c, :]
        dkv[r, at : at + c, :] = part

    def key_grad(jb, r):
        add_to(0, r, jb, dot(q_s[r, jb, :c, :], grads[jb % 2, r], ((1,), (1,))))

    def value_grad(jb, r):
        add_to(c, r, jb, dot(scaled[jb, r], weights[jb % 2, r], ((1,), (1,))))

    def each(step, jb, *ranges):
        if not 0 <= jb < n_col:
            return []
        return [functools.partial(step, jb, *at) for at in itertools.product(*ranges)]

    def finish(jb):
        return each(value_grad, jb, some) + each(query_grad, jb, some) + each(key_grad, jb, some)

    woven(each(score, 0, some, tiles))
    for jb in range(n_col):
        woven(each(expand, jb, some, tiles), finish(jb - 1))
        woven(each(attend, jb, some), each(score, jb + 1, some, tiles[: len(tiles) // 2]))
        woven(each(back, jb, tiles), each(score, jb + 1, some, tiles[len(tiles) // 2 :]))
    woven(finish(n_col - 1))

    for r in some:
        for jb in range(n_col):
            span = slice(jb * blk, (jb + 1) * blk)
            out[jb, rows_of(r, 0), :] = dq_s[r, jb]
            out[jb, rows_of(r, 1), :] = (dkv[r, :c, span] * (1.0 / LOG2E)).astype(jnp.bfloat16)
            out[jb, rows_of(r, 2), :] = dkv[r, c:, span].astype(jnp.bfloat16)
            out[jb, rows_of(r, 3), :] = at_s[r, jb]

    if last:

        @pl.when(pl.program_id(0) == pl.num_programs(0) - 1)
        def _():
            width = total_out.shape[2]
            for jb in range(n_col):
                for at in range(0, blk, width):
                    share = total[jb, :, at : at + width].astype(jnp.bfloat16)
                    total_out[(jb * blk + at) // width] = share


def params(mib):
    return pltpu.CompilerParams(
        dimension_semantics=("arbitrary",), vmem_limit_bytes=mib * 1024 * 1024
    )


def on_device(n_row, n_col, query, key, value, gate, d_out, bias, length):
    rows, blk, channels = query.shape
    heads, _, n = bias.shape
    c = channels // heads
    groups = n_col // heads
    share = rows // groups
    sizes = [share * weight // sum(SHARES) for weight in SHARES]
    starts = [sum(sizes[:m]) for m in range(len(sizes))]
    assert groups * heads == n_col and n == n_col * blk and groups * sum(sizes) == rows
    scaling = c ** (-0.5)
    per = 2 if all(size % 2 == 0 for size in sizes) else 1
    split_rows = (groups, share, blk, channels)
    query, key, value, gate, d_out = (x.reshape(split_rows) for x in (query, key, value, gate, d_out))
    info = length.astype(jnp.int32)
    width = n // n_row
    lines = PIECES * c

    def exchange(x):
        return lax.all_to_all(x, "col", split_axis=0, concat_axis=0, tiled=True)

    def cost(m, flops):
        return pl.CostEstimate(
            flops=sizes[m] * flops, bytes_accessed=sizes[m] * blk * channels * 18, transcendentals=0
        )

    def pack(m):
        base, with_bias = starts[m] // per, m == 0
        step = sizes[m] if with_bias else per
        whole = pl.BlockSpec((groups, step, blk, channels), lambda i: (0, base + i, 0, 0))
        size = n * with_bias + sizes[m] * lines
        return pl.pallas_call(
            functools.partial(pack_kernel, heads, groups, with_bias),
            grid=(sizes[m] // step,),
            in_specs=[whole] * 5 + [pl.BlockSpec((heads, blk, n), lambda i: (0, 0, 0))] * with_bias,
            out_specs=pl.BlockSpec((n_col, n * with_bias + step * lines, blk), lambda i: (0, i, 0)),
            out_shape=jax.ShapeDtypeStruct((n_col, size, blk), jnp.bfloat16),
            compiler_params=params(60),
            cost_estimate=cost(m, 10**6),
            name="pack",
        )(query, key, value, gate, d_out, *[bias] * with_bias)

    def attend(m, total, pieces, after):
        first, last = m == 0, m == len(sizes) - 1
        together = per
        skip = n // (together * lines) if first else 0
        some = (n_col, together * lines, blk)

        def still(*shape):
            return pl.BlockSpec(shape, lambda i, info: (0,) * len(shape), pipeline_mode=pl.Buffered(1))

        def scratch(*shape, dtype=jnp.bfloat16):
            return pltpu.VMEM((together, *shape), dtype)

        kept = [] if first else [total]
        deep = 4 * c
        square = (n_col, n, blk)
        if last:
            total_shape = jax.ShapeDtypeStruct((n_row, n, width), jnp.bfloat16)
        else:
            total_shape = jax.ShapeDtypeStruct(square, jnp.float32)
        return pl.pallas_call(
            functools.partial(attention_kernel, n_col, together, c, scaling, first, last),
            grid_spec=pltpu.PrefetchScalarGridSpec(
                num_scalar_prefetch=1,
                grid=(sizes[m] // together,),
                in_specs=[still(*square)] * (1 + len(kept))
                + [pl.BlockSpec(some, lambda i, info: (0, skip + i, 0))]
                + [pl.BlockSpec(memory_space=pl.ANY)] * len(after),
                out_specs=[pl.BlockSpec(some, lambda i, info: (0, i, 0)), still(*total_shape.shape)],
                scratch_shapes=[
                    pltpu.VMEM(square, jnp.float32),
                    pltpu.VMEM(square if last else (8, 128), jnp.float32),
                    scratch(n_col, deep, blk),
                    scratch(n_col, c, blk),
                    scratch(deep, n),
                    scratch(deep, n),
                    scratch(n, deep),
                    scratch(n, deep),
                    scratch(n_col, c, blk),
                    scratch(n_col, c, blk),
                    scratch(2 * c, n, dtype=jnp.float32),
                    pltpu.VMEM((2, together, n, blk), jnp.float32),
                    pltpu.VMEM((2, together, n, blk), jnp.bfloat16),
                    pltpu.VMEM((2, together, n, blk), jnp.bfloat16),
                ],
            ),
            out_shape=[
                jax.ShapeDtypeStruct((n_col, sizes[m] * lines, blk), jnp.bfloat16),
                total_shape,
            ],
            compiler_params=params(60),
            cost_estimate=cost(m, 4 * 10**9),
            name="attend",
        )(info, arrived[0], *kept, pieces, *after)

    def unpack(m, pieces, grads):
        base = starts[m] // per
        whole = pl.BlockSpec((groups, per, blk, channels), lambda i: (0, base + i, 0, 0))
        kept = [] if grads is None else list(grads)
        return pl.pallas_call(
            functools.partial(unpack_kernel, heads, groups),
            grid=(sizes[m] // per,),
            in_specs=[whole] * 2
            + [pl.BlockSpec((n_col, per * lines, blk), lambda i: (0, i, 0))]
            + [pl.BlockSpec(memory_space=pl.ANY)] * len(kept),
            out_specs=[whole] * 4 + [pl.BlockSpec((8, 128), lambda i: (0, 0))],
            out_shape=[jax.ShapeDtypeStruct(query.shape, jnp.bfloat16)] * 4
            + [jax.ShapeDtypeStruct((8, 128), jnp.float32)],
            input_output_aliases={3 + a: a for a in range(len(kept))},
            compiler_params=params(60),
            cost_estimate=cost(m, 10**6),
            name="unpack",
        )(gate, d_out, pieces, *kept)

    arrived = [exchange(pack(m)) for m in range(len(sizes))]
    total, sent, grads, home = None, [], None, []
    for m in range(len(sizes)):
        results, total = attend(m, total, arrived[m], home[m - 2 : m - 1] if m >= 2 else [])
        sent.append(exchange(results))
        if m >= 1:
            *grads, token = unpack(m - 1, sent[m - 1], grads)
            home.append(token)
    *grads, token = unpack(len(sizes) - 1, sent[-1], grads)

    total = lax.psum_scatter(total, "row", scatter_dimension=0, tiled=False)
    total = exchange(total.reshape(n_col, blk, width) + token[0, 0].astype(jnp.bfloat16))
    total = jnp.sum(total.reshape(heads, groups, blk, width).astype(jnp.float32), axis=1)
    bias_grad = jnp.transpose(total, (0, 2, 1))
    d_query, d_key, d_value, d_gate = (x.reshape(rows, blk, channels) for x in grads)
    return d_query, d_key, d_value, d_gate, bias_grad


def solution(mesh):
    pair = P("row", "col", None)
    return jax.shard_map(
        functools.partial(on_device, mesh.shape["row"], mesh.shape["col"]),
        mesh=mesh,
        in_specs=(pair, pair, pair, pair, pair, P(None, "col", None), P()),
        out_specs=(pair, pair, pair, pair, P(None, "row", "col")),
        check_vma=False,
    )
```

```python
import functools
import itertools

import jax
import jax.numpy as jnp
from jax import lax
from jax.experimental import pallas as pl
from jax.experimental.pallas import tpu as pltpu
from jax.sharding import PartitionSpec as P

LOG2E = 1.4426950408889634
MASKED = -1e30
SHARES = (1, 3, 3, 3, 2)
PIECES = 4


def dot(a, b, dims):
    return lax.dot_general(a, b, (dims, ((), ())), preferred_element_type=jnp.float32)


def peer_of(me, step):
    return jnp.bitwise_xor(me, step)


def pack_kernel(heads, groups, with_bias, info, q_ref, k_ref, v_ref, g_ref, o_ref, *refs):
    n_col = heads * groups
    outs, turned = refs[-1 - n_col : -1], refs[-1]
    me = info[1]
    count, _, channels = q_ref.shape[1:]
    c = channels // heads
    base = outs[0].shape[0] - count * PIECES * c
    for i in range(count):
        for g in range(groups):
            gated = o_ref[g, i].astype(jnp.float32) * jax.nn.sigmoid(g_ref[g, i].astype(jnp.float32))
            pieces = (q_ref[g, i], k_ref[g, i], v_ref[g, i], gated.astype(jnp.bfloat16))
            for piece, x in enumerate(pieces):
                turned[g, i, piece] = x.T
        for step in range(n_col):
            peer = peer_of(me, step)
            head = pl.multiple_of(peer // groups * c, c)
            for piece in range(PIECES):
                at = base + (i * PIECES + piece) * c
                outs[step][at : at + c, :] = turned[peer % groups, i, piece, pl.ds(head, c), :]
    if with_bias:
        for step in range(n_col):
            outs[step][:base, :] = refs[0][peer_of(me, step) // groups].T


def unpack_kernel(heads, groups, info, g_ref, o_ref, *refs):
    n_col = heads * groups
    ins, (dq, dk, dv, dg, token, whole) = refs[:n_col], refs[-6:]
    token[...] = jnp.zeros_like(token)
    me = info[1]
    count, _, channels = g_ref.shape[1:]
    c = channels // heads
    for i in range(count):
        for step in range(n_col):
            peer = peer_of(me, step)
            head = pl.multiple_of(peer // groups * c, c)
            for piece in range(PIECES):
                at = (i * PIECES + piece) * c
                whole[peer % groups, i, piece, pl.ds(head, c), :] = ins[step][at : at + c, :]
        for g in range(groups):
            dq[g, i] = whole[g, i, 0].T
            dk[g, i] = whole[g, i, 1].T
            dv[g, i] = whole[g, i, 2].T
            attended = whole[g, i, 3].T.astype(jnp.float32)
            s = jax.nn.sigmoid(g_ref[g, i].astype(jnp.float32))
            dg[g, i] = (o_ref[g, i].astype(jnp.float32) * attended * s * (1.0 - s)).astype(jnp.bfloat16)


def woven(*queues):
    order = [(at / len(q), which, at) for which, q in enumerate(queues) for at in range(len(q))]
    for _, which, at in sorted(order):
        queues[which][at]()


def attention_kernel(n_col, together, c, scaling, first, last, info, *refs):
    bias_in, ins, refs = refs[:n_col], refs[n_col : 2 * n_col], refs[2 * n_col :]
    scratch, refs = refs[-14:], refs[:-14]
    bias, total_s, q_s, g_s, k_s, v_s, k_turned, v_turned, dq_s, at_s, dkv, logits, weights, grads = scratch
    if not first:
        total_in = refs[0]
    totals = refs[-2:] if last else refs[-1:]
    outs, total_out = refs[-n_col - len(totals) : -len(totals)], totals[0]
    total = total_s if last else total_out
    length, me, side = info[0], info[1], info[2]
    blk = ins[0].shape[1]
    n = n_col * blk
    tile = min(256, n)
    tiles = range(0, n, tile)
    deep = k_s.shape[1]
    some = range(together)

    @pl.when(pl.program_id(0) == 0)
    def _():
        for step in range(n_col):
            bias[peer_of(me, step)] = bias_in[step][...].astype(jnp.float32) * LOG2E
        if first:
            total[...] = jnp.zeros_like(total)
        else:
            total[...] = total_in[...]
        rows = lax.broadcasted_iota(jnp.int32, (deep - 2 * c, n), 0)
        keys = lax.broadcasted_iota(jnp.int32, (deep - 2 * c, n), 1)
        mask = jnp.logical_and(rows == 0, keys >= length)
        for r in some:
            k_s[r, 2 * c :, :] = jnp.where(mask, MASKED, 0.0).astype(jnp.bfloat16)
            v_s[r, c:, :] = jnp.ones((deep - c, n), jnp.bfloat16)
            q_s[r, :, 2 * c :, :] = jnp.ones((n_col, deep - 2 * c, blk), jnp.bfloat16)

    def rows_of(r, piece):
        at = (r * PIECES + piece) * c
        return slice(at, at + c)

    for r in some:
        for step in range(n_col):
            jb = peer_of(me, step)
            span = pl.ds(pl.multiple_of(jb * blk, blk), blk)
            q = ins[step][rows_of(r, 0), :].astype(jnp.float32) * (scaling * LOG2E)
            high = q.astype(jnp.bfloat16)
            q_s[r, jb, :c, :] = high
            q_s[r, jb, c : 2 * c, :] = (q - high.astype(jnp.float32)).astype(jnp.bfloat16)
            k = ins[step][rows_of(r, 1), :]
            k_s[r, :c, span] = k
            k_s[r, c : 2 * c, span] = k
            v_s[r, :c, span] = ins[step][rows_of(r, 2), :]
            g_s[r, jb] = ins[step][rows_of(r, 3), :]
    for r in some:
        k_turned[r] = k_s[r].T
        v_turned[r] = v_s[r].T
    tops, scaled, scales = {}, {}, {}

    def score(jb, r, t):
        part = dot(k_turned[r, t : t + tile, :], q_s[r, jb], ((1,), (0,))) + bias[jb, t : t + tile, :]
        logits[jb % 2, r, t : t + tile, :] = part
        top = jnp.max(part.reshape(tile // 8, 8, blk), axis=0)
        tops[jb, r] = jnp.maximum(tops[jb, r], top) if t else top

    def expand(jb, r, t):
        if t == 0:
            tops[jb, r] = jnp.max(tops[jb, r], axis=0, keepdims=True)
        part = jnp.exp2(logits[jb % 2, r, t : t + tile, :] - tops[jb, r])
        weights[jb % 2, r, t : t + tile, :] = part.astype(jnp.bfloat16)

    def attend(jb, r):
        summed = dot(v_s[r, : c + 16, :], weights[jb % 2, r], ((1,), (0,)))
        inverse = 1.0 / summed[c : c + 1, :]
        attended = summed[:c, :] * inverse
        at_s[r, jb] = attended.astype(jnp.bfloat16)
        g = g_s[r, jb].astype(jnp.float32)
        row_dot = jnp.sum(g * attended, axis=0, keepdims=True) * (-inverse)
        high = row_dot.astype(jnp.bfloat16).astype(jnp.float32)
        rows = lax.broadcasted_iota(jnp.int32, (deep - c, blk), 0)
        tail = jnp.where(rows == 0, high, jnp.where(rows == 1, row_dot - high, 0.0))
        scaled[jb, r] = (g * inverse).astype(jnp.bfloat16)
        scales[jb, r] = jnp.concatenate([scaled[jb, r], tail.astype(jnp.bfloat16)], axis=0)

    def back(jb, t):
        added = total[jb, t : t + tile, :]
        for r in some:
            grad = dot(v_turned[r, t : t + tile, :], scales[jb, r], ((1,), (0,)))
            grad = grad * weights[jb % 2, r, t : t + tile, :].astype(jnp.float32)
            added = added + grad
            grads[jb % 2, r, t : t + tile, :] = grad.astype(jnp.bfloat16)
        total[jb, t : t + tile, :] = added

    def query_grad(jb, r):
        dq_s[r, jb] = (dot(k_s[r, :c, :], grads[jb % 2, r], ((1,), (0,))) * scaling).astype(jnp.bfloat16)

    def add_to(at, r, jb, part):
        if jb:
            part = part + dkv[r, at : at + c, :]
        dkv[r, at : at + c, :] = part

    def key_grad(jb, r):
        add_to(0, r, jb, dot(q_s[r, jb, :c, :], grads[jb % 2, r], ((1,), (1,))))

    def value_grad(jb, r):
        add_to(c, r, jb, dot(scaled[jb, r], weights[jb % 2, r], ((1,), (1,))))

    def each(step, jb, *ranges):
        if not 0 <= jb < n_col:
            return []
        return [functools.partial(step, jb, *at) for at in itertools.product(*ranges)]

    def finish(jb):
        return each(value_grad, jb, some) + each(query_grad, jb, some) + each(key_grad, jb, some)

    woven(each(score, 0, some, tiles))
    for jb in range(n_col):
        woven(each(expand, jb, some, tiles), finish(jb - 1))
        woven(each(attend, jb, some), each(score, jb + 1, some, tiles[: len(tiles) // 2]))
        woven(each(back, jb, tiles), each(score, jb + 1, some, tiles[len(tiles) // 2 :]))
    woven(finish(n_col - 1))

    for r in some:
        for step in range(n_col):
            jb = peer_of(me, step)
            span = pl.ds(pl.multiple_of(jb * blk, blk), blk)
            outs[step][rows_of(r, 0), :] = dq_s[r, jb]
            outs[step][rows_of(r, 1), :] = (dkv[r, :c, span] * (1.0 / LOG2E)).astype(jnp.bfloat16)
            outs[step][rows_of(r, 2), :] = dkv[r, c:, span].astype(jnp.bfloat16)
            outs[step][rows_of(r, 3), :] = at_s[r, jb]

    if last:

        @pl.when(pl.program_id(0) == pl.num_programs(0) - 1)
        def _():
            mine, others = totals
            pairs, _, width = mine.shape
            for pair in range(pairs):
                at = 2 * pair * width
                both = total[at // blk, :, at % blk : at % blk + 2 * width].astype(jnp.bfloat16)
                even, odd = both[:, :width], both[:, width:]
                mine[pair] = jnp.where(side == 0, even, odd)
                others[pair] = jnp.where(side == 0, odd, even)


def params(mib):
    return pltpu.CompilerParams(
        dimension_semantics=("arbitrary",), vmem_limit_bytes=mib * 1024 * 1024
    )


def on_device(n_row, n_col, query, key, value, gate, d_out, bias, length):
    rows, blk, channels = query.shape
    heads, _, n = bias.shape
    c = channels // heads
    groups = n_col // heads
    share = rows // groups
    sizes = [share * weight // sum(SHARES) for weight in SHARES]
    starts = [sum(sizes[:m]) for m in range(len(sizes))]
    assert groups * heads == n_col and n == n_col * blk and groups * sum(sizes) == rows
    scaling = c ** (-0.5)
    per = 2 if all(size % 2 == 0 for size in sizes) else 1
    split_rows = (groups, share, blk, channels)
    query, key, value, gate, d_out = (x.reshape(split_rows) for x in (query, key, value, gate, d_out))
    row = lax.axis_index("row")
    info = jnp.stack([length[0], lax.axis_index("col"), row % 2]).astype(jnp.int32)
    width = n // n_row
    lines = PIECES * c
    chunks = len(sizes)
    turned_shape = (groups, per, PIECES, channels, blk)

    def exchange(blocks):
        pairs = [[(a, a ^ step) for a in range(n_col)] for step in range(n_col)]
        return [blocks[0]] + [lax.ppermute(blocks[step], "col", pairs[step]) for step in range(1, n_col)]

    def call(kernel, name, m, flops, grid, operands, out_specs, out_shape, scratch, aliases):
        return pl.pallas_call(
            kernel,
            grid_spec=pltpu.PrefetchScalarGridSpec(
                num_scalar_prefetch=1,
                grid=(grid,),
                in_specs=[spec for spec, _ in operands],
                out_specs=out_specs,
                scratch_shapes=scratch,
            ),
            out_shape=out_shape,
            input_output_aliases=aliases,
            compiler_params=params(60),
            cost_estimate=pl.CostEstimate(
                flops=sizes[m] * flops, bytes_accessed=sizes[m] * blk * channels * 18, transcendentals=0
            ),
            name=name,
        )(info, *[x for _, x in operands])

    def still(*shape):
        return pl.BlockSpec(shape, lambda i, info: (0,) * len(shape), pipeline_mode=pl.Buffered(1))

    def part(size, skip):
        return pl.BlockSpec((size, blk), lambda i, info: (skip + i, 0))

    untouched = pl.BlockSpec(memory_space=pl.ANY)

    def pack(m):
        with_bias = m == 0
        step = sizes[m] if with_bias else per
        base = starts[m] // step
        whole = pl.BlockSpec((groups, step, blk, channels), lambda i, info: (0, base + i, 0, 0))
        ahead = n if with_bias else 0
        size = ahead + (sizes[m] + (sizes[m - 2] if m >= 2 else 0)) * lines
        operands = [(whole, x) for x in (query, key, value, gate, d_out)]
        if with_bias:
            operands.append((still(heads, blk, n), bias))
        return call(
            functools.partial(pack_kernel, heads, groups, with_bias),
            "pack",
            m,
            10**6,
            sizes[m] // step,
            operands,
            [part(ahead + step * lines, 0)] * n_col,
            [jax.ShapeDtypeStruct((size, blk), jnp.bfloat16)] * n_col,
            [pltpu.VMEM((groups, step, PIECES, channels, blk), jnp.bfloat16)],
            {},
        )

    def attend(m, total, bias_blocks, blocks, room):
        first, last = m == 0, m == chunks - 1

        def scratch(*shape, dtype=jnp.bfloat16):
            return pltpu.VMEM((per, *shape), dtype)

        skip = n // (per * lines) if first else 0
        operands = [(still(n, blk), x) for x in bias_blocks]
        operands += [(part(per * lines, skip), x) for x in blocks]
        square = (n_col, n, blk)
        if not first:
            operands.append((still(*square), total))
        aliases, ahead = {}, 0
        if room is not None:
            aliases = {1 + len(operands) + a: a for a in range(n_col)}
            operands += [(untouched, x) for x in room]
            ahead = sizes[m + 2] // per
            out_shape = [jax.ShapeDtypeStruct(x.shape, x.dtype) for x in room]
        else:
            out_shape = [jax.ShapeDtypeStruct((sizes[m] * lines, blk), jnp.bfloat16)] * n_col
        if last:
            totals = [jax.ShapeDtypeStruct((n_row // 2, n, width), jnp.bfloat16)] * 2
        else:
            totals = [jax.ShapeDtypeStruct(square, jnp.float32)]
        deep = 4 * c
        result = call(
            functools.partial(attention_kernel, n_col, per, c, scaling, first, last),
            "attend",
            m,
            4 * 10**9,
            sizes[m] // per,
            operands,
            [part(per * lines, ahead)] * n_col + [still(*x.shape) for x in totals],
            out_shape + totals,
            [
                pltpu.VMEM(square, jnp.float32),
                pltpu.VMEM(square if last else (8, 128), jnp.float32),
                scratch(n_col, deep, blk),
                scratch(n_col, c, blk),
                scratch(deep, n),
                scratch(deep, n),
                scratch(n, deep),
                scratch(n, deep),
                scratch(n_col, c, blk),
                scratch(n_col, c, blk),
                scratch(2 * c, n, dtype=jnp.float32),
                pltpu.VMEM((2, per, n, blk), jnp.float32),
                pltpu.VMEM((2, per, n, blk), jnp.bfloat16),
                pltpu.VMEM((2, per, n, blk), jnp.bfloat16),
            ],
            aliases,
        )
        return result[:n_col], result[n_col:]

    def unpack(m, blocks, grads):
        base = starts[m] // per
        ahead = sizes[m + 2] // per if m + 2 < chunks else 0
        whole = pl.BlockSpec((groups, per, blk, channels), lambda i, info: (0, base + i, 0, 0))
        kept = [] if grads is None else list(grads)
        operands = [(whole, gate), (whole, d_out)]
        operands += [(part(per * lines, ahead), x) for x in blocks]
        aliases = {1 + len(operands) + a: a for a in range(len(kept))}
        operands += [(untouched, x) for x in kept]
        return call(
            functools.partial(unpack_kernel, heads, groups),
            "unpack",
            m,
            10**6,
            sizes[m] // per,
            operands,
            [whole] * 4 + [pl.BlockSpec((8, 128), lambda i, info: (0, 0))],
            [jax.ShapeDtypeStruct(query.shape, jnp.bfloat16)] * 4
            + [jax.ShapeDtypeStruct((8, 128), jnp.float32)],
            [pltpu.VMEM(turned_shape, jnp.bfloat16)],
            aliases,
        )

    packed = [pack(m) for m in range(chunks)]
    arrived = [exchange(packed[m]) for m in range(2)]
    totals, grads = [None], None
    for m in range(chunks):
        room = packed[m + 2] if m + 2 < chunks else None
        results, totals = attend(m, totals[0], arrived[0], arrived[m], room)
        arrived.append(exchange(results))
    for m in range(chunks):
        *grads, token = unpack(m, arrived[m + 2], grads)

    mine, others = totals
    others = lax.ppermute(others, "row", [(r, r ^ 1) for r in range(n_row)])
    total = (mine.astype(jnp.float32) + others.astype(jnp.float32)).astype(jnp.bfloat16)
    alternate = [[r for r in range(n_row) if r % 2 == s] for s in range(2)]
    total = lax.psum_scatter(
        total, "row", scatter_dimension=0, tiled=False, axis_index_groups=alternate
    )
    total = total.reshape(n_col, blk, width) + token[0, 0].astype(jnp.bfloat16)
    total = lax.all_to_all(total, "col", split_axis=0, concat_axis=0, tiled=True)
    total = jnp.sum(total.reshape(heads, groups, blk, width).astype(jnp.float32), axis=1)
    bias_grad = jnp.transpose(total, (0, 2, 1))
    d_query, d_key, d_value, d_gate = (x.reshape(rows, blk, channels) for x in grads)
    return d_query, d_key, d_value, d_gate, bias_grad


def solution(mesh):
    pair = P("row", "col", None)
    return jax.shard_map(
        functools.partial(on_device, mesh.shape["row"], mesh.shape["col"]),
        mesh=mesh,
        in_specs=(pair, pair, pair, pair, pair, P(None, "col", None), P()),
        out_specs=(pair, pair, pair, pair, P(None, "row", "col")),
        check_vma=False,
    )
```

```python
import functools
import itertools

import jax
import jax.numpy as jnp
from jax import lax
from jax.experimental import pallas as pl
from jax.experimental.pallas import tpu as pltpu
from jax.sharding import PartitionSpec as P

LOG2E = 1.4426950408889634
MASKED = -1e30
SHARES = (1, 3, 4, 4)
PIECES = 4


def dot(a, b, dims):
    return lax.dot_general(a, b, (dims, ((), ())), preferred_element_type=jnp.float32)


def peer_of(me, step):
    return jnp.bitwise_xor(me, step)


def pack_kernel(heads, groups, with_bias, info, q_ref, k_ref, v_ref, g_ref, o_ref, *refs):
    n_col = heads * groups
    outs, turned = refs[-1 - n_col : -1], refs[-1]
    me = info[1]
    count, _, channels = q_ref.shape[1:]
    c = channels // heads
    lines = count * PIECES * c
    for i in range(count):
        for g in range(groups):
            gated = o_ref[g, i].astype(jnp.float32) * jax.nn.sigmoid(g_ref[g, i].astype(jnp.float32))
            pieces = (q_ref[g, i], k_ref[g, i], v_ref[g, i], gated.astype(jnp.bfloat16))
            for piece, x in enumerate(pieces):
                turned[g, i, piece] = x.T
        for step in range(n_col):
            peer = peer_of(me, step)
            head = pl.multiple_of(peer // groups * c, c)
            base = outs[step].shape[0] - lines
            for piece in range(PIECES):
                at = base + (i * PIECES + piece) * c
                outs[step][at : at + c, :] = turned[peer % groups, i, piece, pl.ds(head, c), :]
    if with_bias:
        for step in range(n_col):
            base = outs[step].shape[0] - lines
            keys = pl.ds(pl.multiple_of(info[2] * base, base), base) if step else slice(None)
            outs[step][:base, :] = refs[0][peer_of(me, step) // groups, :, keys].T


def unpack_kernel(heads, groups, info, g_ref, o_ref, *refs):
    n_col = heads * groups
    ins, (dq, dk, dv, dg, token, whole) = refs[:n_col], refs[-6:]
    token[...] = jnp.zeros_like(token)
    me = info[1]
    count, _, channels = g_ref.shape[1:]
    c = channels // heads
    for i in range(count):
        for step in range(n_col):
            peer = peer_of(me, step)
            head = pl.multiple_of(peer // groups * c, c)
            for piece in range(PIECES):
                at = (i * PIECES + piece) * c
                whole[peer % groups, i, piece, pl.ds(head, c), :] = ins[step][at : at + c, :]
        for g in range(groups):
            dq[g, i] = whole[g, i, 0].T
            dk[g, i] = whole[g, i, 1].T
            dv[g, i] = whole[g, i, 2].T
            attended = whole[g, i, 3].T.astype(jnp.float32)
            s = jax.nn.sigmoid(g_ref[g, i].astype(jnp.float32))
            dg[g, i] = (o_ref[g, i].astype(jnp.float32) * attended * s * (1.0 - s)).astype(jnp.bfloat16)


def woven(*queues):
    order = [(at / len(q), which, at) for which, q in enumerate(queues) for at in range(len(q))]
    for _, which, at in sorted(order):
        queues[which][at]()


def attention_kernel(n_col, together, c, scaling, first, last, info, *refs):
    bias_in, ins, refs = refs[: 2 * n_col - 1], refs[2 * n_col - 1 : 3 * n_col - 1], refs[3 * n_col - 1 :]
    scratch, refs = refs[-14:], refs[:-14]
    bias, total_s, q_s, g_s, k_s, v_s, k_turned, v_turned, dq_s, at_s, dkv, logits, weights, grads = scratch
    if not first:
        total_in = refs[0]
    totals = refs[-2:] if last else refs[-1:]
    outs, total_out = refs[-n_col - len(totals) : -len(totals)], totals[0]
    total = total_s if last else total_out
    length, me, side, level = info[0], info[1], info[2], info[3]
    blk = ins[0].shape[1]
    n = n_col * blk
    tile = min(256, n)
    tiles = range(0, n, tile)
    deep = k_s.shape[1]
    some = range(together)

    @pl.when(pl.program_id(0) == 0)
    def _():
        half = n // 2
        bias[me] = bias_in[0][...].astype(jnp.float32) * LOG2E
        for step in range(1, n_col):
            for table, which in ((bias_in[step], side), (bias_in[n_col + step - 1], 1 - side)):
                keys = pl.ds(pl.multiple_of(which * half, half), half)
                bias[peer_of(me, step), keys, :] = table[...].astype(jnp.float32) * LOG2E
        if first:
            total[...] = jnp.zeros_like(total)
        else:
            total[...] = total_in[...]
        rows = lax.broadcasted_iota(jnp.int32, (deep - 2 * c, n), 0)
        keys = lax.broadcasted_iota(jnp.int32, (deep - 2 * c, n), 1)
        mask = jnp.logical_and(rows == 0, keys >= length)
        for r in some:
            k_s[r, 2 * c :, :] = jnp.where(mask, MASKED, 0.0).astype(jnp.bfloat16)
            v_s[r, c:, :] = jnp.ones((deep - c, n), jnp.bfloat16)
            q_s[r, :, 2 * c :, :] = jnp.ones((n_col, deep - 2 * c, blk), jnp.bfloat16)

    def rows_of(r, piece):
        at = (r * PIECES + piece) * c
        return slice(at, at + c)

    for r in some:
        for step in range(n_col):
            jb = peer_of(me, step)
            span = pl.ds(pl.multiple_of(jb * blk, blk), blk)
            q = ins[step][rows_of(r, 0), :].astype(jnp.float32) * (scaling * LOG2E)
            high = q.astype(jnp.bfloat16)
            q_s[r, jb, :c, :] = high
            q_s[r, jb, c : 2 * c, :] = (q - high.astype(jnp.float32)).astype(jnp.bfloat16)
            k = ins[step][rows_of(r, 1), :]
            k_s[r, :c, span] = k
            k_s[r, c : 2 * c, span] = k
            v_s[r, :c, span] = ins[step][rows_of(r, 2), :]
            g_s[r, jb] = ins[step][rows_of(r, 3), :]
    for r in some:
        k_turned[r] = k_s[r].T
        v_turned[r] = v_s[r].T
    tops, scaled, scales = {}, {}, {}

    def score(jb, r, t):
        part = dot(k_turned[r, t : t + tile, :], q_s[r, jb], ((1,), (0,))) + bias[jb, t : t + tile, :]
        logits[jb % 2, r, t : t + tile, :] = part
        top = jnp.max(part.reshape(tile // 8, 8, blk), axis=0)
        tops[jb, r] = jnp.maximum(tops[jb, r], top) if t else top

    def expand(jb, r, t):
        if t == 0:
            tops[jb, r] = jnp.max(tops[jb, r], axis=0, keepdims=True)
        part = jnp.exp2(logits[jb % 2, r, t : t + tile, :] - tops[jb, r])
        weights[jb % 2, r, t : t + tile, :] = part.astype(jnp.bfloat16)

    def attend(jb, r):
        summed = dot(v_s[r, : c + 16, :], weights[jb % 2, r], ((1,), (0,)))
        inverse = 1.0 / summed[c : c + 1, :]
        attended = summed[:c, :] * inverse
        at_s[r, jb] = attended.astype(jnp.bfloat16)
        g = g_s[r, jb].astype(jnp.float32)
        row_dot = jnp.sum(g * attended, axis=0, keepdims=True) * (-inverse)
        high = row_dot.astype(jnp.bfloat16).astype(jnp.float32)
        rows = lax.broadcasted_iota(jnp.int32, (deep - c, blk), 0)
        tail = jnp.where(rows == 0, high, jnp.where(rows == 1, row_dot - high, 0.0))
        scaled[jb, r] = (g * inverse).astype(jnp.bfloat16)
        scales[jb, r] = jnp.concatenate([scaled[jb, r], tail.astype(jnp.bfloat16)], axis=0)

    def back(jb, t):
        added = total[jb, t : t + tile, :]
        for r in some:
            grad = dot(v_turned[r, t : t + tile, :], scales[jb, r], ((1,), (0,)))
            grad = grad * weights[jb % 2, r, t : t + tile, :].astype(jnp.float32)
            added = added + grad
            grads[jb % 2, r, t : t + tile, :] = grad.astype(jnp.bfloat16)
        total[jb, t : t + tile, :] = added

    def query_grad(jb, r):
        dq_s[r, jb] = (dot(k_s[r, :c, :], grads[jb % 2, r], ((1,), (0,))) * scaling).astype(jnp.bfloat16)

    def add_to(at, r, jb, part):
        if jb:
            part = part + dkv[r, at : at + c, :]
        dkv[r, at : at + c, :] = part

    def key_grad(jb, r):
        add_to(0, r, jb, dot(q_s[r, jb, :c, :], grads[jb % 2, r], ((1,), (1,))))

    def value_grad(jb, r):
        add_to(c, r, jb, dot(scaled[jb, r], weights[jb % 2, r], ((1,), (1,))))

    def each(step, jb, *ranges):
        if not 0 <= jb < n_col:
            return []
        return [functools.partial(step, jb, *at) for at in itertools.product(*ranges)]

    def finish(jb):
        return each(value_grad, jb, some) + each(query_grad, jb, some) + each(key_grad, jb, some)

    woven(each(score, 0, some, tiles))
    for jb in range(n_col):
        woven(each(expand, jb, some, tiles), finish(jb - 1))
        woven(each(attend, jb, some), each(score, jb + 1, some, tiles[: len(tiles) // 2]))
        woven(each(back, jb, tiles), each(score, jb + 1, some, tiles[len(tiles) // 2 :]))
    woven(finish(n_col - 1))

    for r in some:
        for step in range(n_col):
            jb = peer_of(me, step)
            span = pl.ds(pl.multiple_of(jb * blk, blk), blk)
            outs[step][rows_of(r, 0), :] = dq_s[r, jb]
            outs[step][rows_of(r, 1), :] = (dkv[r, :c, span] * (1.0 / LOG2E)).astype(jnp.bfloat16)
            outs[step][rows_of(r, 2), :] = dkv[r, c:, span].astype(jnp.bfloat16)
            outs[step][rows_of(r, 3), :] = at_s[r, jb]

    if last:

        @pl.when(pl.program_id(0) == pl.num_programs(0) - 1)
        def _():
            mine, others = totals
            pairs, _, width = mine.shape
            for pair in range(pairs):
                at = 2 * pair * width
                both = total[at // blk, :, at % blk : at % blk + 2 * width].astype(jnp.bfloat16)
                even, odd = both[:, :width], both[:, width:]
                mine[peer_of(level, pair)] = jnp.where(side == 0, even, odd)
                others[peer_of(level, pair)] = jnp.where(side == 0, odd, even)


def hold_kernel(*refs):
    pass


def params(mib):
    return pltpu.CompilerParams(
        dimension_semantics=("arbitrary",), vmem_limit_bytes=mib * 1024 * 1024
    )


def on_device(n_row, n_col, query, key, value, gate, d_out, bias, length):
    rows, blk, channels = query.shape
    heads, _, n = bias.shape
    c = channels // heads
    groups = n_col // heads
    share = rows // groups
    sizes = [share * weight // sum(SHARES) for weight in SHARES]
    starts = [sum(sizes[:m]) for m in range(len(sizes))]
    assert groups * heads == n_col and n == n_col * blk and groups * sum(sizes) == rows
    scaling = c ** (-0.5)
    per = 2 if all(size % 2 == 0 for size in sizes) else 1
    split_rows = (groups, share, blk, channels)
    query, key, value, gate, d_out = (x.reshape(split_rows) for x in (query, key, value, gate, d_out))
    row = lax.axis_index("row")
    info = jnp.stack([length[0], lax.axis_index("col"), row % 2, row // 2]).astype(jnp.int32)
    width = n // n_row
    lines = PIECES * c
    chunks = len(sizes)
    turned_shape = (groups, per, PIECES, channels, blk)

    untouched = pl.BlockSpec(memory_space=pl.ANY)

    def exchange(blocks):
        pairs = [[(a, a ^ step) for a in range(n_col)] for step in range(n_col)]
        return [blocks[0]] + [lax.ppermute(blocks[step], "col", pairs[step]) for step in range(1, n_col)]

    def swap(x):
        return lax.ppermute(x, "row", [(r, r ^ 1) for r in range(n_row)])

    def hold(blocks, until):
        count = len(blocks)
        return pl.pallas_call(
            hold_kernel,
            in_specs=[untouched] * (count + len(until)),
            out_specs=[untouched] * count,
            out_shape=[jax.ShapeDtypeStruct(x.shape, x.dtype) for x in blocks],
            input_output_aliases={a: a for a in range(count)},
            name="hold",
        )(*blocks, *until)

    def call(kernel, name, m, flops, grid, operands, out_specs, out_shape, scratch, aliases):
        return pl.pallas_call(
            kernel,
            grid_spec=pltpu.PrefetchScalarGridSpec(
                num_scalar_prefetch=1,
                grid=(grid,),
                in_specs=[spec for spec, _ in operands],
                out_specs=out_specs,
                scratch_shapes=scratch,
            ),
            out_shape=out_shape,
            input_output_aliases=aliases,
            compiler_params=params(60),
            cost_estimate=pl.CostEstimate(
                flops=sizes[m] * flops, bytes_accessed=sizes[m] * blk * channels * 18, transcendentals=0
            ),
            name=name,
        )(info, *[x for _, x in operands])

    def still(*shape):
        return pl.BlockSpec(shape, lambda i, info: (0,) * len(shape), pipeline_mode=pl.Buffered(1))

    def part(size, skip):
        return pl.BlockSpec((size, blk), lambda i, info: (skip + i, 0))

    def pack(m):
        with_bias = m == 0
        step = sizes[m] if with_bias else per
        base = starts[m] // step
        whole = pl.BlockSpec((groups, step, blk, channels), lambda i, info: (0, base + i, 0, 0))
        ahead = [n] + [n // 2] * (n_col - 1) if with_bias else [0] * n_col
        size = (sizes[m] + (sizes[m - 2] if m >= 2 else 0)) * lines
        operands = [(whole, x) for x in (query, key, value, gate, d_out)]
        if with_bias:
            operands.append((still(heads, blk, n), bias))
        return call(
            functools.partial(pack_kernel, heads, groups, with_bias),
            "pack",
            m,
            10**6,
            sizes[m] // step,
            operands,
            [part(x + step * lines, 0) for x in ahead],
            [jax.ShapeDtypeStruct((x + size, blk), jnp.bfloat16) for x in ahead],
            [pltpu.VMEM((groups, step, PIECES, channels, blk), jnp.bfloat16)],
            {},
        )

    def attend(m, total, bias_blocks, blocks, room):
        first, last = m == 0, m == chunks - 1

        def scratch(*shape, dtype=jnp.bfloat16):
            return pltpu.VMEM((per, *shape), dtype)

        operands = [(still(n if a == 0 else n // 2, blk), x) for a, x in enumerate(bias_blocks)]
        for a, x in enumerate(blocks):
            skip = (n if a == 0 else n // 2) // (per * lines) if first else 0
            operands.append((part(per * lines, skip), x))
        square = (n_col, n, blk)
        if not first:
            operands.append((still(*square), total))
        aliases, ahead = {}, 0
        if room is not None:
            aliases = {1 + len(operands) + a: a for a in range(n_col)}
            operands += [(untouched, x) for x in room]
            ahead = sizes[m + 2] // per
            out_shape = [jax.ShapeDtypeStruct(x.shape, x.dtype) for x in room]
        else:
            out_shape = [jax.ShapeDtypeStruct((sizes[m] * lines, blk), jnp.bfloat16)] * n_col
        if last:
            totals = [jax.ShapeDtypeStruct((n_row // 2, n, width), jnp.bfloat16)] * 2
        else:
            totals = [jax.ShapeDtypeStruct(square, jnp.float32)]
        deep = 4 * c
        result = call(
            functools.partial(attention_kernel, n_col, per, c, scaling, first, last),
            "attend",
            m,
            4 * 10**9,
            sizes[m] // per,
            operands,
            [part(per * lines, ahead)] * n_col + [still(*x.shape) for x in totals],
            out_shape + totals,
            [
                pltpu.VMEM(square, jnp.float32),
                pltpu.VMEM(square if last else (8, 128), jnp.float32),
                scratch(n_col, deep, blk),
                scratch(n_col, c, blk),
                scratch(deep, n),
                scratch(deep, n),
                scratch(n, deep),
                scratch(n, deep),
                scratch(n_col, c, blk),
                scratch(n_col, c, blk),
                scratch(2 * c, n, dtype=jnp.float32),
                pltpu.VMEM((2, per, n, blk), jnp.float32),
                pltpu.VMEM((2, per, n, blk), jnp.bfloat16),
                pltpu.VMEM((2, per, n, blk), jnp.bfloat16),
            ],
            aliases,
        )
        return result[:n_col], result[n_col:]

    def unpack(m, blocks, grads):
        base = starts[m] // per
        ahead = sizes[m + 2] // per if m + 2 < chunks else 0
        whole = pl.BlockSpec((groups, per, blk, channels), lambda i, info: (0, base + i, 0, 0))
        kept = [] if grads is None else list(grads)
        operands = [(whole, gate), (whole, d_out)]
        operands += [(part(per * lines, ahead), x) for x in blocks]
        aliases = {1 + len(operands) + a: a for a in range(len(kept))}
        operands += [(untouched, x) for x in kept]
        return call(
            functools.partial(unpack_kernel, heads, groups),
            "unpack",
            m,
            10**6,
            sizes[m] // per,
            operands,
            [whole] * 4 + [pl.BlockSpec((8, 128), lambda i, info: (0, 0))],
            [jax.ShapeDtypeStruct(query.shape, jnp.bfloat16)] * 4
            + [jax.ShapeDtypeStruct((8, 128), jnp.float32)],
            [pltpu.VMEM(turned_shape, jnp.bfloat16)],
            aliases,
        )

    packed = [pack(m) for m in range(chunks)]
    own, *fetched = exchange(packed[0])
    fetched = hold(fetched, [x[0] for x in packed[1:]])
    tables = [own, *fetched] + [swap(x[: n // 2]) for x in fetched]
    later = hold(packed[1][1:], fetched)
    arrived = [[own, *fetched], exchange([packed[1][0], *later])]
    totals, grads = [None], None
    for m in range(chunks):
        room = packed[m + 2] if m + 2 < chunks else None
        results, totals = attend(m, totals[0], tables, arrived[m], room)
        arrived.append(exchange(results))
    for m in range(chunks):
        *grads, token = unpack(m, arrived[m + 2], grads)

    mine, others = totals
    (others,) = hold([others], arrived[chunks][1:])
    others = swap(others)
    shares = []
    for step in range(n_row // 2):
        share = mine[step].astype(jnp.float32) + others[step].astype(jnp.float32)
        pairs = [(r, r ^ (2 * step)) for r in range(n_row)]
        share = share.astype(jnp.bfloat16)
        shares.append(lax.ppermute(share, "row", pairs) if step else share)
    total = sum(x.astype(jnp.float32) for x in shares) + token[0, 0]
    total = total.astype(jnp.bfloat16).reshape(n_col, blk, width)
    total = lax.all_to_all(total, "col", split_axis=0, concat_axis=0, tiled=True)
    total = jnp.sum(total.reshape(heads, groups, blk, width).astype(jnp.float32), axis=1)
    bias_grad = jnp.transpose(total, (0, 2, 1))
    d_query, d_key, d_value, d_gate = (x.reshape(rows, blk, channels) for x in grads)
    return d_query, d_key, d_value, d_gate, bias_grad


def solution(mesh):
    pair = P("row", "col", None)
    return jax.shard_map(
        functools.partial(on_device, mesh.shape["row"], mesh.shape["col"]),
        mesh=mesh,
        in_specs=(pair, pair, pair, pair, pair, P(None, "col", None), P()),
        out_specs=(pair, pair, pair, pair, P(None, "row", "col")),
        check_vma=False,
    )
```

```python
import functools
import itertools

import jax
import jax.numpy as jnp
from jax import lax
from jax.experimental import pallas as pl
from jax.experimental.pallas import tpu as pltpu
from jax.sharding import PartitionSpec as P

LOG2E = 1.4426950408889634
MASKED = -1e30
SHARES = (1, 3, 4, 4)
PIECES = 4


def dot(a, b, dims):
    return lax.dot_general(a, b, (dims, ((), ())), preferred_element_type=jnp.float32)


def peer_of(me, step):
    return jnp.bitwise_xor(me, step)


def selection(groups, c, me, shape, group):
    place = lax.broadcasted_iota(jnp.int32, shape, 0)
    channel = lax.broadcasted_iota(jnp.int32, shape, 1)
    peer = peer_of(me, place // c)
    found = jnp.logical_and(peer % groups == group, channel == peer // groups * c + place % c)
    return jnp.where(found, 1.0, 0.0).astype(jnp.bfloat16)


def pack_kernel(heads, groups, with_bias, info, q_ref, k_ref, v_ref, g_ref, o_ref, *refs):
    n_col = heads * groups
    outs = refs[-n_col:]
    me = info[1]
    count, _, channels = q_ref.shape[1:]
    c = channels // heads
    lines = count * PIECES * c
    selections = [selection(groups, c, me, (n_col * c, channels), g) for g in range(groups)]
    for i in range(count):
        turned = [0.0] * PIECES
        for g in range(groups):
            gated = o_ref[g, i].astype(jnp.float32) * jax.nn.sigmoid(g_ref[g, i].astype(jnp.float32))
            pieces = (q_ref[g, i], k_ref[g, i], v_ref[g, i], gated.astype(jnp.bfloat16))
            for piece, x in enumerate(pieces):
                turned[piece] += dot(selections[g], x, ((1,), (1,)))
        for step in range(n_col):
            base = outs[step].shape[0] - lines
            for piece in range(PIECES):
                at = base + (i * PIECES + piece) * c
                block = turned[piece][step * c : (step + 1) * c]
                outs[step][at : at + c, :] = block.astype(jnp.bfloat16)
    if with_bias:
        for step in range(n_col):
            base = outs[step].shape[0] - lines
            keys = pl.ds(pl.multiple_of(info[2] * base, base), base) if step else slice(None)
            outs[step][:base, :] = refs[0][peer_of(me, step) // groups, :, keys].T


def unpack_kernel(heads, groups, info, g_ref, o_ref, *refs):
    n_col = heads * groups
    ins, (dq, dk, dv, dg, token, whole) = refs[:n_col], refs[-6:]
    token[...] = jnp.zeros_like(token)
    me = info[1]
    count, blk, channels = g_ref.shape[1:]
    c = channels // heads
    square = (blk, blk)
    same = lax.broadcasted_iota(jnp.int32, square, 0) == lax.broadcasted_iota(jnp.int32, square, 1)
    same = jnp.where(same, 1.0, 0.0).astype(jnp.bfloat16)
    for i in range(count):
        for step in range(n_col):
            peer = peer_of(me, step)
            head = pl.multiple_of(peer // groups * c, c)
            for piece in range(PIECES):
                at = (i * PIECES + piece) * c
                whole[peer % groups, i, piece, pl.ds(head, c), :] = ins[step][at : at + c, :]
        for g in range(groups):
            turned = [dot(same, whole[g, i, piece], ((1,), (1,))) for piece in range(PIECES)]
            dq[g, i] = turned[0].astype(jnp.bfloat16)
            dk[g, i] = turned[1].astype(jnp.bfloat16)
            dv[g, i] = turned[2].astype(jnp.bfloat16)
            s = jax.nn.sigmoid(g_ref[g, i].astype(jnp.float32))
            up = o_ref[g, i].astype(jnp.float32)
            dg[g, i] = (up * turned[3] * s * (1.0 - s)).astype(jnp.bfloat16)


def woven(*queues):
    order = [(at / len(q), which, at) for which, q in enumerate(queues) for at in range(len(q))]
    for _, which, at in sorted(order):
        queues[which][at]()


def attention_kernel(n_col, together, c, scaling, first, last, info, *refs):
    bias_in, ins, refs = refs[: 2 * n_col - 1], refs[2 * n_col - 1 : 3 * n_col - 1], refs[3 * n_col - 1 :]
    scratch, refs = refs[-14:], refs[:-14]
    bias, total_s, q_s, g_s, k_s, v_s, k_turned, v_turned, dq_s, at_s, dkv, logits, both, sides = scratch
    if not first:
        total_in = refs[0]
    totals = refs[-2:] if last else refs[-1:]
    outs, total_out = refs[-n_col - len(totals) : -len(totals)], totals[0]
    total = total_s if last else total_out
    length, me, side, level = info[0], info[1], info[2], info[3]
    blk = ins[0].shape[1]
    n = n_col * blk
    tile = min(256, n)
    tiles = range(0, n, tile)
    deep = k_s.shape[1]
    some = range(together)

    @pl.when(pl.program_id(0) == 0)
    def _():
        half = n // 2
        bias[me] = bias_in[0][...].astype(jnp.float32) * LOG2E
        for step in range(1, n_col):
            for table, which in ((bias_in[step], side), (bias_in[n_col + step - 1], 1 - side)):
                keys = pl.ds(pl.multiple_of(which * half, half), half)
                bias[peer_of(me, step), keys, :] = table[...].astype(jnp.float32) * LOG2E
        if first:
            total[...] = jnp.zeros_like(total)
        else:
            total[...] = total_in[...]
        rows = lax.broadcasted_iota(jnp.int32, (deep - 2 * c, n), 0)
        keys = lax.broadcasted_iota(jnp.int32, (deep - 2 * c, n), 1)
        mask = jnp.logical_and(rows == 0, keys >= length)
        for r in some:
            k_s[r, 2 * c :, :] = jnp.where(mask, MASKED, 0.0).astype(jnp.bfloat16)
            v_s[r, c:, :] = jnp.ones((deep - c, n), jnp.bfloat16)
            q_s[r, :, 2 * c :, :] = jnp.ones((n_col, deep - 2 * c, blk), jnp.bfloat16)
        sides[...] = jnp.zeros_like(sides)

    def rows_of(r, piece):
        at = (r * PIECES + piece) * c
        return slice(at, at + c)

    for r in some:
        for step in range(n_col):
            jb = peer_of(me, step)
            span = pl.ds(pl.multiple_of(jb * blk, blk), blk)
            q = ins[step][rows_of(r, 0), :].astype(jnp.float32) * (scaling * LOG2E)
            high = q.astype(jnp.bfloat16)
            q_s[r, jb, :c, :] = high
            q_s[r, jb, c : 2 * c, :] = (q - high.astype(jnp.float32)).astype(jnp.bfloat16)
            k = ins[step][rows_of(r, 1), :]
            k_s[r, :c, span] = k
            k_s[r, c : 2 * c, span] = k
            v_s[r, :c, span] = ins[step][rows_of(r, 2), :]
            g_s[r, jb] = ins[step][rows_of(r, 3), :]
    for r in some:
        k_turned[r] = k_s[r].T
        v_turned[r] = v_s[r].T
    tops, scales = {}, {}

    def gradient(r):
        return slice(2 * r * blk, (2 * r + 1) * blk)

    def weight(r):
        return slice((2 * r + 1) * blk, (2 * r + 2) * blk)

    def score(jb, r, t):
        part = dot(k_turned[r, t : t + tile, :], q_s[r, jb], ((1,), (0,))) + bias[jb, t : t + tile, :]
        logits[jb % 2, r, t : t + tile, :] = part
        top = jnp.max(part.reshape(tile // 8, 8, blk), axis=0)
        tops[jb, r] = jnp.maximum(tops[jb, r], top) if t else top

    def expand(jb, r, t):
        if t == 0:
            tops[jb, r] = jnp.max(tops[jb, r], axis=0, keepdims=True)
        part = jnp.exp2(logits[jb % 2, r, t : t + tile, :] - tops[jb, r])
        both[jb % 2, t : t + tile, weight(r)] = part.astype(jnp.bfloat16)

    def attend(jb, r):
        summed = dot(v_s[r, : c + 16, :], both[jb % 2, :, weight(r)], ((1,), (0,)))
        inverse = 1.0 / summed[c : c + 1, :]
        attended = summed[:c, :] * inverse
        at_s[r, jb] = attended.astype(jnp.bfloat16)
        g = g_s[r, jb].astype(jnp.float32)
        row_dot = jnp.sum(g * attended, axis=0, keepdims=True) * (-inverse)
        high = row_dot.astype(jnp.bfloat16).astype(jnp.float32)
        rows = lax.broadcasted_iota(jnp.int32, (deep - c, blk), 0)
        tail = jnp.where(rows == 0, high, jnp.where(rows == 1, row_dot - high, 0.0))
        scaled = (g * inverse).astype(jnp.bfloat16)
        scales[jb, r] = jnp.concatenate([scaled, tail.astype(jnp.bfloat16)], axis=0)
        sides[jb % 2, 2 * r * c : (2 * r + 1) * c, gradient(r)] = q_s[r, jb, :c, :]
        sides[jb % 2, (2 * r + 1) * c : (2 * r + 2) * c, weight(r)] = scaled

    def back(jb, t):
        added = total[jb, t : t + tile, :]
        for r in some:
            grad = dot(v_turned[r, t : t + tile, :], scales[jb, r], ((1,), (0,)))
            grad = grad * both[jb % 2, t : t + tile, weight(r)].astype(jnp.float32)
            added = added + grad
            both[jb % 2, t : t + tile, gradient(r)] = grad.astype(jnp.bfloat16)
        total[jb, t : t + tile, :] = added

    def query_grad(jb, r):
        part = dot(k_s[r, :c, :], both[jb % 2, :, gradient(r)], ((1,), (0,)))
        dq_s[r, jb] = (part * scaling).astype(jnp.bfloat16)

    def key_value_grad(jb, t):
        part = dot(both[jb % 2, t : t + tile, :], sides[jb % 2], ((1,), (1,)))
        dkv[t : t + tile, :] = part + dkv[t : t + tile, :] if jb else part

    def each(step, jb, *ranges):
        if not 0 <= jb < n_col:
            return []
        return [functools.partial(step, jb, *at) for at in itertools.product(*ranges)]

    def finish(jb):
        return each(query_grad, jb, some) + each(key_value_grad, jb, tiles)

    woven(each(score, 0, some, tiles))
    for jb in range(n_col):
        woven(each(expand, jb, some, tiles), finish(jb - 1))
        woven(each(attend, jb, some), each(score, jb + 1, some, tiles[: len(tiles) // 2]))
        woven(each(back, jb, tiles), each(score, jb + 1, some, tiles[len(tiles) // 2 :]))
    woven(finish(n_col - 1))

    for step in range(n_col):
        jb = peer_of(me, step)
        turned = dkv[pl.ds(pl.multiple_of(jb * blk, blk), blk), :].T
        for r in some:
            at = 2 * r * c
            outs[step][rows_of(r, 0), :] = dq_s[r, jb]
            outs[step][rows_of(r, 1), :] = (turned[at : at + c] * (1.0 / LOG2E)).astype(jnp.bfloat16)
            outs[step][rows_of(r, 2), :] = turned[at + c : at + 2 * c].astype(jnp.bfloat16)
            outs[step][rows_of(r, 3), :] = at_s[r, jb]

    if last:

        @pl.when(pl.program_id(0) == pl.num_programs(0) - 1)
        def _():
            mine, others = totals
            pairs, _, width = mine.shape
            for pair in range(pairs):
                at = 2 * pair * width
                both = total[at // blk, :, at % blk : at % blk + 2 * width].astype(jnp.bfloat16)
                even, odd = both[:, :width], both[:, width:]
                mine[peer_of(level, pair)] = jnp.where(side == 0, even, odd)
                others[peer_of(level, pair)] = jnp.where(side == 0, odd, even)


def hold_kernel(*refs):
    pass


def params(mib):
    return pltpu.CompilerParams(
        dimension_semantics=("arbitrary",), vmem_limit_bytes=mib * 1024 * 1024
    )


def on_device(n_row, n_col, query, key, value, gate, d_out, bias, length):
    rows, blk, channels = query.shape
    heads, _, n = bias.shape
    c = channels // heads
    groups = n_col // heads
    share = rows // groups
    sizes = [share * weight // sum(SHARES) for weight in SHARES]
    starts = [sum(sizes[:m]) for m in range(len(sizes))]
    assert groups * heads == n_col and n == n_col * blk and groups * sum(sizes) == rows
    scaling = c ** (-0.5)
    per = 2 if all(size % 2 == 0 for size in sizes) else 1
    split_rows = (groups, share, blk, channels)
    query, key, value, gate, d_out = (x.reshape(split_rows) for x in (query, key, value, gate, d_out))
    row = lax.axis_index("row")
    info = jnp.stack([length[0], lax.axis_index("col"), row % 2, row // 2]).astype(jnp.int32)
    width = n // n_row
    lines = PIECES * c
    chunks = len(sizes)
    turned_shape = (groups, per, PIECES, channels, blk)

    untouched = pl.BlockSpec(memory_space=pl.ANY)

    def exchange(blocks):
        pairs = [[(a, a ^ step) for a in range(n_col)] for step in range(n_col)]
        return [blocks[0]] + [lax.ppermute(blocks[step], "col", pairs[step]) for step in range(1, n_col)]

    def swap(x):
        return lax.ppermute(x, "row", [(r, r ^ 1) for r in range(n_row)])

    def hold(blocks, until):
        count = len(blocks)
        return pl.pallas_call(
            hold_kernel,
            in_specs=[untouched] * (count + len(until)),
            out_specs=[untouched] * count,
            out_shape=[jax.ShapeDtypeStruct(x.shape, x.dtype) for x in blocks],
            input_output_aliases={a: a for a in range(count)},
            name="hold",
        )(*blocks, *until)

    def call(kernel, name, m, flops, grid, operands, out_specs, out_shape, scratch, aliases):
        return pl.pallas_call(
            kernel,
            grid_spec=pltpu.PrefetchScalarGridSpec(
                num_scalar_prefetch=1,
                grid=(grid,),
                in_specs=[spec for spec, _ in operands],
                out_specs=out_specs,
                scratch_shapes=scratch,
            ),
            out_shape=out_shape,
            input_output_aliases=aliases,
            compiler_params=params(60),
            cost_estimate=pl.CostEstimate(
                flops=sizes[m] * flops, bytes_accessed=sizes[m] * blk * channels * 18, transcendentals=0
            ),
            name=name,
        )(info, *[x for _, x in operands])

    def still(*shape):
        return pl.BlockSpec(shape, lambda i, info: (0,) * len(shape), pipeline_mode=pl.Buffered(1))

    def part(size, skip):
        return pl.BlockSpec((size, blk), lambda i, info: (skip + i, 0))

    def pack(m):
        with_bias = m == 0
        step = sizes[m] if with_bias else per
        base = starts[m] // step
        whole = pl.BlockSpec((groups, step, blk, channels), lambda i, info: (0, base + i, 0, 0))
        ahead = [n] + [n // 2] * (n_col - 1) if with_bias else [0] * n_col
        size = (sizes[m] + (sizes[m - 2] if m >= 2 else 0)) * lines
        operands = [(whole, x) for x in (query, key, value, gate, d_out)]
        if with_bias:
            operands.append((still(heads, blk, n), bias))
        return call(
            functools.partial(pack_kernel, heads, groups, with_bias),
            "pack",
            m,
            10**6,
            sizes[m] // step,
            operands,
            [part(x + step * lines, 0) for x in ahead],
            [jax.ShapeDtypeStruct((x + size, blk), jnp.bfloat16) for x in ahead],
            [],
            {},
        )

    def attend(m, total, bias_blocks, blocks, room):
        first, last = m == 0, m == chunks - 1

        def scratch(*shape, dtype=jnp.bfloat16):
            return pltpu.VMEM((per, *shape), dtype)

        operands = [(still(n if a == 0 else n // 2, blk), x) for a, x in enumerate(bias_blocks)]
        for a, x in enumerate(blocks):
            skip = (n if a == 0 else n // 2) // (per * lines) if first else 0
            operands.append((part(per * lines, skip), x))
        square = (n_col, n, blk)
        if not first:
            operands.append((still(*square), total))
        aliases, ahead = {}, 0
        if room is not None:
            aliases = {1 + len(operands) + a: a for a in range(n_col)}
            operands += [(untouched, x) for x in room]
            ahead = sizes[m + 2] // per
            out_shape = [jax.ShapeDtypeStruct(x.shape, x.dtype) for x in room]
        else:
            out_shape = [jax.ShapeDtypeStruct((sizes[m] * lines, blk), jnp.bfloat16)] * n_col
        if last:
            totals = [jax.ShapeDtypeStruct((n_row // 2, n, width), jnp.bfloat16)] * 2
        else:
            totals = [jax.ShapeDtypeStruct(square, jnp.float32)]
        deep = 4 * c
        result = call(
            functools.partial(attention_kernel, n_col, per, c, scaling, first, last),
            "attend",
            m,
            4 * 10**9,
            sizes[m] // per,
            operands,
            [part(per * lines, ahead)] * n_col + [still(*x.shape) for x in totals],
            out_shape + totals,
            [
                pltpu.VMEM(square, jnp.float32),
                pltpu.VMEM(square if last else (8, 128), jnp.float32),
                scratch(n_col, deep, blk),
                scratch(n_col, c, blk),
                scratch(deep, n),
                scratch(deep, n),
                scratch(n, deep),
                scratch(n, deep),
                scratch(n_col, c, blk),
                scratch(n_col, c, blk),
                pltpu.VMEM((n, 2 * per * c), jnp.float32),
                pltpu.VMEM((2, per, n, blk), jnp.float32),
                pltpu.VMEM((2, n, 2 * per * blk), jnp.bfloat16),
                pltpu.VMEM((2, 2 * per * c, 2 * per * blk), jnp.bfloat16),
            ],
            aliases,
        )
        return result[:n_col], result[n_col:]

    def unpack(m, blocks, grads):
        base = starts[m] // per
        ahead = sizes[m + 2] // per if m + 2 < chunks else 0
        whole = pl.BlockSpec((groups, per, blk, channels), lambda i, info: (0, base + i, 0, 0))
        kept = [] if grads is None else list(grads)
        operands = [(whole, gate), (whole, d_out)]
        operands += [(part(per * lines, ahead), x) for x in blocks]
        aliases = {1 + len(operands) + a: a for a in range(len(kept))}
        operands += [(untouched, x) for x in kept]
        return call(
            functools.partial(unpack_kernel, heads, groups),
            "unpack",
            m,
            10**6,
            sizes[m] // per,
            operands,
            [whole] * 4 + [pl.BlockSpec((8, 128), lambda i, info: (0, 0))],
            [jax.ShapeDtypeStruct(query.shape, jnp.bfloat16)] * 4
            + [jax.ShapeDtypeStruct((8, 128), jnp.float32)],
            [pltpu.VMEM(turned_shape, jnp.bfloat16)],
            aliases,
        )

    packed = [pack(m) for m in range(chunks)]
    own, *fetched = exchange(packed[0])
    fetched = hold(fetched, [x[0] for x in packed[1:]])
    tables = [own, *fetched] + [swap(x[: n // 2]) for x in fetched]
    later = hold(packed[1][1:], fetched)
    arrived = [[own, *fetched], exchange([packed[1][0], *later])]
    totals, grads = [None], None
    for m in range(chunks):
        room = packed[m + 2] if m + 2 < chunks else None
        results, totals = attend(m, totals[0], tables, arrived[m], room)
        arrived.append(exchange(results))
    tokens = []
    for m in range(chunks):
        *grads, token = unpack(m, arrived[m + 2], grads)
        tokens.append(token)

    mine, others = totals
    (others,) = hold([others], arrived[chunks][1:])
    others = swap(others)
    shares = []
    for step in range(n_row // 2):
        share = mine[step].astype(jnp.float32) + others[step].astype(jnp.float32)
        pairs = [(r, r ^ (2 * step)) for r in range(n_row)]
        share = share.astype(jnp.bfloat16)
        shares.append(lax.ppermute(share, "row", pairs) if step else share)
    total = sum(x.astype(jnp.float32) for x in shares) + tokens[-2][0, 0]
    total = total.astype(jnp.bfloat16).reshape(n_col, blk, width)
    total = lax.all_to_all(total, "col", split_axis=0, concat_axis=0, tiled=True)
    total = jnp.sum(total.reshape(heads, groups, blk, width).astype(jnp.float32), axis=1)
    bias_grad = jnp.transpose(total, (0, 2, 1))
    d_query, d_key, d_value, d_gate = (x.reshape(rows, blk, channels) for x in grads)
    return d_query, d_key, d_value, d_gate, bias_grad


def solution(mesh):
    pair = P("row", "col", None)
    return jax.shard_map(
        functools.partial(on_device, mesh.shape["row"], mesh.shape["col"]),
        mesh=mesh,
        in_specs=(pair, pair, pair, pair, pair, P(None, "col", None), P()),
        out_specs=(pair, pair, pair, pair, P(None, "row", "col")),
        check_vma=False,
    )
```

```python
import functools
import itertools

import jax
import jax.numpy as jnp
from jax import lax
from jax.experimental import pallas as pl
from jax.experimental.pallas import tpu as pltpu
from jax.sharding import PartitionSpec as P

LOG2E = 1.4426950408889634
MASKED = -1e30
SHARES = (1, 3, 4, 4)
PIECES = 4


def dot(a, b, dims):
    return lax.dot_general(a, b, (dims, ((), ())), preferred_element_type=jnp.float32)


def peer_of(me, step):
    return jnp.bitwise_xor(me, step)


def pack_kernel(heads, groups, with_bias, info, q_ref, k_ref, v_ref, g_ref, o_ref, *refs):
    n_col = heads * groups
    outs, turned = refs[-1 - n_col : -1], refs[-1]
    me = info[1]
    count, _, channels = q_ref.shape[1:]
    c = channels // heads
    lines = count * PIECES * c
    for i in range(count):
        for g in range(groups):
            gated = o_ref[g, i].astype(jnp.float32) * jax.nn.sigmoid(g_ref[g, i].astype(jnp.float32))
            pieces = (q_ref[g, i], k_ref[g, i], v_ref[g, i], gated.astype(jnp.bfloat16))
            for piece, x in enumerate(pieces):
                turned[g, i, piece] = x.T
        for step in range(n_col):
            peer = peer_of(me, step)
            head = pl.multiple_of(peer // groups * c, c)
            base = outs[step].shape[0] - lines
            for piece in range(PIECES):
                at = base + (i * PIECES + piece) * c
                outs[step][at : at + c, :] = turned[peer % groups, i, piece, pl.ds(head, c), :]
    if with_bias:
        for step in range(n_col):
            base = outs[step].shape[0] - lines
            keys = pl.ds(pl.multiple_of(info[2] * base, base), base) if step else slice(None)
            outs[step][:base, :] = refs[0][peer_of(me, step) // groups, :, keys].T


def unpack_kernel(heads, groups, info, g_ref, o_ref, *refs):
    n_col = heads * groups
    ins, (dq, dk, dv, dg, token, whole) = refs[:n_col], refs[-6:]
    token[...] = jnp.zeros_like(token)
    me = info[1]
    count, _, channels = g_ref.shape[1:]
    c = channels // heads
    for i in range(count):
        for step in range(n_col):
            peer = peer_of(me, step)
            head = pl.multiple_of(peer // groups * c, c)
            for piece in range(PIECES):
                at = (i * PIECES + piece) * c
                whole[peer % groups, i, piece, pl.ds(head, c), :] = ins[step][at : at + c, :]
        for g in range(groups):
            dq[g, i] = whole[g, i, 0].T
            dk[g, i] = whole[g, i, 1].T
            dv[g, i] = whole[g, i, 2].T
            attended = whole[g, i, 3].T.astype(jnp.float32)
            s = jax.nn.sigmoid(g_ref[g, i].astype(jnp.float32))
            dg[g, i] = (o_ref[g, i].astype(jnp.float32) * attended * s * (1.0 - s)).astype(jnp.bfloat16)


def reversed_bits(x, count):
    return sum((x // 2**bit % 2) * (count // 2 ** (bit + 1)) for bit in range(count.bit_length() - 1))


def woven(*queues):
    order = [(at / len(q), which, at) for which, q in enumerate(queues) for at in range(len(q))]
    for _, which, at in sorted(order):
        queues[which][at]()


def attention_kernel(n_col, together, c, scaling, first, last, info, *refs):
    bias_in, ins, refs = refs[: 2 * n_col - 1], refs[2 * n_col - 1 : 3 * n_col - 1], refs[3 * n_col - 1 :]
    scratch, refs = refs[-14:], refs[:-14]
    bias, total_s, q_s, g_s, k_s, v_s, k_turned, v_turned, dq_s, at_s, dkv, logits, weights, grads = scratch
    if not first:
        total_in = refs[0]
    totals = refs[-2:] if last else refs[-1:]
    outs, total_out = refs[-n_col - len(totals) : -len(totals)], totals[0]
    total = total_s if last else total_out
    length, me, side, level = info[0], info[1], info[2], info[3]
    blk = ins[0].shape[1]
    n = n_col * blk
    tile = min(256, n)
    tiles = range(0, n, tile)
    deep = k_s.shape[1]
    some = range(together)

    @pl.when(pl.program_id(0) == 0)
    def _():
        half = n // 2
        bias[me] = bias_in[0][...].astype(jnp.float32) * LOG2E
        for step in range(1, n_col):
            for table, which in ((bias_in[step], side), (bias_in[n_col + step - 1], 1 - side)):
                keys = pl.ds(pl.multiple_of(which * half, half), half)
                bias[peer_of(me, step), keys, :] = table[...].astype(jnp.float32) * LOG2E
        if first:
            total[...] = jnp.zeros_like(total)
        else:
            total[...] = total_in[...]
        rows = lax.broadcasted_iota(jnp.int32, (deep - 2 * c, n), 0)
        keys = lax.broadcasted_iota(jnp.int32, (deep - 2 * c, n), 1)
        mask = jnp.logical_and(rows == 0, keys >= length)
        for r in some:
            k_s[r, 2 * c :, :] = jnp.where(mask, MASKED, 0.0).astype(jnp.bfloat16)
            v_s[r, c:, :] = jnp.ones((deep - c, n), jnp.bfloat16)
            q_s[r, :, 2 * c :, :] = jnp.ones((n_col, deep - 2 * c, blk), jnp.bfloat16)

    def rows_of(r, piece):
        at = (r * PIECES + piece) * c
        return slice(at, at + c)

    for r in some:
        for step in range(n_col):
            jb = peer_of(me, step)
            span = pl.ds(pl.multiple_of(jb * blk, blk), blk)
            q = ins[step][rows_of(r, 0), :].astype(jnp.float32) * (scaling * LOG2E)
            high = q.astype(jnp.bfloat16)
            q_s[r, jb, :c, :] = high
            q_s[r, jb, c : 2 * c, :] = (q - high.astype(jnp.float32)).astype(jnp.bfloat16)
            k = ins[step][rows_of(r, 1), :]
            k_s[r, :c, span] = k
            k_s[r, c : 2 * c, span] = k
            v_s[r, :c, span] = ins[step][rows_of(r, 2), :]
            g_s[r, jb] = ins[step][rows_of(r, 3), :]
    for r in some:
        k_turned[r] = k_s[r].T
        v_turned[r] = v_s[r].T
    tops, scaled, scales = {}, {}, {}

    def score(jb, r, t):
        part = dot(k_turned[r, t : t + tile, :], q_s[r, jb], ((1,), (0,))) + bias[jb, t : t + tile, :]
        logits[jb % 2, r, t : t + tile, :] = part
        top = jnp.max(part.reshape(tile // 8, 8, blk), axis=0)
        tops[jb, r] = jnp.maximum(tops[jb, r], top) if t else top

    def expand(jb, r, t):
        if t == 0:
            tops[jb, r] = jnp.max(tops[jb, r], axis=0, keepdims=True)
        part = jnp.exp2(logits[jb % 2, r, t : t + tile, :] - tops[jb, r])
        weights[jb % 2, r, t : t + tile, :] = part.astype(jnp.bfloat16)

    def attend(jb, r):
        summed = dot(v_s[r, : c + 16, :], weights[jb % 2, r], ((1,), (0,)))
        inverse = 1.0 / summed[c : c + 1, :]
        attended = summed[:c, :] * inverse
        at_s[r, jb] = attended.astype(jnp.bfloat16)
        g = g_s[r, jb].astype(jnp.float32)
        row_dot = jnp.sum(g * attended, axis=0, keepdims=True) * (-inverse)
        high = row_dot.astype(jnp.bfloat16).astype(jnp.float32)
        rows = lax.broadcasted_iota(jnp.int32, (deep - c, blk), 0)
        tail = jnp.where(rows == 0, high, jnp.where(rows == 1, row_dot - high, 0.0))
        scaled[jb, r] = (g * inverse).astype(jnp.bfloat16)
        scales[jb, r] = jnp.concatenate([scaled[jb, r], tail.astype(jnp.bfloat16)], axis=0)

    def back(jb, t):
        added = total[jb, t : t + tile, :]
        for r in some:
            grad = dot(v_turned[r, t : t + tile, :], scales[jb, r], ((1,), (0,)))
            grad = grad * weights[jb % 2, r, t : t + tile, :].astype(jnp.float32)
            added = added + grad
            grads[jb % 2, r, t : t + tile, :] = grad.astype(jnp.bfloat16)
        total[jb, t : t + tile, :] = added

    def query_grad(jb, r):
        dq_s[r, jb] = (dot(k_s[r, :c, :], grads[jb % 2, r], ((1,), (0,))) * scaling).astype(jnp.bfloat16)

    def add_to(at, r, jb, part):
        if jb:
            part = part + dkv[r, at : at + c, :]
        dkv[r, at : at + c, :] = part

    def key_grad(jb, r):
        add_to(0, r, jb, dot(q_s[r, jb, :c, :], grads[jb % 2, r], ((1,), (1,))))

    def value_grad(jb, r):
        add_to(c, r, jb, dot(scaled[jb, r], weights[jb % 2, r], ((1,), (1,))))

    def each(step, jb, *ranges):
        if not 0 <= jb < n_col:
            return []
        return [functools.partial(step, jb, *at) for at in itertools.product(*ranges)]

    def finish(jb):
        return each(value_grad, jb, some) + each(query_grad, jb, some) + each(key_grad, jb, some)

    woven(each(score, 0, some, tiles))
    for jb in range(n_col):
        woven(each(expand, jb, some, tiles), finish(jb - 1))
        woven(each(attend, jb, some), each(score, jb + 1, some, tiles[: len(tiles) // 2]))
        woven(each(back, jb, tiles), each(score, jb + 1, some, tiles[len(tiles) // 2 :]))
    woven(finish(n_col - 1))

    for r in some:
        for step in range(n_col):
            jb = peer_of(me, step)
            span = pl.ds(pl.multiple_of(jb * blk, blk), blk)
            outs[step][rows_of(r, 0), :] = dq_s[r, jb]
            outs[step][rows_of(r, 1), :] = (dkv[r, :c, span] * (1.0 / LOG2E)).astype(jnp.bfloat16)
            outs[step][rows_of(r, 2), :] = dkv[r, c:, span].astype(jnp.bfloat16)
            outs[step][rows_of(r, 3), :] = at_s[r, jb]

    if last:

        @pl.when(pl.program_id(0) == pl.num_programs(0) - 1)
        def _():
            mine, others = totals
            pairs, _, width = mine.shape
            for pair in range(pairs):
                at = 2 * pair * width
                both = total[at // blk, :, at % blk : at % blk + 2 * width].astype(jnp.bfloat16)
                even, odd = both[:, :width], both[:, width:]
                place = peer_of(level, reversed_bits(pair, pairs))
                mine[place] = jnp.where(side == 0, even, odd)
                others[place] = jnp.where(side == 0, odd, even)


def hold_kernel(*refs):
    pass


def params(mib):
    return pltpu.CompilerParams(
        dimension_semantics=("arbitrary",), vmem_limit_bytes=mib * 1024 * 1024
    )


def on_device(n_row, n_col, query, key, value, gate, d_out, bias, length):
    rows, blk, channels = query.shape
    heads, _, n = bias.shape
    c = channels // heads
    groups = n_col // heads
    share = rows // groups
    sizes = [share * weight // sum(SHARES) for weight in SHARES]
    order = [m for m in range(len(sizes)) if m >= 2] + [0, 1]
    starts = [sum(sizes[o] for o in order[: order.index(m)]) for m in range(len(sizes))]
    assert groups * heads == n_col and n == n_col * blk and groups * sum(sizes) == rows
    scaling = c ** (-0.5)
    per = 2 if all(size % 2 == 0 for size in sizes) else 1
    split_rows = (groups, share, blk, channels)
    query, key, value, gate, d_out = (x.reshape(split_rows) for x in (query, key, value, gate, d_out))
    row = lax.axis_index("row")
    level = reversed_bits(row // 2, n_row // 2)
    info = jnp.stack([length[0], lax.axis_index("col"), row % 2, level]).astype(jnp.int32)
    width = n // n_row
    lines = PIECES * c
    chunks = len(sizes)

    untouched = pl.BlockSpec(memory_space=pl.ANY)

    def exchange(blocks):
        pairs = [[(a, a ^ step) for a in range(n_col)] for step in range(n_col)]
        return [blocks[0]] + [lax.ppermute(blocks[step], "col", pairs[step]) for step in range(1, n_col)]

    def swap(x):
        return lax.ppermute(x, "row", [(r, r ^ 1) for r in range(n_row)])

    def hold(blocks, until):
        count = len(blocks)
        return pl.pallas_call(
            hold_kernel,
            in_specs=[untouched] * (count + len(until)),
            out_specs=[untouched] * count,
            out_shape=[jax.ShapeDtypeStruct(x.shape, x.dtype) for x in blocks],
            input_output_aliases={a: a for a in range(count)},
            name="hold",
        )(*blocks, *until)

    def call(kernel, name, m, flops, grid, operands, out_specs, out_shape, scratch, aliases):
        return pl.pallas_call(
            kernel,
            grid_spec=pltpu.PrefetchScalarGridSpec(
                num_scalar_prefetch=1,
                grid=(grid,),
                in_specs=[spec for spec, _ in operands],
                out_specs=out_specs,
                scratch_shapes=scratch,
            ),
            out_shape=out_shape,
            input_output_aliases=aliases,
            compiler_params=params(34 if name == "attend" else 60),
            cost_estimate=pl.CostEstimate(
                flops=sizes[m] * flops, bytes_accessed=sizes[m] * blk * channels * 18, transcendentals=0
            ),
            name=name,
        )(info, *[x for _, x in operands])

    def still(*shape):
        return pl.BlockSpec(shape, lambda i, info: (0,) * len(shape), pipeline_mode=pl.Buffered(1))

    def part(size, skip):
        return pl.BlockSpec((size, blk), lambda i, info: (skip + i, 0))

    def rows_a_step(*counts):
        return max(step for step in range(1, 5) if all(count % step == 0 for count in counts))

    def pack(m):
        with_bias = m == 0
        step = rows_a_step(sizes[m], starts[m])
        assert not with_bias or step == sizes[m]
        base = starts[m] // step
        whole = pl.BlockSpec((groups, step, blk, channels), lambda i, info: (0, base + i, 0, 0))
        ahead = [n] + [n // 2] * (n_col - 1) if with_bias else [0] * n_col
        size = (sizes[m] + (sizes[m - 2] if m >= 2 else 0)) * lines
        operands = [(whole, x) for x in (query, key, value, gate, d_out)]
        if with_bias:
            operands.append((still(heads, blk, n), bias))
        return call(
            functools.partial(pack_kernel, heads, groups, with_bias),
            "pack",
            m,
            10**6,
            sizes[m] // step,
            operands,
            [part(x + step * lines, 0) for x in ahead],
            [jax.ShapeDtypeStruct((x + size, blk), jnp.bfloat16) for x in ahead],
            [pltpu.VMEM((groups, step, PIECES, channels, blk), jnp.bfloat16)],
            {},
        )

    def attend(m, total, bias_blocks, blocks, room):
        first, last = m == 0, m == chunks - 1

        def scratch(*shape, dtype=jnp.bfloat16):
            return pltpu.VMEM((per, *shape), dtype)

        operands = [(still(n if a == 0 else n // 2, blk), x) for a, x in enumerate(bias_blocks)]
        for a, x in enumerate(blocks):
            skip = (n if a == 0 else n // 2) // (per * lines) if first else 0
            operands.append((part(per * lines, skip), x))
        square = (n_col, n, blk)
        if not first:
            operands.append((still(*square), total))
        aliases, ahead = {}, 0
        if room is not None:
            aliases = {1 + len(operands) + a: a for a in range(n_col)}
            operands += [(untouched, x) for x in room]
            ahead = sizes[m + 2] // per
            out_shape = [jax.ShapeDtypeStruct(x.shape, x.dtype) for x in room]
        else:
            out_shape = [jax.ShapeDtypeStruct((sizes[m] * lines, blk), jnp.bfloat16)] * n_col
        if last:
            totals = [jax.ShapeDtypeStruct((n_row // 2, n, width), jnp.bfloat16)] * 2
        else:
            totals = [jax.ShapeDtypeStruct(square, jnp.float32)]
        deep = 4 * c
        result = call(
            functools.partial(attention_kernel, n_col, per, c, scaling, first, last),
            "attend",
            m,
            4 * 10**9,
            sizes[m] // per,
            operands,
            [part(per * lines, ahead)] * n_col + [still(*x.shape) for x in totals],
            out_shape + totals,
            [
                pltpu.VMEM(square, jnp.float32),
                pltpu.VMEM(square if last else (8, 128), jnp.float32),
                scratch(n_col, deep, blk),
                scratch(n_col, c, blk),
                scratch(deep, n),
                scratch(deep, n),
                scratch(n, deep),
                scratch(n, deep),
                scratch(n_col, c, blk),
                scratch(n_col, c, blk),
                scratch(2 * c, n, dtype=jnp.float32),
                pltpu.VMEM((2, per, n, blk), jnp.float32),
                pltpu.VMEM((2, per, n, blk), jnp.bfloat16),
                pltpu.VMEM((2, per, n, blk), jnp.bfloat16),
            ],
            aliases,
        )
        return result[:n_col], result[n_col:]

    def unpack(m, blocks, grads):
        ahead = sizes[m + 2] if m + 2 < chunks else 0
        step = rows_a_step(sizes[m], starts[m], ahead)
        base = starts[m] // step
        whole = pl.BlockSpec((groups, step, blk, channels), lambda i, info: (0, base + i, 0, 0))
        kept = [] if grads is None else list(grads)
        operands = [(whole, gate), (whole, d_out)]
        operands += [(part(step * lines, ahead // step), x) for x in blocks]
        aliases = {1 + len(operands) + a: a for a in range(len(kept))}
        operands += [(untouched, x) for x in kept]
        return call(
            functools.partial(unpack_kernel, heads, groups),
            "unpack",
            m,
            10**6,
            sizes[m] // step,
            operands,
            [whole] * 4 + [pl.BlockSpec((8, 128), lambda i, info: (0, 0))],
            [jax.ShapeDtypeStruct(query.shape, jnp.bfloat16)] * 4
            + [jax.ShapeDtypeStruct((8, 128), jnp.float32)],
            [pltpu.VMEM((groups, step, PIECES, channels, blk), jnp.bfloat16)],
            aliases,
        )

    packed = [pack(m) for m in range(chunks)]
    own, *fetched = exchange(packed[0])
    fetched = hold(fetched, [x[0] for x in packed[1:]])
    tables = [own, *fetched] + [swap(x[: n // 2]) for x in fetched]
    later = hold(packed[1][1:], fetched)
    arrived = [[own, *fetched], exchange([packed[1][0], *later])]
    totals, grads = [None], None
    for m in range(chunks):
        room = packed[m + 2] if m + 2 < chunks else None
        results, totals = attend(m, totals[0], tables, arrived[m], room)
        arrived.append(exchange(results))
    tokens = []
    for m in range(chunks):
        *grads, token = unpack(m, arrived[m + 2], grads)
        tokens.append(token)

    mine, others = totals
    (others,) = hold([others], arrived[chunks][1:])
    total = mine.astype(jnp.float32) + swap(others).astype(jnp.float32)
    apart = 2
    while total.shape[0] > 1:
        kept, given = jnp.split(total, 2)
        pairs = [(r, r ^ apart) for r in range(n_row)]
        total = kept + lax.ppermute(given.astype(jnp.bfloat16), "row", pairs).astype(jnp.float32)
        apart *= 2
    total = (total + tokens[-2][0, 0]).astype(jnp.bfloat16).reshape(n_col, blk, width)
    total = lax.all_to_all(total, "col", split_axis=0, concat_axis=0, tiled=True)
    total = jnp.sum(total.reshape(heads, groups, blk, width).astype(jnp.float32), axis=1)
    bias_grad = jnp.transpose(total, (0, 2, 1))
    d_query, d_key, d_value, d_gate = (x.reshape(rows, blk, channels) for x in grads)
    return d_query, d_key, d_value, d_gate, bias_grad


def solution(mesh):
    pair = P("row", "col", None)
    return jax.shard_map(
        functools.partial(on_device, mesh.shape["row"], mesh.shape["col"]),
        mesh=mesh,
        in_specs=(pair, pair, pair, pair, pair, P(None, "col", None), P()),
        out_specs=(pair, pair, pair, pair, P(None, "row", "col")),
        check_vma=False,
    )
```

```python
import functools
import itertools

import jax
import jax.numpy as jnp
from jax import lax
from jax.experimental import pallas as pl
from jax.experimental.pallas import tpu as pltpu
from jax.sharding import PartitionSpec as P

LOG2E = 1.4426950408889634
MASKED = -1e30
SHARES = (1, 3, 2, 2, 2, 1, 1)
INWARD = ((0,), (1,), (2, 3), (4, 5, 6))
OUTWARD = ((0, 1, 2), (3, 4, 5, 6))
PIECES = 4


def dot(a, b, dims):
    return lax.dot_general(a, b, (dims, ((), ())), preferred_element_type=jnp.float32)


def peer_of(me, step):
    return jnp.bitwise_xor(me, step)


def pack_kernel(heads, groups, with_bias, info, q_ref, k_ref, v_ref, g_ref, o_ref, *refs):
    n_col = heads * groups
    outs, turned = refs[-1 - n_col : -1], refs[-1]
    me = info[1]
    count, _, channels = q_ref.shape[1:]
    c = channels // heads
    lines = count * PIECES * c
    for i in range(count):
        for g in range(groups):
            gated = o_ref[g, i].astype(jnp.float32) * jax.nn.sigmoid(g_ref[g, i].astype(jnp.float32))
            pieces = (q_ref[g, i], k_ref[g, i], v_ref[g, i], gated.astype(jnp.bfloat16))
            for piece, x in enumerate(pieces):
                turned[g, i, piece] = x.T
        for step in range(n_col):
            peer = peer_of(me, step)
            head = pl.multiple_of(peer // groups * c, c)
            base = outs[step].shape[0] - lines
            for piece in range(PIECES):
                at = base + (i * PIECES + piece) * c
                outs[step][at : at + c, :] = turned[peer % groups, i, piece, pl.ds(head, c), :]
    if with_bias:
        for step in range(n_col):
            base = outs[step].shape[0] - lines
            keys = pl.ds(pl.multiple_of(info[2] * base, base), base) if step else slice(None)
            outs[step][:base, :] = refs[0][peer_of(me, step) // groups, :, keys].T


def unpack_kernel(heads, groups, info, g_ref, o_ref, *refs):
    n_col = heads * groups
    ins, (dq, dk, dv, dg, token, whole) = refs[:n_col], refs[-6:]
    token[...] = jnp.zeros_like(token)
    me = info[1]
    count, _, channels = g_ref.shape[1:]
    c = channels // heads
    for i in range(count):
        for step in range(n_col):
            peer = peer_of(me, step)
            head = pl.multiple_of(peer // groups * c, c)
            for piece in range(PIECES):
                at = (i * PIECES + piece) * c
                whole[peer % groups, i, piece, pl.ds(head, c), :] = ins[step][at : at + c, :]
        for g in range(groups):
            dq[g, i] = whole[g, i, 0].T
            dk[g, i] = whole[g, i, 1].T
            dv[g, i] = whole[g, i, 2].T
            attended = whole[g, i, 3].T.astype(jnp.float32)
            s = jax.nn.sigmoid(g_ref[g, i].astype(jnp.float32))
            dg[g, i] = (o_ref[g, i].astype(jnp.float32) * attended * s * (1.0 - s)).astype(jnp.bfloat16)


def reversed_bits(x, count):
    return sum((x // 2**bit % 2) * (count // 2 ** (bit + 1)) for bit in range(count.bit_length() - 1))


def woven(*queues):
    order = [(at / len(q), which, at) for which, q in enumerate(queues) for at in range(len(q))]
    for _, which, at in sorted(order):
        queues[which][at]()


def attention_kernel(n_col, together, c, scaling, first, last, info, *refs):
    bias_in, ins, refs = refs[: 2 * n_col - 1], refs[2 * n_col - 1 : 3 * n_col - 1], refs[3 * n_col - 1 :]
    scratch, refs = refs[-14:], refs[:-14]
    bias, total_s, q_s, g_s, k_s, v_s, k_turned, v_turned, dq_s, at_s, dkv, logits, weights, grads = scratch
    if not first:
        total_in = refs[0]
    totals = refs[-2:] if last else refs[-1:]
    outs, total_out = refs[-n_col - len(totals) : -len(totals)], totals[0]
    total = total_s if last else total_out
    length, me, side, level = info[0], info[1], info[2], info[3]
    blk = ins[0].shape[1]
    n = n_col * blk
    tile = min(256, n)
    tiles = range(0, n, tile)
    deep = k_s.shape[1]
    some = range(together)

    @pl.when(pl.program_id(0) == 0)
    def _():
        half = n // 2
        bias[me] = bias_in[0][...].astype(jnp.float32) * LOG2E
        for step in range(1, n_col):
            for table, which in ((bias_in[step], side), (bias_in[n_col + step - 1], 1 - side)):
                keys = pl.ds(pl.multiple_of(which * half, half), half)
                bias[peer_of(me, step), keys, :] = table[...].astype(jnp.float32) * LOG2E
        if first:
            total[...] = jnp.zeros_like(total)
        else:
            total[...] = total_in[...]
        rows = lax.broadcasted_iota(jnp.int32, (deep - 2 * c, n), 0)
        keys = lax.broadcasted_iota(jnp.int32, (deep - 2 * c, n), 1)
        mask = jnp.logical_and(rows == 0, keys >= length)
        for r in some:
            k_s[r, 2 * c :, :] = jnp.where(mask, MASKED, 0.0).astype(jnp.bfloat16)
            v_s[r, c:, :] = jnp.ones((deep - c, n), jnp.bfloat16)
            q_s[r, :, 2 * c :, :] = jnp.ones((n_col, deep - 2 * c, blk), jnp.bfloat16)

    def rows_of(r, piece):
        at = (r * PIECES + piece) * c
        return slice(at, at + c)

    for r in some:
        for step in range(n_col):
            jb = peer_of(me, step)
            span = pl.ds(pl.multiple_of(jb * blk, blk), blk)
            q = ins[step][rows_of(r, 0), :].astype(jnp.float32) * (scaling * LOG2E)
            high = q.astype(jnp.bfloat16)
            q_s[r, jb, :c, :] = high
            q_s[r, jb, c : 2 * c, :] = (q - high.astype(jnp.float32)).astype(jnp.bfloat16)
            k = ins[step][rows_of(r, 1), :]
            k_s[r, :c, span] = k
            k_s[r, c : 2 * c, span] = k
            v_s[r, :c, span] = ins[step][rows_of(r, 2), :]
            g_s[r, jb] = ins[step][rows_of(r, 3), :]
    for r in some:
        k_turned[r] = k_s[r].T
        v_turned[r] = v_s[r].T
    tops, scaled, scales = {}, {}, {}

    def score(jb, r, t):
        part = dot(k_turned[r, t : t + tile, :], q_s[r, jb], ((1,), (0,))) + bias[jb, t : t + tile, :]
        logits[jb % 2, r, t : t + tile, :] = part
        top = jnp.max(part.reshape(tile // 8, 8, blk), axis=0)
        tops[jb, r] = jnp.maximum(tops[jb, r], top) if t else top

    def expand(jb, r, t):
        if t == 0:
            tops[jb, r] = jnp.max(tops[jb, r], axis=0, keepdims=True)
        part = jnp.exp2(logits[jb % 2, r, t : t + tile, :] - tops[jb, r])
        weights[jb % 2, r, t : t + tile, :] = part.astype(jnp.bfloat16)

    def attend(jb, r):
        summed = dot(v_s[r, : c + 16, :], weights[jb % 2, r], ((1,), (0,)))
        inverse = 1.0 / summed[c : c + 1, :]
        attended = summed[:c, :] * inverse
        at_s[r, jb] = attended.astype(jnp.bfloat16)
        g = g_s[r, jb].astype(jnp.float32)
        row_dot = jnp.sum(g * attended, axis=0, keepdims=True) * (-inverse)
        high = row_dot.astype(jnp.bfloat16).astype(jnp.float32)
        rows = lax.broadcasted_iota(jnp.int32, (deep - c, blk), 0)
        tail = jnp.where(rows == 0, high, jnp.where(rows == 1, row_dot - high, 0.0))
        scaled[jb, r] = (g * inverse).astype(jnp.bfloat16)
        scales[jb, r] = jnp.concatenate([scaled[jb, r], tail.astype(jnp.bfloat16)], axis=0)

    def back(jb, t):
        added = total[jb, t : t + tile, :]
        for r in some:
            grad = dot(v_turned[r, t : t + tile, :], scales[jb, r], ((1,), (0,)))
            grad = grad * weights[jb % 2, r, t : t + tile, :].astype(jnp.float32)
            added = added + grad
            grads[jb % 2, r, t : t + tile, :] = grad.astype(jnp.bfloat16)
        total[jb, t : t + tile, :] = added

    def query_grad(jb, r):
        dq_s[r, jb] = (dot(k_s[r, :c, :], grads[jb % 2, r], ((1,), (0,))) * scaling).astype(jnp.bfloat16)

    def add_to(at, r, jb, part):
        if jb:
            part = part + dkv[r, at : at + c, :]
        dkv[r, at : at + c, :] = part

    def key_grad(jb, r):
        add_to(0, r, jb, dot(q_s[r, jb, :c, :], grads[jb % 2, r], ((1,), (1,))))

    def value_grad(jb, r):
        add_to(c, r, jb, dot(scaled[jb, r], weights[jb % 2, r], ((1,), (1,))))

    def each(step, jb, *ranges):
        if not 0 <= jb < n_col:
            return []
        return [functools.partial(step, jb, *at) for at in itertools.product(*ranges)]

    def finish(jb):
        return each(value_grad, jb, some) + each(query_grad, jb, some) + each(key_grad, jb, some)

    woven(each(score, 0, some, tiles))
    for jb in range(n_col):
        woven(each(expand, jb, some, tiles), finish(jb - 1))
        woven(each(attend, jb, some), each(score, jb + 1, some, tiles[: len(tiles) // 2]))
        woven(each(back, jb, tiles), each(score, jb + 1, some, tiles[len(tiles) // 2 :]))
    woven(finish(n_col - 1))

    for r in some:
        for step in range(n_col):
            jb = peer_of(me, step)
            span = pl.ds(pl.multiple_of(jb * blk, blk), blk)
            outs[step][rows_of(r, 0), :] = dq_s[r, jb]
            outs[step][rows_of(r, 1), :] = (dkv[r, :c, span] * (1.0 / LOG2E)).astype(jnp.bfloat16)
            outs[step][rows_of(r, 2), :] = dkv[r, c:, span].astype(jnp.bfloat16)
            outs[step][rows_of(r, 3), :] = at_s[r, jb]

    if last:

        @pl.when(pl.program_id(0) == pl.num_programs(0) - 1)
        def _():
            mine, others = totals
            pairs, _, width = mine.shape
            for pair in range(pairs):
                at = 2 * pair * width
                both = total[at // blk, :, at % blk : at % blk + 2 * width].astype(jnp.bfloat16)
                even, odd = both[:, :width], both[:, width:]
                place = peer_of(level, reversed_bits(pair, pairs))
                mine[place] = jnp.where(side == 0, even, odd)
                others[place] = jnp.where(side == 0, odd, even)


def hold_kernel(*refs):
    pass


def params(mib):
    return pltpu.CompilerParams(
        dimension_semantics=("arbitrary",), vmem_limit_bytes=mib * 1024 * 1024
    )


def on_device(n_row, n_col, query, key, value, gate, d_out, bias, length):
    rows, blk, channels = query.shape
    heads, _, n = bias.shape
    c = channels // heads
    groups = n_col // heads
    share = rows // groups
    sizes = [share * weight // sum(SHARES) for weight in SHARES]
    starts = [sum(sizes[:m]) for m in range(len(sizes))]
    assert groups * heads == n_col and n == n_col * blk and groups * sum(sizes) == rows
    scaling = c ** (-0.5)
    per = 2 if all(size % 2 == 0 for size in sizes) else 1
    split_rows = (groups, share, blk, channels)
    query, key, value, gate, d_out = (x.reshape(split_rows) for x in (query, key, value, gate, d_out))
    row = lax.axis_index("row")
    level = reversed_bits(row // 2, n_row // 2)
    info = jnp.stack([length[0], lax.axis_index("col"), row % 2, level]).astype(jnp.int32)
    width = n // n_row
    lines = PIECES * c
    chunks = len(sizes)

    untouched = pl.BlockSpec(memory_space=pl.ANY)

    def exchange(blocks):
        pairs = [[(a, a ^ step) for a in range(n_col)] for step in range(n_col)]
        return [blocks[0]] + [lax.ppermute(blocks[step], "col", pairs[step]) for step in range(1, n_col)]

    def swap(x):
        return lax.ppermute(x, "row", [(r, r ^ 1) for r in range(n_row)])

    def hold(blocks, until):
        count = len(blocks)
        return pl.pallas_call(
            hold_kernel,
            in_specs=[untouched] * (count + len(until)),
            out_specs=[untouched] * count,
            out_shape=[jax.ShapeDtypeStruct(x.shape, x.dtype) for x in blocks],
            input_output_aliases={a: a for a in range(count)},
            name="hold",
        )(*blocks, *until)

    def call(kernel, name, flops, grid, operands, out_specs, out_shape, scratch, aliases):
        return pl.pallas_call(
            kernel,
            grid_spec=pltpu.PrefetchScalarGridSpec(
                num_scalar_prefetch=1,
                grid=(grid,),
                in_specs=[spec for spec, _ in operands],
                out_specs=out_specs,
                scratch_shapes=scratch,
            ),
            out_shape=out_shape,
            input_output_aliases=aliases,
            compiler_params=params({"pack": 60, "attend": 34, "unpack": 24}[name]),
            cost_estimate=pl.CostEstimate(flops=flops, bytes_accessed=1, transcendentals=0),
            name=name,
        )(info, *[x for _, x in operands])

    def still(*shape):
        return pl.BlockSpec(shape, lambda i, info: (0,) * len(shape), pipeline_mode=pl.Buffered(1))

    def part(size, skip):
        return pl.BlockSpec((size, blk), lambda i, info: (skip + i, 0))

    def rows_a_step(*counts):
        return max(step for step in range(1, 5) if all(count % step == 0 for count in counts))

    def rows_of(group):
        return starts[group[0]], sum(sizes[m] for m in group)

    def pack(group):
        with_bias = group[0] == 0
        start, count = rows_of(group)
        step = rows_a_step(start, count)
        assert not with_bias or step == count
        base = start // step
        whole = pl.BlockSpec((groups, step, blk, channels), lambda i, info: (0, base + i, 0, 0))
        ahead = [n] + [n // 2] * (n_col - 1) if with_bias else [0] * n_col
        size = count * lines
        operands = [(whole, x) for x in (query, key, value, gate, d_out)]
        if with_bias:
            operands.append((still(heads, blk, n), bias))
        return call(
            functools.partial(pack_kernel, heads, groups, with_bias),
            "pack",
            count * 10**6,
            count // step,
            operands,
            [part(x + step * lines, 0) for x in ahead],
            [jax.ShapeDtypeStruct((x + size, blk), jnp.bfloat16) for x in ahead],
            [pltpu.VMEM((groups, step, PIECES, channels, blk), jnp.bfloat16)],
            {},
        )

    def attend(m, total, bias_blocks, blocks, room):
        first, last = m == 0, m == chunks - 1

        def scratch(*shape, dtype=jnp.bfloat16):
            return pltpu.VMEM((per, *shape), dtype)

        operands = [(still(n if a == 0 else n // 2, blk), x) for a, x in enumerate(bias_blocks)]
        (inward,) = [group for group in INWARD if m in group]
        (outward,) = [group for group in OUTWARD if m in group]
        behind = sum(sizes[o] for o in inward if o < m) // per
        ahead = sum(sizes[o] for o in outward if o < m) // per
        for a, x in enumerate(blocks):
            skip = (n if a == 0 else n // 2) // (per * lines) if first else behind
            operands.append((part(per * lines, skip), x))
        square = (n_col, n, blk)
        if not first:
            operands.append((still(*square), total))
        aliases = {}
        if ahead:
            aliases = {1 + len(operands) + a: a for a in range(n_col)}
            operands += [(untouched, x) for x in room]
        size = rows_of(outward)[1]
        out_shape = [jax.ShapeDtypeStruct((size * lines, blk), jnp.bfloat16)] * n_col
        if last:
            totals = [jax.ShapeDtypeStruct((n_row // 2, n, width), jnp.bfloat16)] * 2
        else:
            totals = [jax.ShapeDtypeStruct(square, jnp.float32)]
        deep = 4 * c
        result = call(
            functools.partial(attention_kernel, n_col, per, c, scaling, first, last),
            "attend",
            sizes[m] * 4 * 10**9,
            sizes[m] // per,
            operands,
            [part(per * lines, ahead)] * n_col + [still(*x.shape) for x in totals],
            out_shape + totals,
            [
                pltpu.VMEM(square, jnp.float32),
                pltpu.VMEM(square if last else (8, 128), jnp.float32),
                scratch(n_col, deep, blk),
                scratch(n_col, c, blk),
                scratch(deep, n),
                scratch(deep, n),
                scratch(n, deep),
                scratch(n, deep),
                scratch(n_col, c, blk),
                scratch(n_col, c, blk),
                scratch(2 * c, n, dtype=jnp.float32),
                pltpu.VMEM((2, per, n, blk), jnp.float32),
                pltpu.VMEM((2, per, n, blk), jnp.bfloat16),
                pltpu.VMEM((2, per, n, blk), jnp.bfloat16),
            ],
            aliases,
        )
        return result[:n_col], result[n_col:]

    def unpack(group, blocks, grads):
        start, count = rows_of(group)
        step = rows_a_step(start, count)
        base = start // step
        whole = pl.BlockSpec((groups, step, blk, channels), lambda i, info: (0, base + i, 0, 0))
        kept = [] if grads is None else list(grads)
        operands = [(whole, gate), (whole, d_out)]
        operands += [(part(step * lines, 0), x) for x in blocks]
        aliases = {1 + len(operands) + a: a for a in range(len(kept))}
        operands += [(untouched, x) for x in kept]
        return call(
            functools.partial(unpack_kernel, heads, groups),
            "unpack",
            1,
            count // step,
            operands,
            [whole] * 4 + [pl.BlockSpec((8, 128), lambda i, info: (0, 0))],
            [jax.ShapeDtypeStruct(query.shape, jnp.bfloat16)] * 4
            + [jax.ShapeDtypeStruct((8, 128), jnp.float32)],
            [pltpu.VMEM((groups, step, PIECES, channels, blk), jnp.bfloat16)],
            aliases,
        )

    packed = [pack(group) for group in INWARD]
    own, *fetched = exchange(packed[0])
    fetched = hold(fetched, [x[0] for x in packed[1:]])
    tables = [own, *fetched] + [swap(x) for x in fetched]
    arrived = [[own, *fetched]]
    for blocks in packed[1:]:
        arrived.append(exchange([blocks[0], *hold(blocks[1:], arrived[-1][1:])]))
    blocks_of = {m: blocks for group, blocks in zip(INWARD, arrived) for m in group}

    totals, results, sent = [None], None, []
    for m in range(chunks):
        if m == chunks - 1:
            totals = hold(totals, sent[0][1:])
        results, totals = attend(m, totals[0], tables, blocks_of[m], results)
        if m in [group[-1] for group in OUTWARD]:
            sent.append(exchange(results))
    grads, tokens = None, []
    for group, blocks in zip(OUTWARD, sent):
        *grads, token = unpack(group, blocks, grads)
        tokens.append(token)

    mine, others = totals
    total = mine.astype(jnp.float32) + swap(others).astype(jnp.float32)
    apart = 2
    while total.shape[0] > 1:
        kept, given = jnp.split(total, 2)
        given = given.astype(jnp.bfloat16)
        given = lax.ppermute(given, "row", [(r, r ^ apart) for r in range(n_row)])
        total = kept + given.astype(jnp.float32)
        apart *= 2
    total = (total + tokens[-2][0, 0]).astype(jnp.bfloat16).reshape(n_col, blk, width)
    total = lax.all_to_all(total, "col", split_axis=0, concat_axis=0, tiled=True)
    total = jnp.sum(total.reshape(heads, groups, blk, width).astype(jnp.float32), axis=1)
    bias_grad = jnp.transpose(total, (0, 2, 1))
    d_query, d_key, d_value, d_gate = (x.reshape(rows, blk, channels) for x in grads)
    return d_query, d_key, d_value, d_gate, bias_grad


def solution(mesh):
    pair = P("row", "col", None)
    return jax.shard_map(
        functools.partial(on_device, mesh.shape["row"], mesh.shape["col"]),
        mesh=mesh,
        in_specs=(pair, pair, pair, pair, pair, P(None, "col", None), P()),
        out_specs=(pair, pair, pair, pair, P(None, "row", "col")),
        check_vma=False,
    )
```

```python
import functools
import itertools

import jax
import jax.numpy as jnp
from jax import lax
from jax.experimental import pallas as pl
from jax.experimental.pallas import tpu as pltpu
from jax.sharding import PartitionSpec as P

LOG2E = 1.4426950408889634
MASKED = -1e30
SHARES = (1, 3, 2, 2, 2, 1, 1)
INWARD = ((0,), (1,), (2, 3), (4, 5, 6))
OUTWARD = ((0, 1, 2), (3, 4, 5, 6))
PIECES = 4


def dot(a, b, dims):
    return lax.dot_general(a, b, (dims, ((), ())), preferred_element_type=jnp.float32)


def peer_of(me, step):
    return jnp.bitwise_xor(me, step)


def pack_kernel(heads, groups, with_bias, info, q_ref, k_ref, v_ref, g_ref, o_ref, *refs):
    n_col = heads * groups
    outs, turned = refs[-1 - n_col : -1], refs[-1]
    me = info[1]
    count, _, channels = q_ref.shape[1:]
    c = channels // heads
    lines = count * PIECES * c
    for i in range(count):
        for g in range(groups):
            gated = o_ref[g, i].astype(jnp.float32) * jax.nn.sigmoid(g_ref[g, i].astype(jnp.float32))
            pieces = (q_ref[g, i], k_ref[g, i], v_ref[g, i], gated.astype(jnp.bfloat16))
            for piece, x in enumerate(pieces):
                turned[g, i, piece] = x.T
        for step in range(n_col):
            peer = peer_of(me, step)
            head = pl.multiple_of(peer // groups * c, c)
            base = outs[step].shape[0] - lines
            for piece in range(PIECES):
                at = base + (i * PIECES + piece) * c
                outs[step][at : at + c, :] = turned[peer % groups, i, piece, pl.ds(head, c), :]
    if with_bias:
        for step in range(n_col):
            base = outs[step].shape[0] - lines
            keys = pl.ds(pl.multiple_of(info[2] * base, base), base) if step else slice(None)
            outs[step][:base, :] = refs[0][peer_of(me, step) // groups, :, keys].T


def unpack_kernel(heads, groups, info, g_ref, o_ref, *refs):
    n_col = heads * groups
    ins, (dq, dk, dv, dg, token, whole) = refs[:n_col], refs[-6:]
    token[...] = jnp.zeros_like(token)
    me = info[1]
    count, _, channels = g_ref.shape[1:]
    c = channels // heads
    for i in range(count):
        for step in range(n_col):
            peer = peer_of(me, step)
            head = pl.multiple_of(peer // groups * c, c)
            for piece in range(PIECES):
                at = (i * PIECES + piece) * c
                whole[peer % groups, i, piece, pl.ds(head, c), :] = ins[step][at : at + c, :]
        for g in range(groups):
            dq[g, i] = whole[g, i, 0].T
            dk[g, i] = whole[g, i, 1].T
            dv[g, i] = whole[g, i, 2].T
            attended = whole[g, i, 3].T.astype(jnp.float32)
            s = jax.nn.sigmoid(g_ref[g, i].astype(jnp.float32))
            dg[g, i] = (o_ref[g, i].astype(jnp.float32) * attended * s * (1.0 - s)).astype(jnp.bfloat16)


def reversed_bits(x, count):
    return sum((x // 2**bit % 2) * (count // 2 ** (bit + 1)) for bit in range(count.bit_length() - 1))


def woven(*queues):
    order = [(at / len(q), which, at) for which, q in enumerate(queues) for at in range(len(q))]
    for _, which, at in sorted(order):
        queues[which][at]()


def attention_kernel(n_col, together, c, scaling, first, last, info, *refs):
    bias_in, ins, refs = refs[: 2 * n_col - 1], refs[2 * n_col - 1 : 3 * n_col - 1], refs[3 * n_col - 1 :]
    scratch, refs = refs[-15:], refs[:-15]
    bias, total, q_s, g_s, k_s, v_s, k_turned, v_turned, dq_s, at_s, dkv, logits, weights, grads, sem = scratch
    if not first:
        total_in = refs[0]
    *totals, token = refs[-3:] if last else refs[-2:]
    outs = refs[-n_col - len(totals) - 1 : -len(totals) - 1]
    length, me, side, level = info[0], info[1], info[2], info[3]
    blk = ins[0].shape[1]
    n = n_col * blk
    tile = min(256, n)
    tiles = range(0, n, tile)
    deep = k_s.shape[1]
    some = range(together)

    @pl.when(pl.program_id(0) == 0)
    def _():
        token[...] = jnp.zeros_like(token)
        if first:
            total[...] = jnp.zeros_like(total)
        else:
            fetch = pltpu.make_async_copy(total_in, total, sem)
            fetch.start()
        half = n // 2
        bias[me] = bias_in[0][...].astype(jnp.float32) * LOG2E
        for step in range(1, n_col):
            for table, which in ((bias_in[step], side), (bias_in[n_col + step - 1], 1 - side)):
                keys = pl.ds(pl.multiple_of(which * half, half), half)
                bias[peer_of(me, step), keys, :] = table[...].astype(jnp.float32) * LOG2E
        rows = lax.broadcasted_iota(jnp.int32, (deep - 2 * c, n), 0)
        keys = lax.broadcasted_iota(jnp.int32, (deep - 2 * c, n), 1)
        mask = jnp.logical_and(rows == 0, keys >= length)
        for r in some:
            k_s[r, 2 * c :, :] = jnp.where(mask, MASKED, 0.0).astype(jnp.bfloat16)
            v_s[r, c:, :] = jnp.ones((deep - c, n), jnp.bfloat16)
            q_s[r, :, 2 * c :, :] = jnp.ones((n_col, deep - 2 * c, blk), jnp.bfloat16)
        if not first:
            fetch.wait()

    def rows_of(r, piece):
        at = (r * PIECES + piece) * c
        return slice(at, at + c)

    for r in some:
        for step in range(n_col):
            jb = peer_of(me, step)
            span = pl.ds(pl.multiple_of(jb * blk, blk), blk)
            q = ins[step][rows_of(r, 0), :].astype(jnp.float32) * (scaling * LOG2E)
            high = q.astype(jnp.bfloat16)
            q_s[r, jb, :c, :] = high
            q_s[r, jb, c : 2 * c, :] = (q - high.astype(jnp.float32)).astype(jnp.bfloat16)
            k = ins[step][rows_of(r, 1), :]
            k_s[r, :c, span] = k
            k_s[r, c : 2 * c, span] = k
            v_s[r, :c, span] = ins[step][rows_of(r, 2), :]
            g_s[r, jb] = ins[step][rows_of(r, 3), :]
    for r in some:
        k_turned[r] = k_s[r].T
        v_turned[r] = v_s[r].T
    tops, scaled, scales = {}, {}, {}

    def score(jb, r, t):
        part = dot(k_turned[r, t : t + tile, :], q_s[r, jb], ((1,), (0,))) + bias[jb, t : t + tile, :]
        logits[jb % 2, r, t : t + tile, :] = part
        top = jnp.max(part.reshape(tile // 8, 8, blk), axis=0)
        tops[jb, r] = jnp.maximum(tops[jb, r], top) if t else top

    def expand(jb, r, t):
        if t == 0:
            tops[jb, r] = jnp.max(tops[jb, r], axis=0, keepdims=True)
        part = jnp.exp2(logits[jb % 2, r, t : t + tile, :] - tops[jb, r])
        weights[jb % 2, r, t : t + tile, :] = part.astype(jnp.bfloat16)

    def attend(jb, r):
        summed = dot(v_s[r, : c + 16, :], weights[jb % 2, r], ((1,), (0,)))
        inverse = 1.0 / summed[c : c + 1, :]
        attended = summed[:c, :] * inverse
        at_s[r, jb] = attended.astype(jnp.bfloat16)
        g = g_s[r, jb].astype(jnp.float32)
        row_dot = jnp.sum(g * attended, axis=0, keepdims=True) * (-inverse)
        high = row_dot.astype(jnp.bfloat16).astype(jnp.float32)
        rows = lax.broadcasted_iota(jnp.int32, (deep - c, blk), 0)
        tail = jnp.where(rows == 0, high, jnp.where(rows == 1, row_dot - high, 0.0))
        scaled[jb, r] = (g * inverse).astype(jnp.bfloat16)
        scales[jb, r] = jnp.concatenate([scaled[jb, r], tail.astype(jnp.bfloat16)], axis=0)

    def back(jb, t):
        added = total[jb, t : t + tile, :]
        for r in some:
            grad = dot(v_turned[r, t : t + tile, :], scales[jb, r], ((1,), (0,)))
            grad = grad * weights[jb % 2, r, t : t + tile, :].astype(jnp.float32)
            added = added + grad
            grads[jb % 2, r, t : t + tile, :] = grad.astype(jnp.bfloat16)
        total[jb, t : t + tile, :] = added

    def query_grad(jb, r):
        dq_s[r, jb] = (dot(k_s[r, :c, :], grads[jb % 2, r], ((1,), (0,))) * scaling).astype(jnp.bfloat16)

    def add_to(at, r, jb, part):
        if jb:
            part = part + dkv[r, at : at + c, :]
        dkv[r, at : at + c, :] = part

    def key_grad(jb, r):
        add_to(0, r, jb, dot(q_s[r, jb, :c, :], grads[jb % 2, r], ((1,), (1,))))

    def value_grad(jb, r):
        add_to(c, r, jb, dot(scaled[jb, r], weights[jb % 2, r], ((1,), (1,))))

    def each(step, jb, *ranges):
        if not 0 <= jb < n_col:
            return []
        return [functools.partial(step, jb, *at) for at in itertools.product(*ranges)]

    def finish(jb):
        return each(value_grad, jb, some) + each(query_grad, jb, some) + each(key_grad, jb, some)

    woven(each(score, 0, some, tiles))
    for jb in range(n_col):
        woven(each(expand, jb, some, tiles), finish(jb - 1))
        woven(each(attend, jb, some), each(score, jb + 1, some, tiles[: len(tiles) // 2]))
        woven(each(back, jb, tiles), each(score, jb + 1, some, tiles[len(tiles) // 2 :]))
    woven(finish(n_col - 1))

    for r in some:
        for step in range(n_col):
            jb = peer_of(me, step)
            span = pl.ds(pl.multiple_of(jb * blk, blk), blk)
            outs[step][rows_of(r, 0), :] = dq_s[r, jb]
            outs[step][rows_of(r, 1), :] = (dkv[r, :c, span] * (1.0 / LOG2E)).astype(jnp.bfloat16)
            outs[step][rows_of(r, 2), :] = dkv[r, c:, span].astype(jnp.bfloat16)
            outs[step][rows_of(r, 3), :] = at_s[r, jb]

    @pl.when(pl.program_id(0) == pl.num_programs(0) - 1)
    def _():
        if not last:
            keep = pltpu.make_async_copy(total, totals[0], sem)
            keep.start()
            keep.wait()
        else:
            mine, others = totals
            pairs, _, width = mine.shape
            for pair in range(pairs):
                at = 2 * pair * width
                both = total[at // blk, :, at % blk : at % blk + 2 * width].astype(jnp.bfloat16)
                even, odd = both[:, :width], both[:, width:]
                place = peer_of(level, reversed_bits(pair, pairs))
                mine[place] = jnp.where(side == 0, even, odd)
                others[place] = jnp.where(side == 0, odd, even)


def hold_kernel(*refs):
    pass


def params(mib):
    return pltpu.CompilerParams(
        dimension_semantics=("arbitrary",), vmem_limit_bytes=mib * 1024 * 1024
    )


def on_device(n_row, n_col, query, key, value, gate, d_out, bias, length):
    rows, blk, channels = query.shape
    heads, _, n = bias.shape
    c = channels // heads
    groups = n_col // heads
    share = rows // groups
    sizes = [share * weight // sum(SHARES) for weight in SHARES]
    starts = [sum(sizes[:m]) for m in range(len(sizes))]
    assert groups * heads == n_col and n == n_col * blk and groups * sum(sizes) == rows
    scaling = c ** (-0.5)
    per = 2 if all(size % 2 == 0 for size in sizes) else 1
    split_rows = (groups, share, blk, channels)
    query, key, value, gate, d_out = (x.reshape(split_rows) for x in (query, key, value, gate, d_out))
    row = lax.axis_index("row")
    level = reversed_bits(row // 2, n_row // 2)
    info = jnp.stack([length[0], lax.axis_index("col"), row % 2, level]).astype(jnp.int32)
    width = n // n_row
    lines = PIECES * c
    chunks = len(sizes)

    untouched = pl.BlockSpec(memory_space=pl.ANY)

    def exchange(blocks):
        pairs = [[(a, a ^ step) for a in range(n_col)] for step in range(n_col)]
        return [blocks[0]] + [lax.ppermute(blocks[step], "col", pairs[step]) for step in range(1, n_col)]

    def swap(x):
        return lax.ppermute(x, "row", [(r, r ^ 1) for r in range(n_row)])

    def hold(blocks, until):
        count = len(blocks)
        return pl.pallas_call(
            hold_kernel,
            in_specs=[untouched] * (count + len(until)),
            out_specs=[untouched] * count,
            out_shape=[jax.ShapeDtypeStruct(x.shape, x.dtype) for x in blocks],
            input_output_aliases={a: a for a in range(count)},
            name="hold",
        )(*blocks, *until)

    def call(kernel, name, flops, grid, operands, out_specs, out_shape, scratch, aliases):
        return pl.pallas_call(
            kernel,
            grid_spec=pltpu.PrefetchScalarGridSpec(
                num_scalar_prefetch=1,
                grid=(grid,),
                in_specs=[spec for spec, _ in operands],
                out_specs=out_specs,
                scratch_shapes=scratch,
            ),
            out_shape=out_shape,
            input_output_aliases=aliases,
            compiler_params=params({"pack": 60, "attend": 28, "unpack": 24}[name]),
            cost_estimate=pl.CostEstimate(flops=flops, bytes_accessed=1, transcendentals=0),
            name=name,
        )(info, *[x for _, x in operands])

    def still(*shape):
        return pl.BlockSpec(shape, lambda i, info: (0,) * len(shape), pipeline_mode=pl.Buffered(1))

    def part(size, skip):
        return pl.BlockSpec((size, blk), lambda i, info: (skip + i, 0))

    def rows_a_step(*counts):
        return max(step for step in range(1, 5) if all(count % step == 0 for count in counts))

    def rows_of(group):
        return starts[group[0]], sum(sizes[m] for m in group)

    def pack(group):
        with_bias = group[0] == 0
        start, count = rows_of(group)
        step = rows_a_step(start, count)
        assert not with_bias or step == count
        base = start // step
        whole = pl.BlockSpec((groups, step, blk, channels), lambda i, info: (0, base + i, 0, 0))
        ahead = [n] + [n // 2] * (n_col - 1) if with_bias else [0] * n_col
        size = count * lines
        operands = [(whole, x) for x in (query, key, value, gate, d_out)]
        if with_bias:
            operands.append((still(heads, blk, n), bias))
        return call(
            functools.partial(pack_kernel, heads, groups, with_bias),
            "pack",
            count * 10**6,
            count // step,
            operands,
            [part(x + step * lines, 0) for x in ahead],
            [jax.ShapeDtypeStruct((x + size, blk), jnp.bfloat16) for x in ahead],
            [pltpu.VMEM((groups, step, PIECES, channels, blk), jnp.bfloat16)],
            {},
        )

    def attend(m, total, bias_blocks, blocks, room):
        first, last = m == 0, m == chunks - 1

        def scratch(*shape, dtype=jnp.bfloat16):
            return pltpu.VMEM((per, *shape), dtype)

        operands = [(still(n if a == 0 else n // 2, blk), x) for a, x in enumerate(bias_blocks)]
        (inward,) = [group for group in INWARD if m in group]
        (outward,) = [group for group in OUTWARD if m in group]
        behind = sum(sizes[o] for o in inward if o < m) // per
        ahead = sum(sizes[o] for o in outward if o < m) // per
        for a, x in enumerate(blocks):
            skip = (n if a == 0 else n // 2) // (per * lines) if first else behind
            operands.append((part(per * lines, skip), x))
        square = (n_col, n, blk)
        aliases = {}
        if not first:
            if not last:
                aliases[1 + len(operands)] = n_col
            operands.append((untouched, total))
        if ahead:
            aliases |= {1 + len(operands) + a: a for a in range(n_col)}
            operands += [(untouched, x) for x in room]
        size = rows_of(outward)[1]
        out_shape = [jax.ShapeDtypeStruct((size * lines, blk), jnp.bfloat16)] * n_col
        if last:
            totals = [jax.ShapeDtypeStruct((n_row // 2, n, width), jnp.bfloat16)] * 2
        else:
            totals = [jax.ShapeDtypeStruct(square, jnp.float32)]
        deep = 4 * c
        result = call(
            functools.partial(attention_kernel, n_col, per, c, scaling, first, last),
            "attend",
            sizes[m] * 4 * 10**9,
            sizes[m] // per,
            operands,
            [part(per * lines, ahead)] * n_col
            + ([still(*x.shape) for x in totals] if last else [untouched])
            + [still(8, 128)],
            out_shape + totals + [jax.ShapeDtypeStruct((8, 128), jnp.float32)],
            [
                pltpu.VMEM(square, jnp.float32),
                pltpu.VMEM(square, jnp.float32),
                scratch(n_col, deep, blk),
                scratch(n_col, c, blk),
                scratch(deep, n),
                scratch(deep, n),
                scratch(n, deep),
                scratch(n, deep),
                scratch(n_col, c, blk),
                scratch(n_col, c, blk),
                scratch(2 * c, n, dtype=jnp.float32),
                pltpu.VMEM((2, per, n, blk), jnp.float32),
                pltpu.VMEM((2, per, n, blk), jnp.bfloat16),
                pltpu.VMEM((2, per, n, blk), jnp.bfloat16),
                pltpu.SemaphoreType.DMA,
            ],
            aliases,
        )
        return result[:n_col], result[n_col:-1], result[-1]

    def unpack(group, blocks, grads):
        start, count = rows_of(group)
        step = rows_a_step(start, count)
        base = start // step
        whole = pl.BlockSpec((groups, step, blk, channels), lambda i, info: (0, base + i, 0, 0))
        kept = [] if grads is None else list(grads)
        operands = [(whole, gate), (whole, d_out)]
        operands += [(part(step * lines, 0), x) for x in blocks]
        aliases = {1 + len(operands) + a: a for a in range(len(kept))}
        operands += [(untouched, x) for x in kept]
        return call(
            functools.partial(unpack_kernel, heads, groups),
            "unpack",
            1,
            count // step,
            operands,
            [whole] * 4 + [pl.BlockSpec((8, 128), lambda i, info: (0, 0))],
            [jax.ShapeDtypeStruct(query.shape, jnp.bfloat16)] * 4
            + [jax.ShapeDtypeStruct((8, 128), jnp.float32)],
            [pltpu.VMEM((groups, step, PIECES, channels, blk), jnp.bfloat16)],
            aliases,
        )

    packed = [pack(group) for group in INWARD]
    own, *fetched = exchange(packed[0])
    fetched = hold(fetched, [x[0] for x in packed[1:]])
    tables = [own, *fetched] + [swap(x) for x in fetched]
    arrived = {0: [own, *fetched]}

    totals, results, sent, done = [None], None, [], []
    for m in range(chunks):
        at = [m in group for group in INWARD].index(True)
        for ahead in range(at + 1, min(at + 2, len(INWARD) - 1) + 1):
            if ahead not in arrived and (ahead == 1 or m >= INWARD[ahead - 1][0]):
                until = arrived[ahead - 1][1:] + (done[m - 1 : m] if m else [])
                arrived[ahead] = exchange([packed[ahead][0], *hold(packed[ahead][1:], until)])
        if m == chunks - 1:
            totals = hold(totals, sent[0][1:])
        results, totals, token = attend(m, totals[0], tables, arrived[at], results)
        done.append(token)
        if m in [group[-1] for group in OUTWARD]:
            sent.append(exchange(results))
    grads, tokens = None, []
    for group, blocks in zip(OUTWARD, sent):
        *grads, token = unpack(group, blocks, grads)
        tokens.append(token)

    mine, others = totals
    total = mine.astype(jnp.float32) + swap(others).astype(jnp.float32)
    apart = 2
    while total.shape[0] > 1:
        kept, given = jnp.split(total, 2)
        given = given.astype(jnp.bfloat16)
        given = lax.ppermute(given, "row", [(r, r ^ apart) for r in range(n_row)])
        total = kept + given.astype(jnp.float32)
        apart *= 2
    total = (total + tokens[-2][0, 0]).astype(jnp.bfloat16).reshape(n_col, blk, width)
    total = lax.all_to_all(total, "col", split_axis=0, concat_axis=0, tiled=True)
    total = jnp.sum(total.reshape(heads, groups, blk, width).astype(jnp.float32), axis=1)
    bias_grad = jnp.transpose(total, (0, 2, 1))
    d_query, d_key, d_value, d_gate = (x.reshape(rows, blk, channels) for x in grads)
    return d_query, d_key, d_value, d_gate, bias_grad


def solution(mesh):
    pair = P("row", "col", None)
    return jax.shard_map(
        functools.partial(on_device, mesh.shape["row"], mesh.shape["col"]),
        mesh=mesh,
        in_specs=(pair, pair, pair, pair, pair, P(None, "col", None), P()),
        out_specs=(pair, pair, pair, pair, P(None, "row", "col")),
        check_vma=False,
    )
```

```python
import functools
import itertools

import jax
import jax.numpy as jnp
from jax import lax
from jax.experimental import pallas as pl
from jax.experimental.pallas import tpu as pltpu
from jax.sharding import PartitionSpec as P

LOG2E = 1.4426950408889634
MASKED = -1e30
SHARES = (1, 3, 2, 2, 2, 1, 1)
INWARD = ((0,), (1,), (2, 3), (4, 5, 6))
OUTWARD = ((0, 1, 2), (3, 4, 5, 6))
PIECES = 4


def dot(a, b, dims):
    return lax.dot_general(a, b, (dims, ((), ())), preferred_element_type=jnp.float32)


def peer_of(me, step):
    return jnp.bitwise_xor(me, step)


def pack_kernel(heads, groups, with_bias, info, q_ref, k_ref, v_ref, g_ref, o_ref, *refs):
    n_col = heads * groups
    outs, turned = refs[-1 - n_col : -1], refs[-1]
    me = info[1]
    count, _, channels = q_ref.shape[1:]
    c = channels // heads
    lines = count * PIECES * c
    for i in range(count):
        for g in range(groups):
            gated = o_ref[g, i].astype(jnp.float32) * jax.nn.sigmoid(g_ref[g, i].astype(jnp.float32))
            pieces = (q_ref[g, i], k_ref[g, i], v_ref[g, i], gated.astype(jnp.bfloat16))
            for piece, x in enumerate(pieces):
                turned[g, i, piece] = x.T
        for step in range(n_col):
            peer = peer_of(me, step)
            head = pl.multiple_of(peer // groups * c, c)
            base = outs[step].shape[0] - lines
            for piece in range(PIECES):
                at = base + (i * PIECES + piece) * c
                outs[step][at : at + c, :] = turned[peer % groups, i, piece, pl.ds(head, c), :]
    if with_bias:
        for step in range(n_col):
            base = outs[step].shape[0] - lines
            keys = pl.ds(pl.multiple_of(info[2] * base, base), base) if step else slice(None)
            outs[step][:base, :] = refs[0][peer_of(me, step) // groups, :, keys].T


def unpack_kernel(heads, groups, info, g_ref, o_ref, *refs):
    n_col = heads * groups
    ins, (dq, dk, dv, dg, token, whole) = refs[:n_col], refs[-6:]
    token[...] = jnp.zeros_like(token)
    me = info[1]
    count, _, channels = g_ref.shape[1:]
    c = channels // heads
    for i in range(count):
        for step in range(n_col):
            peer = peer_of(me, step)
            head = pl.multiple_of(peer // groups * c, c)
            for piece in range(PIECES):
                at = (i * PIECES + piece) * c
                whole[peer % groups, i, piece, pl.ds(head, c), :] = ins[step][at : at + c, :]
        for g in range(groups):
            dq[g, i] = whole[g, i, 0].T
            dk[g, i] = whole[g, i, 1].T
            dv[g, i] = whole[g, i, 2].T
            attended = whole[g, i, 3].T.astype(jnp.float32)
            s = jax.nn.sigmoid(g_ref[g, i].astype(jnp.float32))
            dg[g, i] = (o_ref[g, i].astype(jnp.float32) * attended * s * (1.0 - s)).astype(jnp.bfloat16)


def reversed_bits(x, count):
    return sum((x // 2**bit % 2) * (count // 2 ** (bit + 1)) for bit in range(count.bit_length() - 1))


def woven(*queues):
    order = [(at / len(q), which, at) for which, q in enumerate(queues) for at in range(len(q))]
    for _, which, at in sorted(order):
        queues[which][at]()


def attention_kernel(n_col, together, c, scaling, first, last, info, *refs):
    bias_in, ins, refs = refs[: 2 * n_col - 1], refs[2 * n_col - 1 : 3 * n_col - 1], refs[3 * n_col - 1 :]
    scratch, refs = refs[-15:], refs[:-15]
    bias, total, q_s, g_s, k_s, v_s, k_turned, v_turned, dq_s, at_s, dkv, logits, weights, grads, sem = scratch
    if not first:
        total_in = refs[0]
    *totals, token = refs[-3:] if last else refs[-2:]
    outs = refs[-n_col - len(totals) - 1 : -len(totals) - 1]
    length, me, side, level = info[0], info[1], info[2], info[3]
    blk = ins[0].shape[1]
    n = n_col * blk
    tile = min(256, n)
    tiles = range(0, n, tile)
    deep = k_s.shape[1]
    some = range(together)

    @pl.when(pl.program_id(0) == 0)
    def _():
        token[...] = jnp.zeros_like(token)
        if first:
            total[...] = jnp.zeros_like(total)
        else:
            fetch = pltpu.make_async_copy(total_in, total, sem)
            fetch.start()
        half = n // 2
        bias[me] = bias_in[0][...].astype(jnp.float32) * LOG2E
        for step in range(1, n_col):
            for table, which in ((bias_in[step], side), (bias_in[n_col + step - 1], 1 - side)):
                keys = pl.ds(pl.multiple_of(which * half, half), half)
                bias[peer_of(me, step), keys, :] = table[...].astype(jnp.float32) * LOG2E
        rows = lax.broadcasted_iota(jnp.int32, (deep - 2 * c, n), 0)
        keys = lax.broadcasted_iota(jnp.int32, (deep - 2 * c, n), 1)
        mask = jnp.logical_and(rows == 0, keys >= length)
        for r in some:
            k_s[r, 2 * c :, :] = jnp.where(mask, MASKED, 0.0).astype(jnp.bfloat16)
            v_s[r, c:, :] = jnp.ones((deep - c, n), jnp.bfloat16)
            q_s[r, :, 2 * c :, :] = jnp.ones((n_col, deep - 2 * c, blk), jnp.bfloat16)
        if not first:
            fetch.wait()

    def rows_of(r, piece):
        at = (r * PIECES + piece) * c
        return slice(at, at + c)

    for r in some:
        for step in range(n_col):
            jb = peer_of(me, step)
            span = pl.ds(pl.multiple_of(jb * blk, blk), blk)
            q = ins[step][rows_of(r, 0), :].astype(jnp.float32) * (scaling * LOG2E)
            high = q.astype(jnp.bfloat16)
            q_s[r, jb, :c, :] = high
            q_s[r, jb, c : 2 * c, :] = (q - high.astype(jnp.float32)).astype(jnp.bfloat16)
            k = ins[step][rows_of(r, 1), :]
            k_s[r, :c, span] = k
            k_s[r, c : 2 * c, span] = k
            v_s[r, :c, span] = ins[step][rows_of(r, 2), :]
            g_s[r, jb] = ins[step][rows_of(r, 3), :]
    for r in some:
        k_turned[r] = k_s[r].T
        v_turned[r] = v_s[r].T
    tops, scaled, scales = {}, {}, {}

    def score(jb, r, t):
        part = dot(k_turned[r, t : t + tile, :], q_s[r, jb], ((1,), (0,))) + bias[jb, t : t + tile, :]
        logits[jb % 2, r, t : t + tile, :] = part
        top = jnp.max(part.reshape(tile // 8, 8, blk), axis=0)
        tops[jb, r] = jnp.maximum(tops[jb, r], top) if t else top

    def expand(jb, r, t):
        if t == 0:
            tops[jb, r] = jnp.max(tops[jb, r], axis=0, keepdims=True)
        part = jnp.exp2(logits[jb % 2, r, t : t + tile, :] - tops[jb, r])
        weights[jb % 2, r, t : t + tile, :] = part.astype(jnp.bfloat16)

    def attend(jb, r):
        summed = dot(v_s[r, : c + 16, :], weights[jb % 2, r], ((1,), (0,)))
        inverse = 1.0 / summed[c : c + 1, :]
        attended = summed[:c, :] * inverse
        at_s[r, jb] = attended.astype(jnp.bfloat16)
        g = g_s[r, jb].astype(jnp.float32)
        row_dot = jnp.sum(g * attended, axis=0, keepdims=True) * (-inverse)
        high = row_dot.astype(jnp.bfloat16).astype(jnp.float32)
        rows = lax.broadcasted_iota(jnp.int32, (deep - c, blk), 0)
        tail = jnp.where(rows == 0, high, jnp.where(rows == 1, row_dot - high, 0.0))
        scaled[jb, r] = (g * inverse).astype(jnp.bfloat16)
        scales[jb, r] = jnp.concatenate([scaled[jb, r], tail.astype(jnp.bfloat16)], axis=0)

    def back(jb, t):
        added = total[jb, t : t + tile, :]
        for r in some:
            grad = dot(v_turned[r, t : t + tile, :], scales[jb, r], ((1,), (0,)))
            grad = grad * weights[jb % 2, r, t : t + tile, :].astype(jnp.float32)
            added = added + grad
            grads[jb % 2, r, t : t + tile, :] = grad.astype(jnp.bfloat16)
        total[jb, t : t + tile, :] = added

    def query_grad(jb, r):
        dq_s[r, jb] = (dot(k_s[r, :c, :], grads[jb % 2, r], ((1,), (0,))) * scaling).astype(jnp.bfloat16)

    def add_to(at, r, jb, part):
        if jb:
            part = part + dkv[r, at : at + c, :]
        dkv[r, at : at + c, :] = part

    def key_grad(jb, r):
        add_to(0, r, jb, dot(q_s[r, jb, :c, :], grads[jb % 2, r], ((1,), (1,))))

    def value_grad(jb, r):
        add_to(c, r, jb, dot(scaled[jb, r], weights[jb % 2, r], ((1,), (1,))))

    def each(step, jb, *ranges):
        if not 0 <= jb < n_col:
            return []
        return [functools.partial(step, jb, *at) for at in itertools.product(*ranges)]

    def finish(jb):
        return each(value_grad, jb, some) + each(query_grad, jb, some) + each(key_grad, jb, some)

    woven(each(score, 0, some, tiles))
    for jb in range(n_col):
        woven(each(expand, jb, some, tiles), finish(jb - 1))
        woven(each(attend, jb, some), each(score, jb + 1, some, tiles[: len(tiles) // 2]))
        woven(each(back, jb, tiles), each(score, jb + 1, some, tiles[len(tiles) // 2 :]))
    woven(finish(n_col - 1))

    for r in some:
        for step in range(n_col):
            jb = peer_of(me, step)
            span = pl.ds(pl.multiple_of(jb * blk, blk), blk)
            outs[step][rows_of(r, 0), :] = dq_s[r, jb]
            outs[step][rows_of(r, 1), :] = (dkv[r, :c, span] * (1.0 / LOG2E)).astype(jnp.bfloat16)
            outs[step][rows_of(r, 2), :] = dkv[r, c:, span].astype(jnp.bfloat16)
            outs[step][rows_of(r, 3), :] = at_s[r, jb]

    @pl.when(pl.program_id(0) == pl.num_programs(0) - 1)
    def _():
        if not last:
            keep = pltpu.make_async_copy(total, totals[0], sem)
            keep.start()
            keep.wait()
        else:
            mine, others = totals
            pairs, _, width = mine.shape
            for pair in range(pairs):
                at = 2 * pair * width
                both = total[at // blk, :, at % blk : at % blk + 2 * width].astype(jnp.bfloat16)
                even, odd = both[:, :width], both[:, width:]
                place = peer_of(level, reversed_bits(pair, pairs))
                mine[place] = jnp.where(side == 0, even, odd)
                others[place] = jnp.where(side == 0, odd, even)


def hold_kernel(*refs):
    pass


def params(mib):
    return pltpu.CompilerParams(
        dimension_semantics=("arbitrary",), vmem_limit_bytes=mib * 1024 * 1024
    )


def on_device(n_row, n_col, query, key, value, gate, d_out, bias, length):
    rows, blk, channels = query.shape
    heads, _, n = bias.shape
    c = channels // heads
    groups = n_col // heads
    share = rows // groups
    sizes = [share * weight // sum(SHARES) for weight in SHARES]
    starts = [sum(sizes[:m]) for m in range(len(sizes))]
    assert groups * heads == n_col and n == n_col * blk and groups * sum(sizes) == rows
    scaling = c ** (-0.5)
    per = 2 if all(size % 2 == 0 for size in sizes) else 1
    split_rows = (groups, share, blk, channels)
    query, key, value, gate, d_out = (x.reshape(split_rows) for x in (query, key, value, gate, d_out))
    row = lax.axis_index("row")
    level = reversed_bits(row // 2, n_row // 2)
    info = jnp.stack([length[0], lax.axis_index("col"), row % 2, level]).astype(jnp.int32)
    width = n // n_row
    lines = PIECES * c
    chunks = len(sizes)

    untouched = pl.BlockSpec(memory_space=pl.ANY)

    def exchange(blocks):
        pairs = [[(a, a ^ step) for a in range(n_col)] for step in range(n_col)]
        return [blocks[0]] + [lax.ppermute(blocks[step], "col", pairs[step]) for step in range(1, n_col)]

    def swap(x):
        return lax.ppermute(x, "row", [(r, r ^ 1) for r in range(n_row)])

    def hold(blocks, until):
        count = len(blocks)
        return pl.pallas_call(
            hold_kernel,
            in_specs=[untouched] * (count + len(until)),
            out_specs=[untouched] * count,
            out_shape=[jax.ShapeDtypeStruct(x.shape, x.dtype) for x in blocks],
            input_output_aliases={a: a for a in range(count)},
            compiler_params=pltpu.CompilerParams(vmem_limit_bytes=1024 * 1024),
            name="hold",
        )(*blocks, *until)

    def call(kernel, name, flops, grid, operands, out_specs, out_shape, scratch, aliases):
        return pl.pallas_call(
            kernel,
            grid_spec=pltpu.PrefetchScalarGridSpec(
                num_scalar_prefetch=1,
                grid=(grid,),
                in_specs=[spec for spec, _ in operands],
                out_specs=out_specs,
                scratch_shapes=scratch,
            ),
            out_shape=out_shape,
            input_output_aliases=aliases,
            compiler_params=params({"pack": 60, "attend": 28, "unpack": 24}[name]),
            cost_estimate=pl.CostEstimate(flops=flops, bytes_accessed=1, transcendentals=0),
            name=name,
        )(info, *[x for _, x in operands])

    def still(*shape):
        return pl.BlockSpec(shape, lambda i, info: (0,) * len(shape), pipeline_mode=pl.Buffered(1))

    def part(size, skip):
        return pl.BlockSpec((size, blk), lambda i, info: (skip + i, 0))

    def rows_a_step(*counts):
        return max(step for step in range(1, 5) if all(count % step == 0 for count in counts))

    def rows_of(group):
        return starts[group[0]], sum(sizes[m] for m in group)

    def pack(group):
        with_bias = group[0] == 0
        start, count = rows_of(group)
        step = rows_a_step(start, count)
        assert not with_bias or step == count
        base = start // step
        whole = pl.BlockSpec((groups, step, blk, channels), lambda i, info: (0, base + i, 0, 0))
        ahead = [n] + [n // 2] * (n_col - 1) if with_bias else [0] * n_col
        size = count * lines
        operands = [(whole, x) for x in (query, key, value, gate, d_out)]
        if with_bias:
            operands.append((still(heads, blk, n), bias))
        return call(
            functools.partial(pack_kernel, heads, groups, with_bias),
            "pack",
            count * 10**6,
            count // step,
            operands,
            [part(x + step * lines, 0) for x in ahead],
            [jax.ShapeDtypeStruct((x + size, blk), jnp.bfloat16) for x in ahead],
            [pltpu.VMEM((groups, step, PIECES, channels, blk), jnp.bfloat16)],
            {},
        )

    def attend(m, total, bias_blocks, blocks, room):
        first, last = m == 0, m == chunks - 1

        def scratch(*shape, dtype=jnp.bfloat16):
            return pltpu.VMEM((per, *shape), dtype)

        operands = [(still(n if a == 0 else n // 2, blk), x) for a, x in enumerate(bias_blocks)]
        (inward,) = [group for group in INWARD if m in group]
        (outward,) = [group for group in OUTWARD if m in group]
        behind = sum(sizes[o] for o in inward if o < m) // per
        ahead = sum(sizes[o] for o in outward if o < m) // per
        for a, x in enumerate(blocks):
            skip = (n if a == 0 else n // 2) // (per * lines) if first else behind
            operands.append((part(per * lines, skip), x))
        square = (n_col, n, blk)
        aliases = {}
        if not first:
            if not last:
                aliases[1 + len(operands)] = n_col
            operands.append((untouched, total))
        if ahead:
            aliases |= {1 + len(operands) + a: a for a in range(n_col)}
            operands += [(untouched, x) for x in room]
        size = rows_of(outward)[1]
        out_shape = [jax.ShapeDtypeStruct((size * lines, blk), jnp.bfloat16)] * n_col
        if last:
            totals = [jax.ShapeDtypeStruct((n_row // 2, n, width), jnp.bfloat16)] * 2
        else:
            totals = [jax.ShapeDtypeStruct(square, jnp.float32)]
        deep = 4 * c
        result = call(
            functools.partial(attention_kernel, n_col, per, c, scaling, first, last),
            "attend",
            sizes[m] * 4 * 10**9,
            sizes[m] // per,
            operands,
            [part(per * lines, ahead)] * n_col
            + ([still(*x.shape) for x in totals] if last else [untouched])
            + [still(8, 128)],
            out_shape + totals + [jax.ShapeDtypeStruct((8, 128), jnp.float32)],
            [
                pltpu.VMEM(square, jnp.float32),
                pltpu.VMEM(square, jnp.float32),
                scratch(n_col, deep, blk),
                scratch(n_col, c, blk),
                scratch(deep, n),
                scratch(deep, n),
                scratch(n, deep),
                scratch(n, deep),
                scratch(n_col, c, blk),
                scratch(n_col, c, blk),
                scratch(2 * c, n, dtype=jnp.float32),
                pltpu.VMEM((2, per, n, blk), jnp.float32),
                pltpu.VMEM((2, per, n, blk), jnp.bfloat16),
                pltpu.VMEM((2, per, n, blk), jnp.bfloat16),
                pltpu.SemaphoreType.DMA,
            ],
            aliases,
        )
        return result[:n_col], result[n_col:-1], result[-1]

    def unpack(group, blocks, grads):
        start, count = rows_of(group)
        step = rows_a_step(start, count)
        base = start // step
        whole = pl.BlockSpec((groups, step, blk, channels), lambda i, info: (0, base + i, 0, 0))
        kept = [] if grads is None else list(grads)
        operands = [(whole, gate), (whole, d_out)]
        operands += [(part(step * lines, 0), x) for x in blocks]
        aliases = {1 + len(operands) + a: a for a in range(len(kept))}
        operands += [(untouched, x) for x in kept]
        return call(
            functools.partial(unpack_kernel, heads, groups),
            "unpack",
            1,
            count // step,
            operands,
            [whole] * 4 + [pl.BlockSpec((8, 128), lambda i, info: (0, 0))],
            [jax.ShapeDtypeStruct(query.shape, jnp.bfloat16)] * 4
            + [jax.ShapeDtypeStruct((8, 128), jnp.float32)],
            [pltpu.VMEM((groups, step, PIECES, channels, blk), jnp.bfloat16)],
            aliases,
        )

    packed = [pack(group) for group in INWARD]
    own, *fetched = exchange(packed[0])
    fetched = hold(fetched, [x[0] for x in packed[1:]])
    tables = [own, *fetched] + [swap(x) for x in fetched]
    arrived = {0: [own, *fetched]}

    totals, results, sent, done = [None], None, [], []
    for m in range(chunks):
        at = [m in group for group in INWARD].index(True)
        for ahead in range(at + 1, min(at + 2, len(INWARD) - 1) + 1):
            if ahead not in arrived and (ahead == 1 or m >= INWARD[ahead - 1][0]):
                until = arrived[ahead - 1][1:] + (done[m - 1 : m] if m else [])
                arrived[ahead] = exchange([packed[ahead][0], *hold(packed[ahead][1:], until)])
        if m == chunks - 1:
            totals = hold(totals, sent[0][1:])
        results, totals, token = attend(m, totals[0], tables, arrived[at], results)
        done.append(token)
        if m in [group[-1] for group in OUTWARD]:
            sent.append(exchange(results))
    grads, tokens = None, []
    for group, blocks in zip(OUTWARD, sent):
        *grads, token = unpack(group, blocks, grads)
        tokens.append(token)

    mine, others = totals
    total = mine.astype(jnp.float32) + swap(others).astype(jnp.float32)
    apart = 2
    while total.shape[0] > 1:
        kept, given = jnp.split(total, 2)
        given = given.astype(jnp.bfloat16)
        given = lax.ppermute(given, "row", [(r, r ^ apart) for r in range(n_row)])
        total = kept + given.astype(jnp.float32)
        apart *= 2
    total = (total + tokens[-2][0, 0]).astype(jnp.bfloat16).reshape(n_col, blk, width)
    total = lax.all_to_all(total, "col", split_axis=0, concat_axis=0, tiled=True)
    total = jnp.sum(total.reshape(heads, groups, blk, width).astype(jnp.float32), axis=1)
    bias_grad = jnp.transpose(total, (0, 2, 1))
    d_query, d_key, d_value, d_gate = (x.reshape(rows, blk, channels) for x in grads)
    return d_query, d_key, d_value, d_gate, bias_grad


def solution(mesh):
    pair = P("row", "col", None)
    return jax.shard_map(
        functools.partial(on_device, mesh.shape["row"], mesh.shape["col"]),
        mesh=mesh,
        in_specs=(pair, pair, pair, pair, pair, P(None, "col", None), P()),
        out_specs=(pair, pair, pair, pair, P(None, "row", "col")),
        check_vma=False,
    )
```

```python
import functools
import itertools

import jax
import jax.numpy as jnp
from jax import lax
from jax.experimental import pallas as pl
from jax.experimental.pallas import tpu as pltpu
from jax.sharding import PartitionSpec as P

LOG2E = 1.4426950408889634
MASKED = -1e30
SHARES = (1, 3, 3, 5)
INWARD = ((0,), (1,), (2,), (3,))
OUTWARD = ((0, 1, 2), (3,))
PIECES = 4


def dot(a, b, dims):
    return lax.dot_general(a, b, (dims, ((), ())), preferred_element_type=jnp.float32)


def peer_of(me, step):
    return jnp.bitwise_xor(me, step)


def pack_kernel(heads, groups, with_bias, info, q_ref, k_ref, v_ref, g_ref, o_ref, *refs):
    n_col = heads * groups
    outs, turned = refs[-1 - n_col : -1], refs[-1]
    me = info[1]
    count, _, channels = q_ref.shape[1:]
    c = channels // heads
    lines = count * PIECES * c
    for i in range(count):
        for g in range(groups):
            gated = o_ref[g, i].astype(jnp.float32) * jax.nn.sigmoid(g_ref[g, i].astype(jnp.float32))
            pieces = (q_ref[g, i], k_ref[g, i], v_ref[g, i], gated.astype(jnp.bfloat16))
            for piece, x in enumerate(pieces):
                turned[g, i, piece] = x.T
        for step in range(n_col):
            peer = peer_of(me, step)
            head = pl.multiple_of(peer // groups * c, c)
            base = outs[step].shape[0] - lines
            for piece in range(PIECES):
                at = base + (i * PIECES + piece) * c
                outs[step][at : at + c, :] = turned[peer % groups, i, piece, pl.ds(head, c), :]
    if with_bias:
        for step in range(n_col):
            base = outs[step].shape[0] - lines
            keys = pl.ds(pl.multiple_of(info[2] * base, base), base) if step else slice(None)
            outs[step][:base, :] = refs[0][peer_of(me, step) // groups, :, keys].T


def unpack_kernel(heads, groups, info, g_ref, o_ref, *refs):
    n_col = heads * groups
    ins, (dq, dk, dv, dg, token, whole) = refs[:n_col], refs[-6:]
    token[...] = jnp.zeros_like(token)
    me = info[1]
    count, _, channels = g_ref.shape[1:]
    c = channels // heads
    for i in range(count):
        for step in range(n_col):
            peer = peer_of(me, step)
            head = pl.multiple_of(peer // groups * c, c)
            for piece in range(PIECES):
                at = (i * PIECES + piece) * c
                whole[peer % groups, i, piece, pl.ds(head, c), :] = ins[step][at : at + c, :]
        for g in range(groups):
            dq[g, i] = whole[g, i, 0].T
            dk[g, i] = whole[g, i, 1].T
            dv[g, i] = whole[g, i, 2].T
            attended = whole[g, i, 3].T.astype(jnp.float32)
            s = jax.nn.sigmoid(g_ref[g, i].astype(jnp.float32))
            dg[g, i] = (o_ref[g, i].astype(jnp.float32) * attended * s * (1.0 - s)).astype(jnp.bfloat16)


def reversed_bits(x, count):
    return sum((x // 2**bit % 2) * (count // 2 ** (bit + 1)) for bit in range(count.bit_length() - 1))


def woven(*queues):
    order = [(at / len(q), which, at) for which, q in enumerate(queues) for at in range(len(q))]
    for _, which, at in sorted(order):
        queues[which][at]()


def attention_kernel(n_col, together, c, scaling, first, last, info, *refs):
    bias_in, ins, refs = refs[: 2 * n_col - 1], refs[2 * n_col - 1 : 3 * n_col - 1], refs[3 * n_col - 1 :]
    scratch, refs = refs[-14:], refs[:-14]
    bias, total_s, q_s, g_s, k_s, v_s, k_turned, v_turned, dq_s, at_s, dkv, logits, weights, grads = scratch
    if not first:
        total_in = refs[0]
    *totals, token = refs[-3:] if last else refs[-2:]
    outs = refs[-n_col - len(totals) - 1 : -len(totals) - 1]
    total = total_s if last else totals[0]
    length, me, side, level = info[0], info[1], info[2], info[3]
    blk = ins[0].shape[1]
    n = n_col * blk
    tile = min(256, n)
    tiles = range(0, n, tile)
    deep = k_s.shape[1]
    some = range(together)

    @pl.when(pl.program_id(0) == 0)
    def _():
        token[...] = jnp.zeros_like(token)
        if first:
            total[...] = jnp.zeros_like(total)
        else:
            total[...] = total_in[...]
        half = n // 2
        bias[me] = bias_in[0][...].astype(jnp.float32) * LOG2E
        for step in range(1, n_col):
            for table, which in ((bias_in[step], side), (bias_in[n_col + step - 1], 1 - side)):
                keys = pl.ds(pl.multiple_of(which * half, half), half)
                bias[peer_of(me, step), keys, :] = table[...].astype(jnp.float32) * LOG2E
        rows = lax.broadcasted_iota(jnp.int32, (deep - 2 * c, n), 0)
        keys = lax.broadcasted_iota(jnp.int32, (deep - 2 * c, n), 1)
        mask = jnp.logical_and(rows == 0, keys >= length)
        for r in some:
            k_s[r, 2 * c :, :] = jnp.where(mask, MASKED, 0.0).astype(jnp.bfloat16)
            v_s[r, c:, :] = jnp.ones((deep - c, n), jnp.bfloat16)
            q_s[r, :, 2 * c :, :] = jnp.ones((n_col, deep - 2 * c, blk), jnp.bfloat16)

    def rows_of(r, piece):
        at = (r * PIECES + piece) * c
        return slice(at, at + c)

    for r in some:
        for step in range(n_col):
            jb = peer_of(me, step)
            span = pl.ds(pl.multiple_of(jb * blk, blk), blk)
            q = ins[step][rows_of(r, 0), :].astype(jnp.float32) * (scaling * LOG2E)
            high = q.astype(jnp.bfloat16)
            q_s[r, jb, :c, :] = high
            q_s[r, jb, c : 2 * c, :] = (q - high.astype(jnp.float32)).astype(jnp.bfloat16)
            k = ins[step][rows_of(r, 1), :]
            k_s[r, :c, span] = k
            k_s[r, c : 2 * c, span] = k
            v_s[r, :c, span] = ins[step][rows_of(r, 2), :]
            g_s[r, jb] = ins[step][rows_of(r, 3), :]
    for r in some:
        k_turned[r] = k_s[r].T
        v_turned[r] = v_s[r].T
    tops, scaled, scales = {}, {}, {}

    def score(jb, r, t):
        part = dot(k_turned[r, t : t + tile, :], q_s[r, jb], ((1,), (0,))) + bias[jb, t : t + tile, :]
        logits[jb % 2, r, t : t + tile, :] = part
        top = jnp.max(part.reshape(tile // 8, 8, blk), axis=0)
        tops[jb, r] = jnp.maximum(tops[jb, r], top) if t else top

    def expand(jb, r, t):
        if t == 0:
            tops[jb, r] = jnp.max(tops[jb, r], axis=0, keepdims=True)
        part = jnp.exp2(logits[jb % 2, r, t : t + tile, :] - tops[jb, r])
        weights[jb % 2, r, t : t + tile, :] = part.astype(jnp.bfloat16)

    def attend(jb, r):
        summed = dot(v_s[r, : c + 16, :], weights[jb % 2, r], ((1,), (0,)))
        inverse = 1.0 / summed[c : c + 1, :]
        attended = summed[:c, :] * inverse
        at_s[r, jb] = attended.astype(jnp.bfloat16)
        g = g_s[r, jb].astype(jnp.float32)
        row_dot = jnp.sum(g * attended, axis=0, keepdims=True) * (-inverse)
        high = row_dot.astype(jnp.bfloat16).astype(jnp.float32)
        rows = lax.broadcasted_iota(jnp.int32, (deep - c, blk), 0)
        tail = jnp.where(rows == 0, high, jnp.where(rows == 1, row_dot - high, 0.0))
        scaled[jb, r] = (g * inverse).astype(jnp.bfloat16)
        scales[jb, r] = jnp.concatenate([scaled[jb, r], tail.astype(jnp.bfloat16)], axis=0)

    def back(jb, t):
        added = total[jb, t : t + tile, :]
        for r in some:
            grad = dot(v_turned[r, t : t + tile, :], scales[jb, r], ((1,), (0,)))
            grad = grad * weights[jb % 2, r, t : t + tile, :].astype(jnp.float32)
            added = added + grad
            grads[jb % 2, r, t : t + tile, :] = grad.astype(jnp.bfloat16)
        total[jb, t : t + tile, :] = added

    def query_grad(jb, r):
        dq_s[r, jb] = (dot(k_s[r, :c, :], grads[jb % 2, r], ((1,), (0,))) * scaling).astype(jnp.bfloat16)

    def add_to(at, r, jb, part):
        if jb:
            part = part + dkv[r, at : at + c, :]
        dkv[r, at : at + c, :] = part

    def key_grad(jb, r):
        add_to(0, r, jb, dot(q_s[r, jb, :c, :], grads[jb % 2, r], ((1,), (1,))))

    def value_grad(jb, r):
        add_to(c, r, jb, dot(scaled[jb, r], weights[jb % 2, r], ((1,), (1,))))

    def each(step, jb, *ranges):
        if not 0 <= jb < n_col:
            return []
        return [functools.partial(step, jb, *at) for at in itertools.product(*ranges)]

    def finish(jb):
        return each(value_grad, jb, some) + each(query_grad, jb, some) + each(key_grad, jb, some)

    woven(each(score, 0, some, tiles))
    for jb in range(n_col):
        woven(each(expand, jb, some, tiles), finish(jb - 1))
        woven(each(attend, jb, some), each(score, jb + 1, some, tiles[: len(tiles) // 2]))
        woven(each(back, jb, tiles), each(score, jb + 1, some, tiles[len(tiles) // 2 :]))
    woven(finish(n_col - 1))

    for r in some:
        for step in range(n_col):
            jb = peer_of(me, step)
            span = pl.ds(pl.multiple_of(jb * blk, blk), blk)
            outs[step][rows_of(r, 0), :] = dq_s[r, jb]
            outs[step][rows_of(r, 1), :] = (dkv[r, :c, span] * (1.0 / LOG2E)).astype(jnp.bfloat16)
            outs[step][rows_of(r, 2), :] = dkv[r, c:, span].astype(jnp.bfloat16)
            outs[step][rows_of(r, 3), :] = at_s[r, jb]

    if last:

        @pl.when(pl.program_id(0) == pl.num_programs(0) - 1)
        def _():
            mine, others = totals
            pairs, _, width = mine.shape
            for pair in range(pairs):
                at = 2 * pair * width
                both = total[at // blk, :, at % blk : at % blk + 2 * width].astype(jnp.bfloat16)
                even, odd = both[:, :width], both[:, width:]
                place = peer_of(level, reversed_bits(pair, pairs))
                mine[place] = jnp.where(side == 0, even, odd)
                others[place] = jnp.where(side == 0, odd, even)


def hold_kernel(*refs):
    pass


def params(mib):
    return pltpu.CompilerParams(
        dimension_semantics=("arbitrary",), vmem_limit_bytes=mib * 1024 * 1024
    )


def on_device(n_row, n_col, query, key, value, gate, d_out, bias, length):
    rows, blk, channels = query.shape
    heads, _, n = bias.shape
    c = channels // heads
    groups = n_col // heads
    share = rows // groups
    sizes = [share * weight // sum(SHARES) for weight in SHARES]
    starts = [sizes[-1] + sum(sizes[:m]) for m in range(len(sizes) - 1)] + [0]
    assert groups * heads == n_col and n == n_col * blk and groups * sum(sizes) == rows
    scaling = c ** (-0.5)
    per = 2 if all(size % 2 == 0 for size in sizes) else 1
    split_rows = (groups, share, blk, channels)
    query, key, value, gate, d_out = (x.reshape(split_rows) for x in (query, key, value, gate, d_out))
    row = lax.axis_index("row")
    level = reversed_bits(row // 2, n_row // 2)
    info = jnp.stack([length[0], lax.axis_index("col"), row % 2, level]).astype(jnp.int32)
    width = n // n_row
    lines = PIECES * c
    chunks = len(sizes)

    untouched = pl.BlockSpec(memory_space=pl.ANY)

    def exchange(blocks):
        pairs = [[(a, a ^ step) for a in range(n_col)] for step in range(n_col)]
        return [blocks[0]] + [lax.ppermute(blocks[step], "col", pairs[step]) for step in range(1, n_col)]

    def swap(x):
        return lax.ppermute(x, "row", [(r, r ^ 1) for r in range(n_row)])

    def hold(blocks, until):
        count = len(blocks)
        return pl.pallas_call(
            hold_kernel,
            in_specs=[untouched] * (count + len(until)),
            out_specs=[untouched] * count,
            out_shape=[jax.ShapeDtypeStruct(x.shape, x.dtype) for x in blocks],
            input_output_aliases={a: a for a in range(count)},
            compiler_params=pltpu.CompilerParams(vmem_limit_bytes=1024 * 1024),
            name="hold",
        )(*blocks, *until)

    def call(kernel, name, flops, grid, operands, out_specs, out_shape, scratch, aliases):
        return pl.pallas_call(
            kernel,
            grid_spec=pltpu.PrefetchScalarGridSpec(
                num_scalar_prefetch=1,
                grid=(grid,),
                in_specs=[spec for spec, _ in operands],
                out_specs=out_specs,
                scratch_shapes=scratch,
            ),
            out_shape=out_shape,
            input_output_aliases=aliases,
            compiler_params=params({"pack": 60, "attend": 34, "unpack": 24}[name]),
            cost_estimate=pl.CostEstimate(flops=flops, bytes_accessed=1, transcendentals=0),
            name=name,
        )(info, *[x for _, x in operands])

    def still(*shape):
        return pl.BlockSpec(shape, lambda i, info: (0,) * len(shape), pipeline_mode=pl.Buffered(1))

    def part(size, skip):
        return pl.BlockSpec((size, blk), lambda i, info: (skip + i, 0))

    def rows_a_step(*counts):
        return max(step for step in range(1, 6) if all(count % step == 0 for count in counts))

    def rows_of(group):
        return starts[group[0]], sum(sizes[m] for m in group)

    def pack(group):
        with_bias = group[0] == 0
        start, count = rows_of(group)
        step = rows_a_step(start, count)
        assert not with_bias or step == count
        base = start // step
        whole = pl.BlockSpec((groups, step, blk, channels), lambda i, info: (0, base + i, 0, 0))
        ahead = [n] + [n // 2] * (n_col - 1) if with_bias else [0] * n_col
        size = count * lines
        operands = [(whole, x) for x in (query, key, value, gate, d_out)]
        if with_bias:
            operands.append((still(heads, blk, n), bias))
        return call(
            functools.partial(pack_kernel, heads, groups, with_bias),
            "pack",
            count * 10**6,
            count // step,
            operands,
            [part(x + step * lines, 0) for x in ahead],
            [jax.ShapeDtypeStruct((x + size, blk), jnp.bfloat16) for x in ahead],
            [pltpu.VMEM((groups, step, PIECES, channels, blk), jnp.bfloat16)],
            {},
        )

    def attend(m, total, bias_blocks, blocks, room):
        first, last = m == 0, m == chunks - 1

        def scratch(*shape, dtype=jnp.bfloat16):
            return pltpu.VMEM((per, *shape), dtype)

        operands = [(still(n if a == 0 else n // 2, blk), x) for a, x in enumerate(bias_blocks)]
        (inward,) = [group for group in INWARD if m in group]
        (outward,) = [group for group in OUTWARD if m in group]
        behind = sum(sizes[o] for o in inward if o < m) // per
        ahead = sum(sizes[o] for o in outward if o < m) // per
        for a, x in enumerate(blocks):
            skip = (n if a == 0 else n // 2) // (per * lines) if first else behind
            operands.append((part(per * lines, skip), x))
        square = (n_col, n, blk)
        aliases = {}
        if not first:
            operands.append((still(*square), total))
        if ahead:
            aliases |= {1 + len(operands) + a: a for a in range(n_col)}
            operands += [(untouched, x) for x in room]
        size = rows_of(outward)[1]
        out_shape = [jax.ShapeDtypeStruct((size * lines, blk), jnp.bfloat16)] * n_col
        if last:
            totals = [jax.ShapeDtypeStruct((n_row // 2, n, width), jnp.bfloat16)] * 2
        else:
            totals = [jax.ShapeDtypeStruct(square, jnp.float32)]
        deep = 4 * c
        result = call(
            functools.partial(attention_kernel, n_col, per, c, scaling, first, last),
            "attend",
            sizes[m] * 4 * 10**9,
            sizes[m] // per,
            operands,
            [part(per * lines, ahead)] * n_col
            + [still(*x.shape) for x in totals]
            + [still(8, 128)],
            out_shape + totals + [jax.ShapeDtypeStruct((8, 128), jnp.float32)],
            [
                pltpu.VMEM(square, jnp.float32),
                pltpu.VMEM(square if last else (8, 128), jnp.float32),
                scratch(n_col, deep, blk),
                scratch(n_col, c, blk),
                scratch(deep, n),
                scratch(deep, n),
                scratch(n, deep),
                scratch(n, deep),
                scratch(n_col, c, blk),
                scratch(n_col, c, blk),
                scratch(2 * c, n, dtype=jnp.float32),
                pltpu.VMEM((2, per, n, blk), jnp.float32),
                pltpu.VMEM((2, per, n, blk), jnp.bfloat16),
                pltpu.VMEM((2, per, n, blk), jnp.bfloat16),
            ],
            aliases,
        )
        return result[:n_col], result[n_col:-1], result[-1]

    def unpack(group, blocks, grads):
        start, count = rows_of(group)
        step = rows_a_step(start, count)
        base = start // step
        whole = pl.BlockSpec((groups, step, blk, channels), lambda i, info: (0, base + i, 0, 0))
        kept = [] if grads is None else list(grads)
        operands = [(whole, gate), (whole, d_out)]
        operands += [(part(step * lines, 0), x) for x in blocks]
        aliases = {1 + len(operands) + a: a for a in range(len(kept))}
        operands += [(untouched, x) for x in kept]
        return call(
            functools.partial(unpack_kernel, heads, groups),
            "unpack",
            1,
            count // step,
            operands,
            [whole] * 4 + [pl.BlockSpec((8, 128), lambda i, info: (0, 0))],
            [jax.ShapeDtypeStruct(query.shape, jnp.bfloat16)] * 4
            + [jax.ShapeDtypeStruct((8, 128), jnp.float32)],
            [pltpu.VMEM((groups, step, PIECES, channels, blk), jnp.bfloat16)],
            aliases,
        )

    packed = [pack(group) for group in INWARD]
    own, *fetched = exchange(packed[0])
    fetched = hold(fetched, [x[0] for x in packed[1:]])
    tables = [own, *fetched] + [swap(x) for x in fetched]
    arrived = {0: [own, *fetched]}

    totals, results, sent, done = [None], None, [], []
    for m in range(chunks):
        at = [m in group for group in INWARD].index(True)
        for ahead in range(at + 1, min(at + 2, len(INWARD) - 1) + 1):
            if ahead not in arrived and (ahead == 1 or m >= INWARD[ahead - 1][0]):
                until = arrived[ahead - 1][1:] + (done[m - 1 : m] if m else [])
                arrived[ahead] = exchange([packed[ahead][0], *hold(packed[ahead][1:], until)])
        results, totals, token = attend(m, totals[0], tables, arrived[at], results)
        done.append(token)
        if m in [group[-1] for group in OUTWARD]:
            sent.append(exchange(results))
    grads, tokens = None, []
    for group, blocks in zip(OUTWARD, sent):
        *grads, token = unpack(group, blocks, grads)
        tokens.append(token)

    mine, others = totals
    (others,) = hold([others], sent[0][1:])
    total = mine.astype(jnp.float32) + swap(others).astype(jnp.float32)
    apart = 2
    while total.shape[0] > 1:
        kept, given = jnp.split(total, 2)
        given = given.astype(jnp.bfloat16)
        given = lax.ppermute(given, "row", [(r, r ^ apart) for r in range(n_row)])
        total = kept + given.astype(jnp.float32)
        apart *= 2
    total = (total + tokens[-2][0, 0]).astype(jnp.bfloat16).reshape(n_col, blk, width)
    total = lax.all_to_all(total, "col", split_axis=0, concat_axis=0, tiled=True)
    total = jnp.sum(total.reshape(heads, groups, blk, width).astype(jnp.float32), axis=1)
    bias_grad = jnp.transpose(total, (0, 2, 1))
    d_query, d_key, d_value, d_gate = (x.reshape(rows, blk, channels) for x in grads)
    return d_query, d_key, d_value, d_gate, bias_grad


def solution(mesh):
    pair = P("row", "col", None)
    return jax.shard_map(
        functools.partial(on_device, mesh.shape["row"], mesh.shape["col"]),
        mesh=mesh,
        in_specs=(pair, pair, pair, pair, pair, P(None, "col", None), P()),
        out_specs=(pair, pair, pair, pair, P(None, "row", "col")),
        check_vma=False,
    )
```

```python
import functools
import itertools

import jax
import jax.numpy as jnp
from jax import lax
from jax.experimental import pallas as pl
from jax.experimental.pallas import tpu as pltpu
from jax.sharding import PartitionSpec as P

LOG2E = 1.4426950408889634
MASKED = -1e30
SHARES = (1, 2, 4, 5)
INWARD = ((0,), (1,), (2,), (3,))
OUTWARD = ((0, 1, 2), (3,))
PIECES = 4


def dot(a, b, dims):
    return lax.dot_general(a, b, (dims, ((), ())), preferred_element_type=jnp.float32)


def peer_of(me, step):
    return jnp.bitwise_xor(me, step)


def pack_kernel(heads, groups, with_bias, info, q_ref, k_ref, v_ref, g_ref, o_ref, *refs):
    n_col = heads * groups
    outs, turned = refs[-1 - n_col : -1], refs[-1]
    me = info[1]
    count, _, channels = q_ref.shape[1:]
    c = channels // heads
    lines = count * PIECES * c
    for i in range(count):
        for g in range(groups):
            gated = o_ref[g, i].astype(jnp.float32) * jax.nn.sigmoid(g_ref[g, i].astype(jnp.float32))
            pieces = (q_ref[g, i], k_ref[g, i], v_ref[g, i], gated.astype(jnp.bfloat16))
            for piece, x in enumerate(pieces):
                turned[g, i, piece] = x.T
        for step in range(n_col):
            peer = peer_of(me, step)
            head = pl.multiple_of(peer // groups * c, c)
            base = outs[step].shape[0] - lines
            for piece in range(PIECES):
                at = base + (i * PIECES + piece) * c
                outs[step][at : at + c, :] = turned[peer % groups, i, piece, pl.ds(head, c), :]
    if with_bias:
        for step in range(n_col):
            base = outs[step].shape[0] - lines
            keys = pl.ds(pl.multiple_of(info[2] * base, base), base) if step else slice(None)
            outs[step][:base, :] = refs[0][peer_of(me, step) // groups, :, keys].T


def unpack_kernel(heads, groups, info, g_ref, o_ref, *refs):
    n_col = heads * groups
    ins, (dq, dk, dv, dg, token, whole) = refs[:n_col], refs[-6:]
    token[...] = jnp.zeros_like(token)
    me = info[1]
    count, _, channels = g_ref.shape[1:]
    c = channels // heads
    for i in range(count):
        for step in range(n_col):
            peer = peer_of(me, step)
            head = pl.multiple_of(peer // groups * c, c)
            for piece in range(PIECES):
                at = (i * PIECES + piece) * c
                whole[peer % groups, i, piece, pl.ds(head, c), :] = ins[step][at : at + c, :]
        for g in range(groups):
            dq[g, i] = whole[g, i, 0].T
            dk[g, i] = whole[g, i, 1].T
            dv[g, i] = whole[g, i, 2].T
            attended = whole[g, i, 3].T.astype(jnp.float32)
            s = jax.nn.sigmoid(g_ref[g, i].astype(jnp.float32))
            dg[g, i] = (o_ref[g, i].astype(jnp.float32) * attended * s * (1.0 - s)).astype(jnp.bfloat16)


def woven(*queues):
    order = [(at / len(q), which, at) for which, q in enumerate(queues) for at in range(len(q))]
    for _, which, at in sorted(order):
        queues[which][at]()


def attention_kernel(n_col, together, c, scaling, first, last, info, *refs):
    bias_in, ins, refs = refs[: 2 * n_col - 1], refs[2 * n_col - 1 : 3 * n_col - 1], refs[3 * n_col - 1 :]
    scratch, refs = refs[-14:], refs[:-14]
    bias, total_s, q_s, g_s, k_s, v_s, k_turned, v_turned, dq_s, at_s, dkv, logits, weights, grads = scratch
    if not first:
        total_in = refs[0]
    *totals, token = refs[-3:] if last else refs[-2:]
    outs = refs[-n_col - len(totals) - 1 : -len(totals) - 1]
    total = total_s if last else totals[0]
    length, me, side, level = info[0], info[1], info[2], info[3]
    blk = ins[0].shape[1]
    n = n_col * blk
    tile = min(256, n)
    tiles = range(0, n, tile)
    deep = k_s.shape[1]
    some = range(together)

    @pl.when(pl.program_id(0) == 0)
    def _():
        token[...] = jnp.zeros_like(token)
        if first:
            total[...] = jnp.zeros_like(total)
        else:
            total[...] = total_in[...]
        half = n // 2
        bias[me] = bias_in[0][...].astype(jnp.float32) * LOG2E
        for step in range(1, n_col):
            for table, which in ((bias_in[step], side), (bias_in[n_col + step - 1], 1 - side)):
                keys = pl.ds(pl.multiple_of(which * half, half), half)
                bias[peer_of(me, step), keys, :] = table[...].astype(jnp.float32) * LOG2E
        rows = lax.broadcasted_iota(jnp.int32, (deep - 2 * c, n), 0)
        keys = lax.broadcasted_iota(jnp.int32, (deep - 2 * c, n), 1)
        mask = jnp.logical_and(rows == 0, keys >= length)
        for r in some:
            k_s[r, 2 * c :, :] = jnp.where(mask, MASKED, 0.0).astype(jnp.bfloat16)
            v_s[r, c:, :] = jnp.ones((deep - c, n), jnp.bfloat16)
            q_s[r, :, 2 * c :, :] = jnp.ones((n_col, deep - 2 * c, blk), jnp.bfloat16)

    def rows_of(r, piece):
        at = (r * PIECES + piece) * c
        return slice(at, at + c)

    for r in some:
        for step in range(n_col):
            jb = peer_of(me, step)
            span = pl.ds(pl.multiple_of(jb * blk, blk), blk)
            q = ins[step][rows_of(r, 0), :].astype(jnp.float32) * (scaling * LOG2E)
            high = q.astype(jnp.bfloat16)
            q_s[r, jb, :c, :] = high
            q_s[r, jb, c : 2 * c, :] = (q - high.astype(jnp.float32)).astype(jnp.bfloat16)
            k = ins[step][rows_of(r, 1), :]
            k_s[r, :c, span] = k
            k_s[r, c : 2 * c, span] = k
            v_s[r, :c, span] = ins[step][rows_of(r, 2), :]
            g_s[r, jb] = ins[step][rows_of(r, 3), :]
    for r in some:
        k_turned[r] = k_s[r].T
        v_turned[r] = v_s[r].T
    tops, scaled, scales = {}, {}, {}

    def score(jb, r, t):
        part = dot(k_turned[r, t : t + tile, :], q_s[r, jb], ((1,), (0,))) + bias[jb, t : t + tile, :]
        logits[jb % 2, r, t : t + tile, :] = part
        top = jnp.max(part.reshape(tile // 8, 8, blk), axis=0)
        tops[jb, r] = jnp.maximum(tops[jb, r], top) if t else top

    def expand(jb, r, t):
        if t == 0:
            tops[jb, r] = jnp.max(tops[jb, r], axis=0, keepdims=True)
        part = jnp.exp2(logits[jb % 2, r, t : t + tile, :] - tops[jb, r])
        weights[jb % 2, r, t : t + tile, :] = part.astype(jnp.bfloat16)

    def attend(jb, r):
        summed = dot(v_s[r, : c + 16, :], weights[jb % 2, r], ((1,), (0,)))
        inverse = 1.0 / summed[c : c + 1, :]
        attended = summed[:c, :] * inverse
        at_s[r, jb] = attended.astype(jnp.bfloat16)
        g = g_s[r, jb].astype(jnp.float32)
        row_dot = jnp.sum(g * attended, axis=0, keepdims=True) * (-inverse)
        high = row_dot.astype(jnp.bfloat16).astype(jnp.float32)
        rows = lax.broadcasted_iota(jnp.int32, (deep - c, blk), 0)
        tail = jnp.where(rows == 0, high, jnp.where(rows == 1, row_dot - high, 0.0))
        scaled[jb, r] = (g * inverse).astype(jnp.bfloat16)
        scales[jb, r] = jnp.concatenate([scaled[jb, r], tail.astype(jnp.bfloat16)], axis=0)

    def back(jb, t):
        added = total[jb, t : t + tile, :]
        for r in some:
            grad = dot(v_turned[r, t : t + tile, :], scales[jb, r], ((1,), (0,)))
            grad = grad * weights[jb % 2, r, t : t + tile, :].astype(jnp.float32)
            added = added + grad
            grads[jb % 2, r, t : t + tile, :] = grad.astype(jnp.bfloat16)
        total[jb, t : t + tile, :] = added

    def query_grad(jb, r):
        dq_s[r, jb] = (dot(k_s[r, :c, :], grads[jb % 2, r], ((1,), (0,))) * scaling).astype(jnp.bfloat16)

    def add_to(at, r, jb, part):
        if jb:
            part = part + dkv[r, at : at + c, :]
        dkv[r, at : at + c, :] = part

    def key_grad(jb, r):
        add_to(0, r, jb, dot(q_s[r, jb, :c, :], grads[jb % 2, r], ((1,), (1,))))

    def value_grad(jb, r):
        add_to(c, r, jb, dot(scaled[jb, r], weights[jb % 2, r], ((1,), (1,))))

    def each(step, jb, *ranges):
        if not 0 <= jb < n_col:
            return []
        return [functools.partial(step, jb, *at) for at in itertools.product(*ranges)]

    def finish(jb):
        return each(value_grad, jb, some) + each(query_grad, jb, some) + each(key_grad, jb, some)

    woven(each(score, 0, some, tiles))
    for jb in range(n_col):
        woven(each(expand, jb, some, tiles), finish(jb - 1))
        woven(each(attend, jb, some), each(score, jb + 1, some, tiles[: len(tiles) // 2]))
        woven(each(back, jb, tiles), each(score, jb + 1, some, tiles[len(tiles) // 2 :]))
    woven(finish(n_col - 1))

    for r in some:
        for step in range(n_col):
            jb = peer_of(me, step)
            span = pl.ds(pl.multiple_of(jb * blk, blk), blk)
            outs[step][rows_of(r, 0), :] = dq_s[r, jb]
            outs[step][rows_of(r, 1), :] = (dkv[r, :c, span] * (1.0 / LOG2E)).astype(jnp.bfloat16)
            outs[step][rows_of(r, 2), :] = dkv[r, c:, span].astype(jnp.bfloat16)
            outs[step][rows_of(r, 3), :] = at_s[r, jb]

    if last:

        @pl.when(pl.program_id(0) == pl.num_programs(0) - 1)
        def _():
            mine, others = totals
            pairs, _, width = mine.shape
            for pair in range(pairs):
                at = 2 * pair * width
                both = total[at // blk, :, at % blk : at % blk + 2 * width].astype(jnp.bfloat16)
                even, odd = both[:, :width], both[:, width:]
                place = peer_of(level, pair)
                mine[place] = jnp.where(side == 0, even, odd)
                others[place] = jnp.where(side == 0, odd, even)


def hold_kernel(*refs):
    pass


def params(mib):
    return pltpu.CompilerParams(
        dimension_semantics=("arbitrary",), vmem_limit_bytes=mib * 1024 * 1024
    )


def on_device(n_row, n_col, query, key, value, gate, d_out, bias, length):
    rows, blk, channels = query.shape
    heads, _, n = bias.shape
    c = channels // heads
    groups = n_col // heads
    share = rows // groups
    sizes = [share * weight // sum(SHARES) for weight in SHARES]
    starts = [sizes[-1] + sum(sizes[:m]) for m in range(len(sizes) - 1)] + [0]
    assert groups * heads == n_col and n == n_col * blk and groups * sum(sizes) == rows
    scaling = c ** (-0.5)
    per = 2 if all(size % 2 == 0 for size in sizes) else 1
    split_rows = (groups, share, blk, channels)
    query, key, value, gate, d_out = (x.reshape(split_rows) for x in (query, key, value, gate, d_out))
    row = lax.axis_index("row")
    info = jnp.stack([length[0], lax.axis_index("col"), row % 2, row // 2]).astype(jnp.int32)
    width = n // n_row
    lines = PIECES * c
    chunks = len(sizes)

    untouched = pl.BlockSpec(memory_space=pl.ANY)

    def exchange(blocks):
        pairs = [[(a, a ^ step) for a in range(n_col)] for step in range(n_col)]
        return [blocks[0]] + [lax.ppermute(blocks[step], "col", pairs[step]) for step in range(1, n_col)]

    def swap(x):
        return lax.ppermute(x, "row", [(r, r ^ 1) for r in range(n_row)])

    def hold(blocks, until):
        count = len(blocks)
        return pl.pallas_call(
            hold_kernel,
            in_specs=[untouched] * (count + len(until)),
            out_specs=[untouched] * count,
            out_shape=[jax.ShapeDtypeStruct(x.shape, x.dtype) for x in blocks],
            input_output_aliases={a: a for a in range(count)},
            compiler_params=pltpu.CompilerParams(vmem_limit_bytes=1024 * 1024),
            name="hold",
        )(*blocks, *until)

    def call(kernel, name, flops, grid, operands, out_specs, out_shape, scratch, aliases):
        return pl.pallas_call(
            kernel,
            grid_spec=pltpu.PrefetchScalarGridSpec(
                num_scalar_prefetch=1,
                grid=(grid,),
                in_specs=[spec for spec, _ in operands],
                out_specs=out_specs,
                scratch_shapes=scratch,
            ),
            out_shape=out_shape,
            input_output_aliases=aliases,
            compiler_params=params({"pack": 60, "attend": 26, "unpack": 24}[name]),
            cost_estimate=pl.CostEstimate(flops=flops, bytes_accessed=1, transcendentals=0),
            name=name,
        )(info, *[x for _, x in operands])

    def still(*shape):
        return pl.BlockSpec(shape, lambda i, info: (0,) * len(shape), pipeline_mode=pl.Buffered(1))

    def part(size, skip):
        return pl.BlockSpec((size, blk), lambda i, info: (skip + i, 0))

    def rows_a_step(*counts):
        return max(step for step in range(1, 6) if all(count % step == 0 for count in counts))

    def rows_of(group):
        return starts[group[0]], sum(sizes[m] for m in group)

    def pack(group):
        with_bias = group[0] == 0
        start, count = rows_of(group)
        step = rows_a_step(start, count)
        assert not with_bias or step == count
        base = start // step
        whole = pl.BlockSpec((groups, step, blk, channels), lambda i, info: (0, base + i, 0, 0))
        ahead = [n] + [n // 2] * (n_col - 1) if with_bias else [0] * n_col
        size = count * lines
        operands = [(whole, x) for x in (query, key, value, gate, d_out)]
        if with_bias:
            operands.append((still(heads, blk, n), bias))
        return call(
            functools.partial(pack_kernel, heads, groups, with_bias),
            "pack",
            count * 10**6,
            count // step,
            operands,
            [part(x + step * lines, 0) for x in ahead],
            [jax.ShapeDtypeStruct((x + size, blk), jnp.bfloat16) for x in ahead],
            [pltpu.VMEM((groups, step, PIECES, channels, blk), jnp.bfloat16)],
            {},
        )

    def attend(m, total, bias_blocks, blocks, room):
        first, last = m == 0, m == chunks - 1

        def scratch(*shape, dtype=jnp.bfloat16):
            return pltpu.VMEM((per, *shape), dtype)

        operands = [(still(n if a == 0 else n // 2, blk), x) for a, x in enumerate(bias_blocks)]
        (inward,) = [group for group in INWARD if m in group]
        (outward,) = [group for group in OUTWARD if m in group]
        behind = sum(sizes[o] for o in inward if o < m) // per
        ahead = sum(sizes[o] for o in outward if o < m) // per
        for a, x in enumerate(blocks):
            skip = (n if a == 0 else n // 2) // (per * lines) if first else behind
            operands.append((part(per * lines, skip), x))
        square = (n_col, n, blk)
        aliases = {}
        if not first:
            operands.append((still(*square), total))
        if ahead:
            aliases |= {1 + len(operands) + a: a for a in range(n_col)}
            operands += [(untouched, x) for x in room]
        size = rows_of(outward)[1]
        out_shape = [jax.ShapeDtypeStruct((size * lines, blk), jnp.bfloat16)] * n_col
        if last:
            totals = [jax.ShapeDtypeStruct((n_row // 2, n, width), jnp.bfloat16)] * 2
        else:
            totals = [jax.ShapeDtypeStruct(square, jnp.float32)]
        deep = 4 * c
        result = call(
            functools.partial(attention_kernel, n_col, per, c, scaling, first, last),
            "attend",
            sizes[m] * 4 * 10**9,
            sizes[m] // per,
            operands,
            [part(per * lines, ahead)] * n_col
            + [still(*x.shape) for x in totals]
            + [still(8, 128)],
            out_shape + totals + [jax.ShapeDtypeStruct((8, 128), jnp.float32)],
            [
                pltpu.VMEM(square, jnp.float32),
                pltpu.VMEM(square if last else (8, 128), jnp.float32),
                scratch(n_col, deep, blk),
                scratch(n_col, c, blk),
                scratch(deep, n),
                scratch(deep, n),
                scratch(n, deep),
                scratch(n, deep),
                scratch(n_col, c, blk),
                scratch(n_col, c, blk),
                scratch(2 * c, n, dtype=jnp.float32),
                pltpu.VMEM((2, per, n, blk), jnp.float32),
                pltpu.VMEM((2, per, n, blk), jnp.bfloat16),
                pltpu.VMEM((2, per, n, blk), jnp.bfloat16),
            ],
            aliases,
        )
        return result[:n_col], result[n_col:-1], result[-1]

    def unpack(group, blocks, grads):
        start, count = rows_of(group)
        step = rows_a_step(start, count)
        base = start // step
        whole = pl.BlockSpec((groups, step, blk, channels), lambda i, info: (0, base + i, 0, 0))
        kept = [] if grads is None else list(grads)
        operands = [(whole, gate), (whole, d_out)]
        operands += [(part(step * lines, 0), x) for x in blocks]
        aliases = {1 + len(operands) + a: a for a in range(len(kept))}
        operands += [(untouched, x) for x in kept]
        return call(
            functools.partial(unpack_kernel, heads, groups),
            "unpack",
            1,
            count // step,
            operands,
            [whole] * 4 + [pl.BlockSpec((8, 128), lambda i, info: (0, 0))],
            [jax.ShapeDtypeStruct(query.shape, jnp.bfloat16)] * 4
            + [jax.ShapeDtypeStruct((8, 128), jnp.float32)],
            [pltpu.VMEM((groups, step, PIECES, channels, blk), jnp.bfloat16)],
            aliases,
        )

    packed = [pack(group) for group in INWARD]
    own, *fetched = exchange(packed[0])
    fetched = hold(fetched, [x[0] for x in packed[1:]])
    tables = [own, *fetched] + [swap(x) for x in fetched]
    arrived = {0: [own, *fetched]}

    totals, results, sent, done = [None], None, [], []
    for m in range(chunks):
        at = [m in group for group in INWARD].index(True)
        for ahead in range(at + 1, min(at + 2, len(INWARD) - 1) + 1):
            if ahead not in arrived and (ahead == 1 or m >= INWARD[ahead - 1][0]):
                until = arrived[ahead - 1][1:] + (done[m - 1 : m] if m else [])
                arrived[ahead] = exchange([packed[ahead][0], *hold(packed[ahead][1:], until)])
        results, totals, token = attend(m, totals[0], tables, arrived[at], results)
        done.append(token)
        if m in [group[-1] for group in OUTWARD]:
            sent.append(exchange(results))
    grads, tokens = None, []
    for group, blocks in zip(OUTWARD, sent):
        *grads, token = unpack(group, blocks, grads)
        tokens.append(token)

    mine, others = totals
    (others,) = hold([others], sent[0][1:])
    others = swap(others)
    total = mine[0].astype(jnp.float32) + others[0].astype(jnp.float32)
    for step in range(1, n_row // 2):
        share = mine[step].astype(jnp.float32) + others[step].astype(jnp.float32)
        pairs = [(r, r ^ (2 * step)) for r in range(n_row)]
        total += lax.ppermute(share.astype(jnp.bfloat16), "row", pairs).astype(jnp.float32)
    total = (total + tokens[-2][0, 0]).astype(jnp.bfloat16).reshape(n_col, blk, width)
    total = lax.all_to_all(total, "col", split_axis=0, concat_axis=0, tiled=True)
    total = jnp.sum(total.reshape(heads, groups, blk, width).astype(jnp.float32), axis=1)
    bias_grad = jnp.transpose(total, (0, 2, 1))
    d_query, d_key, d_value, d_gate = (x.reshape(rows, blk, channels) for x in grads)
    return d_query, d_key, d_value, d_gate, bias_grad


def solution(mesh):
    pair = P("row", "col", None)
    return jax.shard_map(
        functools.partial(on_device, mesh.shape["row"], mesh.shape["col"]),
        mesh=mesh,
        in_specs=(pair, pair, pair, pair, pair, P(None, "col", None), P()),
        out_specs=(pair, pair, pair, pair, P(None, "row", "col")),
        check_vma=False,
    )
```

```python
import functools
import itertools

import jax
import jax.numpy as jnp
from jax import lax
from jax.experimental import pallas as pl
from jax.experimental.pallas import tpu as pltpu
from jax.sharding import PartitionSpec as P

LOG2E = 1.4426950408889634
MASKED = -1e30
SHARES = (1, 2, 4, 5)
INWARD = ((0,), (1,), (2,), (3,))
OUTWARD = ((0, 1, 2), (3,))
PIECES = 4


def dot(a, b, dims):
    return lax.dot_general(a, b, (dims, ((), ())), preferred_element_type=jnp.float32)


def peer_of(me, step):
    return jnp.bitwise_xor(me, step)


def pack_kernel(heads, groups, with_bias, info, q_ref, k_ref, v_ref, g_ref, o_ref, *refs):
    n_col = heads * groups
    outs, turned = refs[-1 - n_col : -1], refs[-1]
    me = info[1]
    count, _, channels = q_ref.shape[1:]
    c = channels // heads
    lines = count * PIECES * c
    for i in range(count):
        for g in range(groups):
            gated = o_ref[g, i].astype(jnp.float32) * jax.nn.sigmoid(g_ref[g, i].astype(jnp.float32))
            pieces = (q_ref[g, i], k_ref[g, i], v_ref[g, i], gated.astype(jnp.bfloat16))
            for piece, x in enumerate(pieces):
                turned[g, i, piece] = x.T
        for step in range(n_col):
            peer = peer_of(me, step)
            head = pl.multiple_of(peer // groups * c, c)
            base = outs[step].shape[0] - lines
            for piece in range(PIECES):
                at = base + (i * PIECES + piece) * c
                outs[step][at : at + c, :] = turned[peer % groups, i, piece, pl.ds(head, c), :]
    if with_bias:
        for step in range(n_col):
            base = outs[step].shape[0] - lines
            keys = pl.ds(pl.multiple_of(info[2] * base, base), base) if step else slice(None)
            outs[step][:base, :] = refs[0][peer_of(me, step) // groups, :, keys].T


def unpack_kernel(heads, groups, info, g_ref, o_ref, *refs):
    n_col = heads * groups
    ins, (dq, dk, dv, dg, token, whole) = refs[:n_col], refs[-6:]
    token[...] = jnp.zeros_like(token)
    me = info[1]
    count, _, channels = g_ref.shape[1:]
    c = channels // heads
    for i in range(count):
        for step in range(n_col):
            peer = peer_of(me, step)
            head = pl.multiple_of(peer // groups * c, c)
            for piece in range(PIECES):
                at = (i * PIECES + piece) * c
                whole[peer % groups, i, piece, pl.ds(head, c), :] = ins[step][at : at + c, :]
        for g in range(groups):
            dq[g, i] = whole[g, i, 0].T
            dk[g, i] = whole[g, i, 1].T
            dv[g, i] = whole[g, i, 2].T
            attended = whole[g, i, 3].T.astype(jnp.float32)
            s = jax.nn.sigmoid(g_ref[g, i].astype(jnp.float32))
            dg[g, i] = (o_ref[g, i].astype(jnp.float32) * attended * s * (1.0 - s)).astype(jnp.bfloat16)


def woven(*queues):
    order = [(at / len(q), which, at) for which, q in enumerate(queues) for at in range(len(q))]
    for _, which, at in sorted(order):
        queues[which][at]()


def attention_kernel(n_col, together, c, scaling, first, last, info, *refs):
    bias_in, ins, refs = refs[: 2 * n_col - 1], refs[2 * n_col - 1 : 3 * n_col - 1], refs[3 * n_col - 1 :]
    scratch, refs = refs[-14:], refs[:-14]
    bias, total_s, q_s, g_s, k_s, v_s, k_turned, v_turned, dq_s, at_s, dkv, logits, weights, grads = scratch
    if not first:
        total_in = refs[0]
    *totals, token = refs[-3:] if last else refs[-2:]
    outs = refs[-n_col - len(totals) - 1 : -len(totals) - 1]
    total = total_s if last else totals[0]
    length, me, side, level = info[0], info[1], info[2], info[3]
    blk = ins[0].shape[1]
    n = n_col * blk
    tile = min(256, n)
    tiles = range(0, n, tile)
    deep = k_s.shape[1]
    some = range(together)

    @pl.when(pl.program_id(0) == 0)
    def _():
        token[...] = jnp.zeros_like(token)
        if first:
            total[...] = jnp.zeros_like(total)
        else:
            total[...] = total_in[...]
        half = n // 2
        bias[me] = bias_in[0][...].astype(jnp.float32) * LOG2E
        for step in range(1, n_col):
            for table, which in ((bias_in[step], side), (bias_in[n_col + step - 1], 1 - side)):
                keys = pl.ds(pl.multiple_of(which * half, half), half)
                bias[peer_of(me, step), keys, :] = table[...].astype(jnp.float32) * LOG2E
        rows = lax.broadcasted_iota(jnp.int32, (deep - 2 * c, n), 0)
        keys = lax.broadcasted_iota(jnp.int32, (deep - 2 * c, n), 1)
        mask = jnp.logical_and(rows == 0, keys >= length)
        for r in some:
            k_s[r, 2 * c :, :] = jnp.where(mask, MASKED, 0.0).astype(jnp.bfloat16)
            v_s[r, c:, :] = jnp.ones((deep - c, n), jnp.bfloat16)
            q_s[r, :, 2 * c :, :] = jnp.ones((n_col, deep - 2 * c, blk), jnp.bfloat16)

    def rows_of(r, piece):
        at = (r * PIECES + piece) * c
        return slice(at, at + c)

    for r in some:
        for step in range(n_col):
            jb = peer_of(me, step)
            span = pl.ds(pl.multiple_of(jb * blk, blk), blk)
            q = ins[step][rows_of(r, 0), :].astype(jnp.float32) * (scaling * LOG2E)
            high = q.astype(jnp.bfloat16)
            q_s[r, jb, :c, :] = high
            q_s[r, jb, c : 2 * c, :] = (q - high.astype(jnp.float32)).astype(jnp.bfloat16)
            k = ins[step][rows_of(r, 1), :]
            k_s[r, :c, span] = k
            k_s[r, c : 2 * c, span] = k
            v_s[r, :c, span] = ins[step][rows_of(r, 2), :]
            g_s[r, jb] = ins[step][rows_of(r, 3), :]
    for r in some:
        k_turned[r] = k_s[r].T
        v_turned[r] = v_s[r].T
    tops, scaled, scales = {}, {}, {}

    def score(jb, r, t):
        part = dot(k_turned[r, t : t + tile, :], q_s[r, jb], ((1,), (0,))) + bias[jb, t : t + tile, :]
        logits[jb % 2, r, t : t + tile, :] = part
        top = jnp.max(part.reshape(tile // 8, 8, blk), axis=0)
        tops[jb, r] = jnp.maximum(tops[jb, r], top) if t else top

    def expand(jb, r, t):
        if t == 0:
            tops[jb, r] = jnp.max(tops[jb, r], axis=0, keepdims=True)
        part = jnp.exp2(logits[jb % 2, r, t : t + tile, :] - tops[jb, r])
        weights[jb % 2, r, t : t + tile, :] = part.astype(jnp.bfloat16)

    def attend(jb, r):
        summed = dot(v_s[r, : c + 16, :], weights[jb % 2, r], ((1,), (0,)))
        inverse = 1.0 / summed[c : c + 1, :]
        attended = summed[:c, :] * inverse
        at_s[r, jb] = attended.astype(jnp.bfloat16)
        g = g_s[r, jb].astype(jnp.float32)
        row_dot = jnp.sum(g * attended, axis=0, keepdims=True) * (-inverse)
        high = row_dot.astype(jnp.bfloat16).astype(jnp.float32)
        rows = lax.broadcasted_iota(jnp.int32, (deep - c, blk), 0)
        tail = jnp.where(rows == 0, high, jnp.where(rows == 1, row_dot - high, 0.0))
        scaled[jb, r] = (g * inverse).astype(jnp.bfloat16)
        scales[jb, r] = jnp.concatenate([scaled[jb, r], tail.astype(jnp.bfloat16)], axis=0)

    def back(jb, t):
        added = total[jb, t : t + tile, :]
        for r in some:
            grad = dot(v_turned[r, t : t + tile, :], scales[jb, r], ((1,), (0,)))
            grad = grad * weights[jb % 2, r, t : t + tile, :].astype(jnp.float32)
            added = added + grad
            grads[jb % 2, r, t : t + tile, :] = grad.astype(jnp.bfloat16)
        total[jb, t : t + tile, :] = added

    def query_grad(jb, r):
        dq_s[r, jb] = (dot(k_s[r, :c, :], grads[jb % 2, r], ((1,), (0,))) * scaling).astype(jnp.bfloat16)

    def add_to(at, r, jb, part):
        if jb:
            part = part + dkv[r, at : at + c, :]
        dkv[r, at : at + c, :] = part

    def key_grad(jb, r):
        add_to(0, r, jb, dot(q_s[r, jb, :c, :], grads[jb % 2, r], ((1,), (1,))))

    def value_grad(jb, r):
        add_to(c, r, jb, dot(scaled[jb, r], weights[jb % 2, r], ((1,), (1,))))

    def each(step, jb, *ranges):
        if not 0 <= jb < n_col:
            return []
        return [functools.partial(step, jb, *at) for at in itertools.product(*ranges)]

    def finish(jb):
        return each(value_grad, jb, some) + each(query_grad, jb, some) + each(key_grad, jb, some)

    woven(each(score, 0, some, tiles))
    for jb in range(n_col):
        woven(each(expand, jb, some, tiles), finish(jb - 1))
        woven(each(attend, jb, some), each(score, jb + 1, some, tiles[: len(tiles) // 2]))
        woven(each(back, jb, tiles), each(score, jb + 1, some, tiles[len(tiles) // 2 :]))
    woven(finish(n_col - 1))

    for r in some:
        for step in range(n_col):
            jb = peer_of(me, step)
            span = pl.ds(pl.multiple_of(jb * blk, blk), blk)
            outs[step][rows_of(r, 0), :] = dq_s[r, jb]
            outs[step][rows_of(r, 1), :] = (dkv[r, :c, span] * (1.0 / LOG2E)).astype(jnp.bfloat16)
            outs[step][rows_of(r, 2), :] = dkv[r, c:, span].astype(jnp.bfloat16)
            outs[step][rows_of(r, 3), :] = at_s[r, jb]

    if last:

        @pl.when(pl.program_id(0) == pl.num_programs(0) - 1)
        def _():
            mine, others = totals
            pairs, _, width = mine.shape
            for pair in range(pairs):
                at = 2 * pair * width
                both = total[at // blk, :, at % blk : at % blk + 2 * width].astype(jnp.bfloat16)
                even, odd = both[:, :width], both[:, width:]
                place = peer_of(level, pair)
                mine[place] = jnp.where(side == 0, even, odd)
                others[place] = jnp.where(side == 0, odd, even)


def hold_kernel(*refs):
    pass


def params(mib):
    return pltpu.CompilerParams(
        dimension_semantics=("arbitrary",), vmem_limit_bytes=mib * 1024 * 1024
    )


def on_device(n_row, n_col, query, key, value, gate, d_out, bias, length):
    rows, blk, channels = query.shape
    heads, _, n = bias.shape
    c = channels // heads
    groups = n_col // heads
    share = rows // groups
    sizes = [share * weight // sum(SHARES) for weight in SHARES]
    starts = [sizes[-1] + sum(sizes[:m]) for m in range(len(sizes) - 1)] + [0]
    assert groups * heads == n_col and n == n_col * blk and groups * sum(sizes) == rows
    scaling = c ** (-0.5)
    per = 2 if all(size % 2 == 0 for size in sizes) else 1
    split_rows = (groups, share, blk, channels)
    query, key, value, gate, d_out = (x.reshape(split_rows) for x in (query, key, value, gate, d_out))
    row = lax.axis_index("row")
    info = jnp.stack([length[0], lax.axis_index("col"), row % 2, row // 2]).astype(jnp.int32)
    width = n // n_row
    lines = PIECES * c
    chunks = len(sizes)

    untouched = pl.BlockSpec(memory_space=pl.ANY)

    def exchange(blocks):
        pairs = [[(a, a ^ step) for a in range(n_col)] for step in range(n_col)]
        return [blocks[0]] + [lax.ppermute(blocks[step], "col", pairs[step]) for step in range(1, n_col)]

    def swap(x):
        return lax.ppermute(x, "row", [(r, r ^ 1) for r in range(n_row)])

    def hold(blocks, until):
        count = len(blocks)
        return pl.pallas_call(
            hold_kernel,
            in_specs=[untouched] * (count + len(until)),
            out_specs=[untouched] * count,
            out_shape=[jax.ShapeDtypeStruct(x.shape, x.dtype) for x in blocks],
            input_output_aliases={a: a for a in range(count)},
            compiler_params=pltpu.CompilerParams(vmem_limit_bytes=1024 * 1024),
            name="hold",
        )(*blocks, *until)

    def call(kernel, name, flops, grid, operands, out_specs, out_shape, scratch, aliases):
        return pl.pallas_call(
            kernel,
            grid_spec=pltpu.PrefetchScalarGridSpec(
                num_scalar_prefetch=1,
                grid=(grid,),
                in_specs=[spec for spec, _ in operands],
                out_specs=out_specs,
                scratch_shapes=scratch,
            ),
            out_shape=out_shape,
            input_output_aliases=aliases,
            compiler_params=params({"pack": 60, "attend": 26, "unpack": 24}[name]),
            cost_estimate=pl.CostEstimate(flops=flops, bytes_accessed=1, transcendentals=0),
            name=name,
        )(info, *[x for _, x in operands])

    def still(*shape):
        return pl.BlockSpec(shape, lambda i, info: (0,) * len(shape), pipeline_mode=pl.Buffered(1))

    def part(size, skip):
        return pl.BlockSpec((size, blk), lambda i, info: (skip + i, 0))

    def rows_a_step(*counts):
        return max(step for step in range(1, 6) if all(count % step == 0 for count in counts))

    def rows_of(group):
        return starts[group[0]], sum(sizes[m] for m in group)

    def pack(group):
        with_bias = group[0] == 0
        start, count = rows_of(group)
        step = rows_a_step(start, count)
        assert not with_bias or step == count
        base = start // step
        whole = pl.BlockSpec((groups, step, blk, channels), lambda i, info: (0, base + i, 0, 0))
        ahead = [n] + [n // 2] * (n_col - 1) if with_bias else [0] * n_col
        size = count * lines
        operands = [(whole, x) for x in (query, key, value, gate, d_out)]
        if with_bias:
            operands.append((still(heads, blk, n), bias))
        return call(
            functools.partial(pack_kernel, heads, groups, with_bias),
            "pack",
            count * 10**6,
            count // step,
            operands,
            [part(x + step * lines, 0) for x in ahead],
            [jax.ShapeDtypeStruct((x + size, blk), jnp.bfloat16) for x in ahead],
            [pltpu.VMEM((groups, step, PIECES, channels, blk), jnp.bfloat16)],
            {},
        )

    def attend(m, total, bias_blocks, blocks, room):
        first, last = m == 0, m == chunks - 1

        def scratch(*shape, dtype=jnp.bfloat16):
            return pltpu.VMEM((per, *shape), dtype)

        operands = [(still(n if a == 0 else n // 2, blk), x) for a, x in enumerate(bias_blocks)]
        (inward,) = [group for group in INWARD if m in group]
        (outward,) = [group for group in OUTWARD if m in group]
        behind = sum(sizes[o] for o in inward if o < m) // per
        ahead = sum(sizes[o] for o in outward if o < m) // per
        for a, x in enumerate(blocks):
            skip = (n if a == 0 else n // 2) // (per * lines) if first else behind
            operands.append((part(per * lines, skip), x))
        square = (n_col, n, blk)
        aliases = {}
        if not first:
            operands.append((still(*square), total))
        if ahead:
            aliases |= {1 + len(operands) + a: a for a in range(n_col)}
            operands += [(untouched, x) for x in room]
        size = rows_of(outward)[1]
        out_shape = [jax.ShapeDtypeStruct((size * lines, blk), jnp.bfloat16)] * n_col
        if last:
            totals = [jax.ShapeDtypeStruct((n_row // 2, n, width), jnp.bfloat16)] * 2
        else:
            totals = [jax.ShapeDtypeStruct(square, jnp.float32)]
        deep = 4 * c
        result = call(
            functools.partial(attention_kernel, n_col, per, c, scaling, first, last),
            "attend",
            sizes[m] * 4 * 10**9,
            sizes[m] // per,
            operands,
            [part(per * lines, ahead)] * n_col
            + [still(*x.shape) for x in totals]
            + [still(8, 128)],
            out_shape + totals + [jax.ShapeDtypeStruct((8, 128), jnp.float32)],
            [
                pltpu.VMEM(square, jnp.float32),
                pltpu.VMEM(square if last else (8, 128), jnp.float32),
                scratch(n_col, deep, blk),
                scratch(n_col, c, blk),
                scratch(deep, n),
                scratch(deep, n),
                scratch(n, deep),
                scratch(n, deep),
                scratch(n_col, c, blk),
                scratch(n_col, c, blk),
                scratch(2 * c, n, dtype=jnp.float32),
                pltpu.VMEM((2, per, n, blk), jnp.float32),
                pltpu.VMEM((2, per, n, blk), jnp.bfloat16),
                pltpu.VMEM((2, per, n, blk), jnp.bfloat16),
            ],
            aliases,
        )
        return result[:n_col], result[n_col:-1], result[-1]

    def unpack(group, blocks, grads):
        start, count = rows_of(group)
        step = rows_a_step(start, count)
        base = start // step
        whole = pl.BlockSpec((groups, step, blk, channels), lambda i, info: (0, base + i, 0, 0))
        kept = [] if grads is None else list(grads)
        operands = [(whole, gate), (whole, d_out)]
        operands += [(part(step * lines, 0), x) for x in blocks]
        aliases = {1 + len(operands) + a: a for a in range(len(kept))}
        operands += [(untouched, x) for x in kept]
        return call(
            functools.partial(unpack_kernel, heads, groups),
            "unpack",
            1,
            count // step,
            operands,
            [whole] * 4 + [pl.BlockSpec((8, 128), lambda i, info: (0, 0))],
            [jax.ShapeDtypeStruct(query.shape, jnp.bfloat16)] * 4
            + [jax.ShapeDtypeStruct((8, 128), jnp.float32)],
            [pltpu.VMEM((groups, step, PIECES, channels, blk), jnp.bfloat16)],
            aliases,
        )

    packed = [pack(group) for group in INWARD]
    own, *fetched = exchange(packed[0])
    fetched = hold(fetched, [x[0] for x in packed[1:]])
    tables = [own, *fetched] + [swap(x) for x in fetched]
    arrived = {0: [own, *fetched]}

    totals, results, sent, done = [None], None, [], []
    for m in range(chunks):
        at = [m in group for group in INWARD].index(True)
        for ahead in range(at + 1, min(at + 2, len(INWARD) - 1) + 1):
            if ahead not in arrived and (ahead == 1 or m >= INWARD[ahead - 1][0]):
                until = arrived[ahead - 1][1:] + (done[m - 1 : m] if m else [])
                arrived[ahead] = exchange([packed[ahead][0], *hold(packed[ahead][1:], until)])
        results, totals, token = attend(m, totals[0], tables, arrived[at], results)
        done.append(token)
        if m in [group[-1] for group in OUTWARD]:
            sent.append(exchange(results))
    grads, tokens = None, []
    for group, blocks in zip(OUTWARD, sent):
        *grads, token = unpack(group, blocks, grads)
        tokens.append(token)

    mine, others = totals
    (others,) = hold([others], sent[0][1:])
    others = swap(others)
    total = mine[0].astype(jnp.float32) + others[0].astype(jnp.float32)
    for step in range(1, n_row // 2):
        share = mine[step].astype(jnp.float32) + others[step].astype(jnp.float32)
        pairs = [(r, r ^ (2 * step)) for r in range(n_row)]
        total += lax.ppermute(share.astype(jnp.bfloat16), "row", pairs).astype(jnp.float32)
    total = (total + tokens[-2][0, 0]).astype(jnp.bfloat16).reshape(n_col, blk, width)
    (total,) = hold([total], sent[-1][1:])
    total = lax.all_to_all(total, "col", split_axis=0, concat_axis=0, tiled=True)
    total = jnp.sum(total.reshape(heads, groups, blk, width).astype(jnp.float32), axis=1)
    bias_grad = jnp.transpose(total, (0, 2, 1))
    d_query, d_key, d_value, d_gate = (x.reshape(rows, blk, channels) for x in grads)
    return d_query, d_key, d_value, d_gate, bias_grad


def solution(mesh):
    pair = P("row", "col", None)
    return jax.shard_map(
        functools.partial(on_device, mesh.shape["row"], mesh.shape["col"]),
        mesh=mesh,
        in_specs=(pair, pair, pair, pair, pair, P(None, "col", None), P()),
        out_specs=(pair, pair, pair, pair, P(None, "row", "col")),
        check_vma=False,
    )
```

```python
import functools
import itertools

import jax
import jax.numpy as jnp
from jax import lax
from jax.experimental import pallas as pl
from jax.experimental.pallas import tpu as pltpu
from jax.sharding import PartitionSpec as P

LOG2E = 1.4426950408889634
MASKED = -1e30
SHARES = (1, 2, 4, 5)
INWARD = ((0,), (1,), (2,), (3,))
OUTWARD = ((0, 1, 2), (3,))
PIECES = 4


def dot(a, b, dims):
    return lax.dot_general(a, b, (dims, ((), ())), preferred_element_type=jnp.float32)


def peer_of(me, step):
    return jnp.bitwise_xor(me, step)


def pack_kernel(heads, groups, with_bias, info, q_ref, k_ref, v_ref, g_ref, o_ref, *refs):
    n_col = heads * groups
    outs, turned = refs[-1 - n_col : -1], refs[-1]
    me = info[1]
    count, _, channels = q_ref.shape[1:]
    c = channels // heads
    lines = count * PIECES * c
    for i in range(count):
        for g in range(groups):
            gated = o_ref[g, i].astype(jnp.float32) * jax.nn.sigmoid(g_ref[g, i].astype(jnp.float32))
            pieces = (q_ref[g, i], k_ref[g, i], v_ref[g, i], gated.astype(jnp.bfloat16))
            for piece, x in enumerate(pieces):
                turned[g, i, piece] = x.T
        for step in range(n_col):
            peer = peer_of(me, step)
            head = pl.multiple_of(peer // groups * c, c)
            base = outs[step].shape[0] - lines
            for piece in range(PIECES):
                at = base + (i * PIECES + piece) * c
                outs[step][at : at + c, :] = turned[peer % groups, i, piece, pl.ds(head, c), :]
    if with_bias:
        for step in range(n_col):
            base = outs[step].shape[0] - lines
            keys = pl.ds(pl.multiple_of(info[2] * base, base), base) if step else slice(None)
            outs[step][:base, :] = refs[0][peer_of(me, step) // groups, :, keys].T


def unpack_kernel(heads, groups, info, g_ref, o_ref, *refs):
    n_col = heads * groups
    ins, (dq, dk, dv, dg, token, whole) = refs[:n_col], refs[-6:]
    token[...] = jnp.zeros_like(token)
    me = info[1]
    count, _, channels = g_ref.shape[1:]
    c = channels // heads
    for i in range(count):
        for step in range(n_col):
            peer = peer_of(me, step)
            head = pl.multiple_of(peer // groups * c, c)
            for piece in range(PIECES):
                at = (i * PIECES + piece) * c
                whole[peer % groups, i, piece, pl.ds(head, c), :] = ins[step][at : at + c, :]
        for g in range(groups):
            dq[g, i] = whole[g, i, 0].T
            dk[g, i] = whole[g, i, 1].T
            dv[g, i] = whole[g, i, 2].T
            attended = whole[g, i, 3].T.astype(jnp.float32)
            s = jax.nn.sigmoid(g_ref[g, i].astype(jnp.float32))
            dg[g, i] = (o_ref[g, i].astype(jnp.float32) * attended * s * (1.0 - s)).astype(jnp.bfloat16)


def woven(*queues):
    order = [(at / len(q), which, at) for which, q in enumerate(queues) for at in range(len(q))]
    for _, which, at in sorted(order):
        queues[which][at]()


def attention_kernel(n_col, together, c, scaling, first, last, info, *refs):
    bias_in, ins, refs = refs[: 2 * n_col - 1], refs[2 * n_col - 1 : 3 * n_col - 1], refs[3 * n_col - 1 :]
    scratch, refs = refs[-14:], refs[:-14]
    bias, total_s, q_s, g_s, k_s, v_s, k_turned, v_turned, dq_s, at_s, dkv, logits, weights, grads = scratch
    if not first:
        total_in = refs[0]
    *totals, token = refs[-3:] if last else refs[-2:]
    outs = refs[-n_col - len(totals) - 1 : -len(totals) - 1]
    total = total_s if last else totals[0]
    length, me, side, level = info[0], info[1], info[2], info[3]
    blk = ins[0].shape[1]
    n = n_col * blk
    tile = min(512, n)
    tiles = range(0, n, tile)
    deep = k_s.shape[1]
    some = range(together)

    @pl.when(pl.program_id(0) == 0)
    def _():
        token[...] = jnp.zeros_like(token)
        if first:
            total[...] = jnp.zeros_like(total)
        else:
            total[...] = total_in[...]
        half = n // 2
        bias[me] = bias_in[0][...].astype(jnp.float32) * LOG2E
        for step in range(1, n_col):
            for table, which in ((bias_in[step], side), (bias_in[n_col + step - 1], 1 - side)):
                keys = pl.ds(pl.multiple_of(which * half, half), half)
                bias[peer_of(me, step), keys, :] = table[...].astype(jnp.float32) * LOG2E
        rows = lax.broadcasted_iota(jnp.int32, (deep - 2 * c, n), 0)
        keys = lax.broadcasted_iota(jnp.int32, (deep - 2 * c, n), 1)
        mask = jnp.logical_and(rows == 0, keys >= length)
        for r in some:
            k_s[r, 2 * c :, :] = jnp.where(mask, MASKED, 0.0).astype(jnp.bfloat16)
            v_s[r, c:, :] = jnp.ones((deep - c, n), jnp.bfloat16)
            q_s[r, :, 2 * c :, :] = jnp.ones((n_col, deep - 2 * c, blk), jnp.bfloat16)

    def rows_of(r, piece):
        at = (r * PIECES + piece) * c
        return slice(at, at + c)

    for r in some:
        for step in range(n_col):
            jb = peer_of(me, step)
            span = pl.ds(pl.multiple_of(jb * blk, blk), blk)
            q = ins[step][rows_of(r, 0), :].astype(jnp.float32) * (scaling * LOG2E)
            high = q.astype(jnp.bfloat16)
            q_s[r, jb, :c, :] = high
            q_s[r, jb, c : 2 * c, :] = (q - high.astype(jnp.float32)).astype(jnp.bfloat16)
            k = ins[step][rows_of(r, 1), :]
            k_s[r, :c, span] = k
            k_s[r, c : 2 * c, span] = k
            v_s[r, :c, span] = ins[step][rows_of(r, 2), :]
            g_s[r, jb] = ins[step][rows_of(r, 3), :]
    for r in some:
        k_turned[r] = k_s[r].T
        v_turned[r] = v_s[r].T
    tops, scaled, scales = {}, {}, {}

    def score(jb, r, t):
        part = dot(k_turned[r, t : t + tile, :], q_s[r, jb], ((1,), (0,))) + bias[jb, t : t + tile, :]
        logits[jb % 2, r, t : t + tile, :] = part
        top = jnp.max(part.reshape(tile // 8, 8, blk), axis=0)
        tops[jb, r] = jnp.maximum(tops[jb, r], top) if t else top

    def expand(jb, r, t):
        if t == 0:
            tops[jb, r] = jnp.max(tops[jb, r], axis=0, keepdims=True)
        part = jnp.exp2(logits[jb % 2, r, t : t + tile, :] - tops[jb, r])
        weights[jb % 2, r, t : t + tile, :] = part.astype(jnp.bfloat16)

    def attend(jb, r):
        summed = dot(v_s[r, : c + 16, :], weights[jb % 2, r], ((1,), (0,)))
        inverse = 1.0 / summed[c : c + 1, :]
        attended = summed[:c, :] * inverse
        at_s[r, jb] = attended.astype(jnp.bfloat16)
        g = g_s[r, jb].astype(jnp.float32)
        row_dot = jnp.sum(g * attended, axis=0, keepdims=True) * (-inverse)
        high = row_dot.astype(jnp.bfloat16).astype(jnp.float32)
        rows = lax.broadcasted_iota(jnp.int32, (deep - c, blk), 0)
        tail = jnp.where(rows == 0, high, jnp.where(rows == 1, row_dot - high, 0.0))
        scaled[jb, r] = (g * inverse).astype(jnp.bfloat16)
        scales[jb, r] = jnp.concatenate([scaled[jb, r], tail.astype(jnp.bfloat16)], axis=0)

    def back(jb, t):
        added = total[jb, t : t + tile, :]
        for r in some:
            grad = dot(v_turned[r, t : t + tile, :], scales[jb, r], ((1,), (0,)))
            grad = grad * weights[jb % 2, r, t : t + tile, :].astype(jnp.float32)
            added = added + grad
            grads[jb % 2, r, t : t + tile, :] = grad.astype(jnp.bfloat16)
        total[jb, t : t + tile, :] = added

    def query_grad(jb, r):
        dq_s[r, jb] = (dot(k_s[r, :c, :], grads[jb % 2, r], ((1,), (0,))) * scaling).astype(jnp.bfloat16)

    def add_to(at, r, jb, part):
        if jb:
            part = part + dkv[r, at : at + c, :]
        dkv[r, at : at + c, :] = part

    def key_grad(jb, r):
        add_to(0, r, jb, dot(q_s[r, jb, :c, :], grads[jb % 2, r], ((1,), (1,))))

    def value_grad(jb, r):
        add_to(c, r, jb, dot(scaled[jb, r], weights[jb % 2, r], ((1,), (1,))))

    def each(step, jb, *ranges):
        if not 0 <= jb < n_col:
            return []
        return [functools.partial(step, jb, *at) for at in itertools.product(*ranges)]

    def finish(jb):
        return each(value_grad, jb, some) + each(query_grad, jb, some) + each(key_grad, jb, some)

    woven(each(score, 0, some, tiles))
    for jb in range(n_col):
        woven(each(expand, jb, some, tiles), finish(jb - 1))
        woven(each(attend, jb, some), each(score, jb + 1, some, tiles[: len(tiles) // 2]))
        woven(each(back, jb, tiles), each(score, jb + 1, some, tiles[len(tiles) // 2 :]))
    woven(finish(n_col - 1))

    for r in some:
        for step in range(n_col):
            jb = peer_of(me, step)
            span = pl.ds(pl.multiple_of(jb * blk, blk), blk)
            outs[step][rows_of(r, 0), :] = dq_s[r, jb]
            outs[step][rows_of(r, 1), :] = (dkv[r, :c, span] * (1.0 / LOG2E)).astype(jnp.bfloat16)
            outs[step][rows_of(r, 2), :] = dkv[r, c:, span].astype(jnp.bfloat16)
            outs[step][rows_of(r, 3), :] = at_s[r, jb]

    if last:

        @pl.when(pl.program_id(0) == pl.num_programs(0) - 1)
        def _():
            mine, others = totals
            pairs, _, width = mine.shape
            for pair in range(pairs):
                at = 2 * pair * width
                both = total[at // blk, :, at % blk : at % blk + 2 * width].astype(jnp.bfloat16)
                even, odd = both[:, :width], both[:, width:]
                place = peer_of(level, pair)
                mine[place] = jnp.where(side == 0, even, odd)
                others[place] = jnp.where(side == 0, odd, even)


def hold_kernel(*refs):
    pass


def params(mib):
    return pltpu.CompilerParams(
        dimension_semantics=("arbitrary",), vmem_limit_bytes=mib * 1024 * 1024
    )


def on_device(n_row, n_col, query, key, value, gate, d_out, bias, length):
    rows, blk, channels = query.shape
    heads, _, n = bias.shape
    c = channels // heads
    groups = n_col // heads
    share = rows // groups
    sizes = [share * weight // sum(SHARES) for weight in SHARES]
    starts = [sizes[-1] + sum(sizes[:m]) for m in range(len(sizes) - 1)] + [0]
    assert groups * heads == n_col and n == n_col * blk and groups * sum(sizes) == rows
    scaling = c ** (-0.5)
    per = 2 if all(size % 2 == 0 for size in sizes) else 1
    split_rows = (groups, share, blk, channels)
    query, key, value, gate, d_out = (x.reshape(split_rows) for x in (query, key, value, gate, d_out))
    row = lax.axis_index("row")
    info = jnp.stack([length[0], lax.axis_index("col"), row % 2, row // 2]).astype(jnp.int32)
    width = n // n_row
    lines = PIECES * c
    chunks = len(sizes)

    untouched = pl.BlockSpec(memory_space=pl.ANY)

    def exchange(blocks):
        pairs = [[(a, a ^ step) for a in range(n_col)] for step in range(n_col)]
        return [blocks[0]] + [lax.ppermute(blocks[step], "col", pairs[step]) for step in range(1, n_col)]

    def swap(x):
        return lax.ppermute(x, "row", [(r, r ^ 1) for r in range(n_row)])

    def hold(blocks, until):
        count = len(blocks)
        return pl.pallas_call(
            hold_kernel,
            in_specs=[untouched] * (count + len(until)),
            out_specs=[untouched] * count,
            out_shape=[jax.ShapeDtypeStruct(x.shape, x.dtype) for x in blocks],
            input_output_aliases={a: a for a in range(count)},
            compiler_params=pltpu.CompilerParams(vmem_limit_bytes=1024 * 1024),
            name="hold",
        )(*blocks, *until)

    def call(kernel, name, flops, grid, operands, out_specs, out_shape, scratch, aliases):
        return pl.pallas_call(
            kernel,
            grid_spec=pltpu.PrefetchScalarGridSpec(
                num_scalar_prefetch=1,
                grid=(grid,),
                in_specs=[spec for spec, _ in operands],
                out_specs=out_specs,
                scratch_shapes=scratch,
            ),
            out_shape=out_shape,
            input_output_aliases=aliases,
            compiler_params=params({"pack": 60, "attend": 26, "unpack": 24}[name]),
            cost_estimate=pl.CostEstimate(flops=flops, bytes_accessed=1, transcendentals=0),
            name=name,
        )(info, *[x for _, x in operands])

    def still(*shape):
        return pl.BlockSpec(shape, lambda i, info: (0,) * len(shape), pipeline_mode=pl.Buffered(1))

    def part(size, skip):
        return pl.BlockSpec((size, blk), lambda i, info: (skip + i, 0))

    def rows_a_step(*counts):
        return max(step for step in range(1, 6) if all(count % step == 0 for count in counts))

    def rows_of(group):
        return starts[group[0]], sum(sizes[m] for m in group)

    def pack(group):
        with_bias = group[0] == 0
        start, count = rows_of(group)
        step = rows_a_step(start, count)
        assert not with_bias or step == count
        base = start // step
        whole = pl.BlockSpec((groups, step, blk, channels), lambda i, info: (0, base + i, 0, 0))
        ahead = [n] + [n // 2] * (n_col - 1) if with_bias else [0] * n_col
        size = count * lines
        operands = [(whole, x) for x in (query, key, value, gate, d_out)]
        if with_bias:
            operands.append((still(heads, blk, n), bias))
        return call(
            functools.partial(pack_kernel, heads, groups, with_bias),
            "pack",
            count * 10**6,
            count // step,
            operands,
            [part(x + step * lines, 0) for x in ahead],
            [jax.ShapeDtypeStruct((x + size, blk), jnp.bfloat16) for x in ahead],
            [pltpu.VMEM((groups, step, PIECES, channels, blk), jnp.bfloat16)],
            {},
        )

    def attend(m, total, bias_blocks, blocks, room):
        first, last = m == 0, m == chunks - 1

        def scratch(*shape, dtype=jnp.bfloat16):
            return pltpu.VMEM((per, *shape), dtype)

        operands = [(still(n if a == 0 else n // 2, blk), x) for a, x in enumerate(bias_blocks)]
        (inward,) = [group for group in INWARD if m in group]
        (outward,) = [group for group in OUTWARD if m in group]
        behind = sum(sizes[o] for o in inward if o < m) // per
        ahead = sum(sizes[o] for o in outward if o < m) // per
        for a, x in enumerate(blocks):
            skip = (n if a == 0 else n // 2) // (per * lines) if first else behind
            operands.append((part(per * lines, skip), x))
        square = (n_col, n, blk)
        aliases = {}
        if not first:
            operands.append((still(*square), total))
        if ahead:
            aliases |= {1 + len(operands) + a: a for a in range(n_col)}
            operands += [(untouched, x) for x in room]
        size = rows_of(outward)[1]
        out_shape = [jax.ShapeDtypeStruct((size * lines, blk), jnp.bfloat16)] * n_col
        if last:
            totals = [jax.ShapeDtypeStruct((n_row // 2, n, width), jnp.bfloat16)] * 2
        else:
            totals = [jax.ShapeDtypeStruct(square, jnp.float32)]
        deep = 4 * c
        result = call(
            functools.partial(attention_kernel, n_col, per, c, scaling, first, last),
            "attend",
            sizes[m] * 4 * 10**9,
            sizes[m] // per,
            operands,
            [part(per * lines, ahead)] * n_col
            + [still(*x.shape) for x in totals]
            + [still(8, 128)],
            out_shape + totals + [jax.ShapeDtypeStruct((8, 128), jnp.float32)],
            [
                pltpu.VMEM(square, jnp.float32),
                pltpu.VMEM(square if last else (8, 128), jnp.float32),
                scratch(n_col, deep, blk),
                scratch(n_col, c, blk),
                scratch(deep, n),
                scratch(deep, n),
                scratch(n, deep),
                scratch(n, deep),
                scratch(n_col, c, blk),
                scratch(n_col, c, blk),
                scratch(2 * c, n, dtype=jnp.float32),
                pltpu.VMEM((2, per, n, blk), jnp.float32),
                pltpu.VMEM((2, per, n, blk), jnp.bfloat16),
                pltpu.VMEM((2, per, n, blk), jnp.bfloat16),
            ],
            aliases,
        )
        return result[:n_col], result[n_col:-1], result[-1]

    def unpack(group, blocks, grads):
        start, count = rows_of(group)
        step = rows_a_step(start, count)
        base = start // step
        whole = pl.BlockSpec((groups, step, blk, channels), lambda i, info: (0, base + i, 0, 0))
        kept = [] if grads is None else list(grads)
        operands = [(whole, gate), (whole, d_out)]
        operands += [(part(step * lines, 0), x) for x in blocks]
        aliases = {1 + len(operands) + a: a for a in range(len(kept))}
        operands += [(untouched, x) for x in kept]
        return call(
            functools.partial(unpack_kernel, heads, groups),
            "unpack",
            1,
            count // step,
            operands,
            [whole] * 4 + [pl.BlockSpec((8, 128), lambda i, info: (0, 0))],
            [jax.ShapeDtypeStruct(query.shape, jnp.bfloat16)] * 4
            + [jax.ShapeDtypeStruct((8, 128), jnp.float32)],
            [pltpu.VMEM((groups, step, PIECES, channels, blk), jnp.bfloat16)],
            aliases,
        )

    packed = [pack(group) for group in INWARD]
    own, *fetched = exchange(packed[0])
    fetched = hold(fetched, [x[0] for x in packed[1:]])
    tables = [own, *fetched] + [swap(x) for x in fetched]
    arrived = {0: [own, *fetched]}

    totals, results, sent, done = [None], None, [], []
    for m in range(chunks):
        at = [m in group for group in INWARD].index(True)
        for ahead in range(at + 1, min(at + 2, len(INWARD) - 1) + 1):
            if ahead not in arrived and (ahead == 1 or m >= INWARD[ahead - 1][0]):
                until = arrived[ahead - 1][1:] + (done[m - 1 : m] if m else [])
                arrived[ahead] = exchange([packed[ahead][0], *hold(packed[ahead][1:], until)])
        results, totals, token = attend(m, totals[0], tables, arrived[at], results)
        done.append(token)
        if m in [group[-1] for group in OUTWARD]:
            sent.append(exchange(results))
    grads, tokens = None, []
    for group, blocks in zip(OUTWARD, sent):
        *grads, token = unpack(group, blocks, grads)
        tokens.append(token)

    mine, others = totals
    (others,) = hold([others], sent[0][1:])
    others = swap(others)
    total = mine[0].astype(jnp.float32) + others[0].astype(jnp.float32)
    for step in range(1, n_row // 2):
        share = mine[step].astype(jnp.float32) + others[step].astype(jnp.float32)
        pairs = [(r, r ^ (2 * step)) for r in range(n_row)]
        total += lax.ppermute(share.astype(jnp.bfloat16), "row", pairs).astype(jnp.float32)
    total = (total + tokens[-2][0, 0]).astype(jnp.bfloat16).reshape(n_col, blk, width)
    total = lax.all_to_all(total, "col", split_axis=0, concat_axis=0, tiled=True)
    total = jnp.sum(total.reshape(heads, groups, blk, width).astype(jnp.float32), axis=1)
    bias_grad = jnp.transpose(total, (0, 2, 1))
    d_query, d_key, d_value, d_gate = (x.reshape(rows, blk, channels) for x in grads)
    return d_query, d_key, d_value, d_gate, bias_grad


def solution(mesh):
    pair = P("row", "col", None)
    return jax.shard_map(
        functools.partial(on_device, mesh.shape["row"], mesh.shape["col"]),
        mesh=mesh,
        in_specs=(pair, pair, pair, pair, pair, P(None, "col", None), P()),
        out_specs=(pair, pair, pair, pair, P(None, "row", "col")),
        check_vma=False,
    )
```

```python
import functools
import itertools

import jax
import jax.numpy as jnp
from jax import lax
from jax.experimental import pallas as pl
from jax.experimental.pallas import tpu as pltpu
from jax.sharding import PartitionSpec as P

LOG2E = 1.4426950408889634
MASKED = -1e30
SHARES = (1, 2, 4, 5)
INWARD = ((0,), (1,), (2,), (3,))
OUTWARD = ((0, 1, 2), (3,))
PIECES = 4


def dot(a, b, dims):
    return lax.dot_general(a, b, (dims, ((), ())), preferred_element_type=jnp.float32)


def peer_of(me, step):
    return jnp.bitwise_xor(me, step)


def pack_kernel(heads, groups, with_bias, info, q_ref, k_ref, v_ref, g_ref, o_ref, *refs):
    n_col = heads * groups
    outs, turned = refs[-1 - n_col : -1], refs[-1]
    me = info[1]
    count, _, channels = q_ref.shape[1:]
    c = channels // heads
    lines = count * PIECES * c
    for i in range(count):
        for g in range(groups):
            gated = o_ref[g, i].astype(jnp.float32) * jax.nn.sigmoid(g_ref[g, i].astype(jnp.float32))
            pieces = (q_ref[g, i], k_ref[g, i], v_ref[g, i], gated.astype(jnp.bfloat16))
            for piece, x in enumerate(pieces):
                turned[g, i, piece] = x.T
        for step in range(n_col):
            peer = peer_of(me, step)
            head = pl.multiple_of(peer // groups * c, c)
            base = outs[step].shape[0] - lines
            for piece in range(PIECES):
                at = base + (i * PIECES + piece) * c
                outs[step][at : at + c, :] = turned[peer % groups, i, piece, pl.ds(head, c), :]
    if with_bias:
        for step in range(n_col):
            base = outs[step].shape[0] - lines
            keys = pl.ds(pl.multiple_of(info[2] * base, base), base) if step else slice(None)
            outs[step][:base, :] = refs[0][peer_of(me, step) // groups, :, keys].T


def unpack_kernel(heads, groups, info, g_ref, o_ref, *refs):
    n_col = heads * groups
    ins, (dq, dk, dv, dg, token, whole) = refs[:n_col], refs[-6:]
    token[...] = jnp.zeros_like(token)
    me = info[1]
    count, _, channels = g_ref.shape[1:]
    c = channels // heads
    for i in range(count):
        for step in range(n_col):
            peer = peer_of(me, step)
            head = pl.multiple_of(peer // groups * c, c)
            for piece in range(PIECES):
                at = (i * PIECES + piece) * c
                whole[peer % groups, i, piece, pl.ds(head, c), :] = ins[step][at : at + c, :]
        for g in range(groups):
            dq[g, i] = whole[g, i, 0].T
            dk[g, i] = whole[g, i, 1].T
            dv[g, i] = whole[g, i, 2].T
            attended = whole[g, i, 3].T.astype(jnp.float32)
            s = jax.nn.sigmoid(g_ref[g, i].astype(jnp.float32))
            dg[g, i] = (o_ref[g, i].astype(jnp.float32) * attended * s * (1.0 - s)).astype(jnp.bfloat16)


def woven(*queues):
    order = [(at / len(q), which, at) for which, q in enumerate(queues) for at in range(len(q))]
    for _, which, at in sorted(order):
        queues[which][at]()


def attention_kernel(n_col, together, c, scaling, first, last, info, *refs):
    bias_in, ins, refs = refs[: 2 * n_col - 1], refs[2 * n_col - 1 : 3 * n_col - 1], refs[3 * n_col - 1 :]
    scratch, refs = refs[-14:], refs[:-14]
    bias, total_s, q_s, g_s, k_s, v_s, k_turned, v_turned, dq_s, at_s, dkv, logits, weights, grads = scratch
    if not first:
        total_in = refs[0]
    *totals, token = refs[-3:] if last else refs[-2:]
    outs = refs[-n_col - len(totals) - 1 : -len(totals) - 1]
    total = total_s if last else totals[0]
    length, me, side, level = info[0], info[1], info[2], info[3]
    blk = ins[0].shape[1]
    n = n_col * blk
    tile = min(512, n)
    tiles = range(0, n, tile)
    deep = k_s.shape[1]
    some = range(together)

    @pl.when(pl.program_id(0) == 0)
    def _():
        token[...] = jnp.zeros_like(token)
        if first:
            total[...] = jnp.zeros_like(total)
        else:
            total[...] = total_in[...]
        half = n // 2
        bias[me] = bias_in[0][...].astype(jnp.float32) * LOG2E
        for step in range(1, n_col):
            for table, which in ((bias_in[step], side), (bias_in[n_col + step - 1], 1 - side)):
                keys = pl.ds(pl.multiple_of(which * half, half), half)
                bias[peer_of(me, step), keys, :] = table[...].astype(jnp.float32) * LOG2E
        rows = lax.broadcasted_iota(jnp.int32, (deep - 2 * c, n), 0)
        keys = lax.broadcasted_iota(jnp.int32, (deep - 2 * c, n), 1)
        mask = jnp.logical_and(rows == 0, keys >= length)
        for r in some:
            k_s[r, 2 * c :, :] = jnp.where(mask, MASKED, 0.0).astype(jnp.bfloat16)
            v_s[r, c:, :] = jnp.ones((deep - c, n), jnp.bfloat16)
            q_s[r, :, 2 * c :, :] = jnp.ones((n_col, deep - 2 * c, blk), jnp.bfloat16)

    def rows_of(r, piece):
        at = (r * PIECES + piece) * c
        return slice(at, at + c)

    for r in some:
        for step in range(n_col):
            jb = peer_of(me, step)
            span = pl.ds(pl.multiple_of(jb * blk, blk), blk)
            q = ins[step][rows_of(r, 0), :].astype(jnp.float32) * (scaling * LOG2E)
            high = q.astype(jnp.bfloat16)
            q_s[r, jb, :c, :] = high
            q_s[r, jb, c : 2 * c, :] = (q - high.astype(jnp.float32)).astype(jnp.bfloat16)
            k = ins[step][rows_of(r, 1), :]
            k_s[r, :c, span] = k
            k_s[r, c : 2 * c, span] = k
            v_s[r, :c, span] = ins[step][rows_of(r, 2), :]
            g_s[r, jb] = ins[step][rows_of(r, 3), :]
    for r in some:
        k_turned[r] = k_s[r].T
        v_turned[r] = v_s[r].T
    tops, scaled, scales = {}, {}, {}

    def score(jb, r, t):
        part = dot(k_turned[r, t : t + tile, :], q_s[r, jb], ((1,), (0,))) + bias[jb, t : t + tile, :]
        logits[jb % 2, r, t : t + tile, :] = part
        top = jnp.max(part.reshape(tile // 8, 8, blk), axis=0)
        tops[jb, r] = jnp.maximum(tops[jb, r], top) if t else top

    def expand(jb, r, t):
        if t == 0:
            tops[jb, r] = jnp.max(tops[jb, r], axis=0, keepdims=True)
        part = jnp.exp2(logits[jb % 2, r, t : t + tile, :] - tops[jb, r])
        weights[jb % 2, r, t : t + tile, :] = part.astype(jnp.bfloat16)

    def attend(jb, r):
        summed = dot(v_s[r, : c + 16, :], weights[jb % 2, r], ((1,), (0,)))
        inverse = 1.0 / summed[c : c + 1, :]
        attended = summed[:c, :] * inverse
        at_s[r, jb] = attended.astype(jnp.bfloat16)
        g = g_s[r, jb].astype(jnp.float32)
        row_dot = jnp.sum(g * attended, axis=0, keepdims=True) * (-inverse)
        high = row_dot.astype(jnp.bfloat16).astype(jnp.float32)
        rows = lax.broadcasted_iota(jnp.int32, (deep - c, blk), 0)
        tail = jnp.where(rows == 0, high, jnp.where(rows == 1, row_dot - high, 0.0))
        scaled[jb, r] = (g * inverse).astype(jnp.bfloat16)
        scales[jb, r] = jnp.concatenate([scaled[jb, r], tail.astype(jnp.bfloat16)], axis=0)

    def back(jb, t):
        added = total[jb, t : t + tile, :]
        for r in some:
            grad = dot(v_turned[r, t : t + tile, :], scales[jb, r], ((1,), (0,)))
            grad = grad * weights[jb % 2, r, t : t + tile, :].astype(jnp.float32)
            added = added + grad
            grads[jb % 2, r, t : t + tile, :] = grad.astype(jnp.bfloat16)
        total[jb, t : t + tile, :] = added

    def query_grad(jb, r):
        dq_s[r, jb] = (dot(k_s[r, :c, :], grads[jb % 2, r], ((1,), (0,))) * scaling).astype(jnp.bfloat16)

    def add_to(at, r, jb, part):
        if jb:
            part = part + dkv[r, at : at + c, :]
        dkv[r, at : at + c, :] = part

    def key_grad(jb, r):
        add_to(0, r, jb, dot(q_s[r, jb, :c, :], grads[jb % 2, r], ((1,), (1,))))

    def value_grad(jb, r):
        add_to(c, r, jb, dot(scaled[jb, r], weights[jb % 2, r], ((1,), (1,))))

    def each(step, jb, *ranges):
        if not 0 <= jb < n_col:
            return []
        return [functools.partial(step, jb, *at) for at in itertools.product(*ranges)]

    def finish(jb):
        return each(query_grad, jb, some) + each(key_grad, jb, some)

    early, late = tiles[: len(tiles) // 2], tiles[len(tiles) // 2 :]
    woven(each(score, 0, some, tiles))
    for jb in range(n_col):
        ahead = each(score, jb + 1, some, early)
        woven(each(expand, jb, some, tiles), finish(jb - 1) if jb else ahead)
        woven(each(attend, jb, some), ahead if jb else [])
        woven(each(back, jb, tiles), each(score, jb + 1, some, late), each(value_grad, jb, some))
    woven(finish(n_col - 1))

    for r in some:
        for step in range(n_col):
            jb = peer_of(me, step)
            span = pl.ds(pl.multiple_of(jb * blk, blk), blk)
            outs[step][rows_of(r, 0), :] = dq_s[r, jb]
            outs[step][rows_of(r, 1), :] = (dkv[r, :c, span] * (1.0 / LOG2E)).astype(jnp.bfloat16)
            outs[step][rows_of(r, 2), :] = dkv[r, c:, span].astype(jnp.bfloat16)
            outs[step][rows_of(r, 3), :] = at_s[r, jb]

    if last:

        @pl.when(pl.program_id(0) == pl.num_programs(0) - 1)
        def _():
            mine, others = totals
            pairs, _, width = mine.shape
            for pair in range(pairs):
                at = 2 * pair * width
                both = total[at // blk, :, at % blk : at % blk + 2 * width].astype(jnp.bfloat16)
                even, odd = both[:, :width], both[:, width:]
                place = peer_of(level, pair)
                mine[place] = jnp.where(side == 0, even, odd)
                others[place] = jnp.where(side == 0, odd, even)


def hold_kernel(*refs):
    pass


def params(mib):
    return pltpu.CompilerParams(
        dimension_semantics=("arbitrary",), vmem_limit_bytes=mib * 1024 * 1024
    )


def on_device(n_row, n_col, query, key, value, gate, d_out, bias, length):
    rows, blk, channels = query.shape
    heads, _, n = bias.shape
    c = channels // heads
    groups = n_col // heads
    share = rows // groups
    sizes = [share * weight // sum(SHARES) for weight in SHARES]
    starts = [sizes[-1] + sum(sizes[:m]) for m in range(len(sizes) - 1)] + [0]
    assert groups * heads == n_col and n == n_col * blk and groups * sum(sizes) == rows
    scaling = c ** (-0.5)
    per = 2 if all(size % 2 == 0 for size in sizes) else 1
    split_rows = (groups, share, blk, channels)
    query, key, value, gate, d_out = (x.reshape(split_rows) for x in (query, key, value, gate, d_out))
    row = lax.axis_index("row")
    info = jnp.stack([length[0], lax.axis_index("col"), row % 2, row // 2]).astype(jnp.int32)
    width = n // n_row
    lines = PIECES * c
    chunks = len(sizes)

    untouched = pl.BlockSpec(memory_space=pl.ANY)

    def exchange(blocks):
        pairs = [[(a, a ^ step) for a in range(n_col)] for step in range(n_col)]
        return [blocks[0]] + [lax.ppermute(blocks[step], "col", pairs[step]) for step in range(1, n_col)]

    def swap(x):
        return lax.ppermute(x, "row", [(r, r ^ 1) for r in range(n_row)])

    def hold(blocks, until):
        count = len(blocks)
        return pl.pallas_call(
            hold_kernel,
            in_specs=[untouched] * (count + len(until)),
            out_specs=[untouched] * count,
            out_shape=[jax.ShapeDtypeStruct(x.shape, x.dtype) for x in blocks],
            input_output_aliases={a: a for a in range(count)},
            compiler_params=pltpu.CompilerParams(vmem_limit_bytes=1024 * 1024),
            name="hold",
        )(*blocks, *until)

    def call(kernel, name, flops, grid, operands, out_specs, out_shape, scratch, aliases):
        return pl.pallas_call(
            kernel,
            grid_spec=pltpu.PrefetchScalarGridSpec(
                num_scalar_prefetch=1,
                grid=(grid,),
                in_specs=[spec for spec, _ in operands],
                out_specs=out_specs,
                scratch_shapes=scratch,
            ),
            out_shape=out_shape,
            input_output_aliases=aliases,
            compiler_params=params({"pack": 60, "attend": 26, "unpack": 24}[name]),
            cost_estimate=pl.CostEstimate(flops=flops, bytes_accessed=1, transcendentals=0),
            name=name,
        )(info, *[x for _, x in operands])

    def still(*shape):
        return pl.BlockSpec(shape, lambda i, info: (0,) * len(shape), pipeline_mode=pl.Buffered(1))

    def part(size, skip):
        return pl.BlockSpec((size, blk), lambda i, info: (skip + i, 0))

    def rows_a_step(*counts):
        return max(step for step in range(1, 6) if all(count % step == 0 for count in counts))

    def rows_of(group):
        return starts[group[0]], sum(sizes[m] for m in group)

    def pack(group):
        with_bias = group[0] == 0
        start, count = rows_of(group)
        step = rows_a_step(start, count)
        assert not with_bias or step == count
        base = start // step
        whole = pl.BlockSpec((groups, step, blk, channels), lambda i, info: (0, base + i, 0, 0))
        ahead = [n] + [n // 2] * (n_col - 1) if with_bias else [0] * n_col
        size = count * lines
        operands = [(whole, x) for x in (query, key, value, gate, d_out)]
        if with_bias:
            operands.append((still(heads, blk, n), bias))
        return call(
            functools.partial(pack_kernel, heads, groups, with_bias),
            "pack",
            count * 10**6,
            count // step,
            operands,
            [part(x + step * lines, 0) for x in ahead],
            [jax.ShapeDtypeStruct((x + size, blk), jnp.bfloat16) for x in ahead],
            [pltpu.VMEM((groups, step, PIECES, channels, blk), jnp.bfloat16)],
            {},
        )

    def attend(m, total, bias_blocks, blocks, room):
        first, last = m == 0, m == chunks - 1

        def scratch(*shape, dtype=jnp.bfloat16):
            return pltpu.VMEM((per, *shape), dtype)

        operands = [(still(n if a == 0 else n // 2, blk), x) for a, x in enumerate(bias_blocks)]
        (inward,) = [group for group in INWARD if m in group]
        (outward,) = [group for group in OUTWARD if m in group]
        behind = sum(sizes[o] for o in inward if o < m) // per
        ahead = sum(sizes[o] for o in outward if o < m) // per
        for a, x in enumerate(blocks):
            skip = (n if a == 0 else n // 2) // (per * lines) if first else behind
            operands.append((part(per * lines, skip), x))
        square = (n_col, n, blk)
        aliases = {}
        if not first:
            operands.append((still(*square), total))
        if ahead:
            aliases |= {1 + len(operands) + a: a for a in range(n_col)}
            operands += [(untouched, x) for x in room]
        size = rows_of(outward)[1]
        out_shape = [jax.ShapeDtypeStruct((size * lines, blk), jnp.bfloat16)] * n_col
        if last:
            totals = [jax.ShapeDtypeStruct((n_row // 2, n, width), jnp.bfloat16)] * 2
        else:
            totals = [jax.ShapeDtypeStruct(square, jnp.float32)]
        deep = 4 * c
        result = call(
            functools.partial(attention_kernel, n_col, per, c, scaling, first, last),
            "attend",
            sizes[m] * 4 * 10**9,
            sizes[m] // per,
            operands,
            [part(per * lines, ahead)] * n_col
            + [still(*x.shape) for x in totals]
            + [still(8, 128)],
            out_shape + totals + [jax.ShapeDtypeStruct((8, 128), jnp.float32)],
            [
                pltpu.VMEM(square, jnp.float32),
                pltpu.VMEM(square if last else (8, 128), jnp.float32),
                scratch(n_col, deep, blk),
                scratch(n_col, c, blk),
                scratch(deep, n),
                scratch(deep, n),
                scratch(n, deep),
                scratch(n, deep),
                scratch(n_col, c, blk),
                scratch(n_col, c, blk),
                scratch(2 * c, n, dtype=jnp.float32),
                pltpu.VMEM((2, per, n, blk), jnp.float32),
                pltpu.VMEM((2, per, n, blk), jnp.bfloat16),
                pltpu.VMEM((2, per, n, blk), jnp.bfloat16),
            ],
            aliases,
        )
        return result[:n_col], result[n_col:-1], result[-1]

    def unpack(group, blocks, grads):
        start, count = rows_of(group)
        step = rows_a_step(start, count)
        base = start // step
        whole = pl.BlockSpec((groups, step, blk, channels), lambda i, info: (0, base + i, 0, 0))
        kept = [] if grads is None else list(grads)
        operands = [(whole, gate), (whole, d_out)]
        operands += [(part(step * lines, 0), x) for x in blocks]
        aliases = {1 + len(operands) + a: a for a in range(len(kept))}
        operands += [(untouched, x) for x in kept]
        return call(
            functools.partial(unpack_kernel, heads, groups),
            "unpack",
            1,
            count // step,
            operands,
            [whole] * 4 + [pl.BlockSpec((8, 128), lambda i, info: (0, 0))],
            [jax.ShapeDtypeStruct(query.shape, jnp.bfloat16)] * 4
            + [jax.ShapeDtypeStruct((8, 128), jnp.float32)],
            [pltpu.VMEM((groups, step, PIECES, channels, blk), jnp.bfloat16)],
            aliases,
        )

    packed = [pack(group) for group in INWARD]
    own, *fetched = exchange(packed[0])
    fetched = hold(fetched, [x[0] for x in packed[1:]])
    tables = [own, *fetched] + [swap(x) for x in fetched]
    arrived = {0: [own, *fetched]}

    totals, results, sent, done = [None], None, [], []
    for m in range(chunks):
        at = [m in group for group in INWARD].index(True)
        for ahead in range(at + 1, min(at + 2, len(INWARD) - 1) + 1):
            if ahead not in arrived and (ahead == 1 or m >= INWARD[ahead - 1][0]):
                until = arrived[ahead - 1][1:] + (done[m - 1 : m] if m else [])
                arrived[ahead] = exchange([packed[ahead][0], *hold(packed[ahead][1:], until)])
        results, totals, token = attend(m, totals[0], tables, arrived[at], results)
        done.append(token)
        if m in [group[-1] for group in OUTWARD]:
            sent.append(exchange(results))
    grads, tokens = None, []
    for group, blocks in zip(OUTWARD, sent):
        *grads, token = unpack(group, blocks, grads)
        tokens.append(token)

    mine, others = totals
    (others,) = hold([others], sent[0][1:])
    others = swap(others)
    total = mine[0].astype(jnp.float32) + others[0].astype(jnp.float32)
    for step in range(1, n_row // 2):
        share = mine[step].astype(jnp.float32) + others[step].astype(jnp.float32)
        pairs = [(r, r ^ (2 * step)) for r in range(n_row)]
        total += lax.ppermute(share.astype(jnp.bfloat16), "row", pairs).astype(jnp.float32)
    total = (total + tokens[-2][0, 0]).astype(jnp.bfloat16).reshape(n_col, blk, width)
    total = lax.all_to_all(total, "col", split_axis=0, concat_axis=0, tiled=True)
    total = jnp.sum(total.reshape(heads, groups, blk, width).astype(jnp.float32), axis=1)
    bias_grad = jnp.transpose(total, (0, 2, 1))
    d_query, d_key, d_value, d_gate = (x.reshape(rows, blk, channels) for x in grads)
    return d_query, d_key, d_value, d_gate, bias_grad


def solution(mesh):
    pair = P("row", "col", None)
    return jax.shard_map(
        functools.partial(on_device, mesh.shape["row"], mesh.shape["col"]),
        mesh=mesh,
        in_specs=(pair, pair, pair, pair, pair, P(None, "col", None), P()),
        out_specs=(pair, pair, pair, pair, P(None, "row", "col")),
        check_vma=False,
    )
```
